256 devices in a mesh: shot: 32 (over x, z_lo, core), dom: 8 (over z_hi, y).
Axes of the slice: x: 4, y: 4, z: 8 (z_hi: 2, z_lo: 4; z = z_hi * 4 + z_lo), core: 2. Of those that a mesh axis runs over, the one named last changes fastest.
Arguments:
- velocity: bfloat16 [192, 320, 128], P('shot', 'dom'), may hold values from 0.19921875 to 0.43945312
- anchors: int32 [32, 2], P('shot'), may hold values from 0 to 128, as said below
- start_step: int32 [32], P('shot'), may hold values from 0 to 62
- source: int32 [32, 3], P('shot'), may hold values from 0 to 255, as said below
- receivers: int32 [32, 3, 512], P('shot'), may hold values from 0 to 255, as said below
- traces: float32 [32, 64, 512], P('shot'), may hold values from -6 to 6
- wavelet: float32 [64], replicated, may hold values from -6 to 6
- fwd_prev: float32 [32, 64, 256, 128], P('shot', 'dom'), may hold values from -6 to 6
- fwd_now: float32 [32, 64, 256, 128], P('shot', 'dom'), may hold values from -6 to 6
- adj_prev: float32 [32, 64, 256, 128], P('shot', 'dom'), may hold values from -6 to 6
- adj_now: float32 [32, 64, 256, 128], P('shot', 'dom'), may hold values from -6 to 6
Outputs:
- forward_field: float32 [32, 64, 256, 128], P('shot', 'dom')
- adjoint_field: float32 [32, 64, 256, 128], P('shot', 'dom')
- gradient: float32 [192, 320, 128], P('shot', 'dom')
The draws below stay inside these ranges and needn't reach their ends.
Inputs may be any that keep to these rules, and one draw needn't show every extreme that they name: `anchors`: column 0 runs from 0 to 128, column 1 from 0 to 64; both ends of both columns occur in every draw. `source`: columns are the cell along the first, second and third aperture dimension, below 64, 256 and 128; some shot sits at the last cell of all three, some at the first. `receivers`: components 0, 1, 2 are below 64, 256 and 128; cells may repeat; some receiver sits at the last cell of all three, some at the first.
All inputs are finite; a program needn't handle non-finite values.
Results may differ from the reference program's by a relative error of at most 0.00055.
Values may be sent and summed in bfloat16 or wider, within the bound.
No kernel may reach another device: no remote copies, remote signals or barrier semaphores. Data moves between devices by JAX's collectives and lax.ppermute only.
A program may use at most 128 MiB of HBM per device.

```python
import jax
import jax.numpy as jnp
from jax import lax

AY = 256
NZ = 128
REC = 512
NT = 64
STEPS = 2
SHOTS = 32
AX = 64
NX = 192
NY = 320


def draw_anchors(key, part):
    key = jax.random.fold_in(key, 1)
    key_x, key_y, key_rank = jax.random.split(key, 3)
    offset_x = jax.random.randint(key_x, (SHOTS,), 0, NX - AX + 1)
    offset_y = jax.random.randint(key_y, (SHOTS,), 0, NY - AY + 1)
    ranking = jax.random.permutation(key_rank, SHOTS)
    offset_x = offset_x.at[ranking[0]].set(0).at[ranking[1]].set(NX - AX)
    offset_y = offset_y.at[ranking[2]].set(0).at[ranking[3]].set(NY - AY)
    return jnp.stack([offset_x, offset_y], axis=1).astype(jnp.int32)


def draw_source(key, part):
    key = jax.random.fold_in(key, 2)
    key_x, key_y, key_z, key_rank = jax.random.split(key, 4)
    cell_x = jax.random.randint(key_x, (SHOTS,), 0, AX)
    cell_y = jax.random.randint(key_y, (SHOTS,), 0, AY)
    cell_z = jax.random.randint(key_z, (SHOTS,), 0, NZ)
    ranking = jax.random.permutation(key_rank, SHOTS)
    cell_x = cell_x.at[ranking[0]].set(AX - 1).at[ranking[1]].set(0)
    cell_y = cell_y.at[ranking[0]].set(AY - 1).at[ranking[1]].set(0)
    cell_z = cell_z.at[ranking[0]].set(NZ - 1).at[ranking[1]].set(0)
    return jnp.stack([cell_x, cell_y, cell_z], axis=1).astype(jnp.int32)


def draw_receivers(key, part):
    key = jax.random.fold_in(key, 3)
    key_x, key_y, key_z, key_rank = jax.random.split(key, 4)
    cell_x = jax.random.randint(key_x, (SHOTS, REC), 0, AX)
    cell_y = jax.random.randint(key_y, (SHOTS, REC), 0, AY)
    cell_z = jax.random.randint(key_z, (SHOTS, REC), 0, NZ)
    ranking = jax.random.permutation(key_rank, SHOTS)
    cell_x = cell_x.at[ranking[0], 0].set(AX - 1).at[ranking[1], 0].set(0)
    cell_y = cell_y.at[ranking[0], 0].set(AY - 1).at[ranking[1], 0].set(0)
    cell_z = cell_z.at[ranking[0], 0].set(NZ - 1).at[ranking[1], 0].set(0)
    return jnp.stack([cell_x, cell_y, cell_z], axis=1).astype(jnp.int32)


def plant(values, stream_key, low, top_value):
    longest = values.shape.index(max(values.shape))
    spots = []
    for shift in (0, 1):
        where = [jax.random.randint(jax.random.fold_in(stream_key, axis), (), 0, length) for axis, length in enumerate(values.shape)]
        where[longest] = (where[longest] + shift) % values.shape[longest]
        spots.append(tuple(where))
    return values.at[spots[0]].set(low).at[spots[1]].set(top_value)


def levels(rng, shape, cuts, low, largest):
    def one(position, parts):
        draws = jax.random.uniform(jax.random.fold_in(jax.random.fold_in(rng, 6), position), (parts,), jnp.float32, low / len(cuts), largest / len(cuts))
        return jnp.repeat(jnp.exp(draws), shape[position] // parts).reshape((-1,) + (1,) * (len(shape) - position - 1))

    gain = one(*cuts[0])
    for cut in cuts[1:]:
        gain = gain * one(*cut)
    return gain


def normal_values(key, shape, width, limit, cuts=(), held_as=jnp.bfloat16):
    level = levels(key, shape, cuts, -0.22, 0.18) if cuts else 1.0
    entries = jax.random.normal(key, shape, jnp.float32) * width * level
    return jnp.minimum(jnp.maximum(entries, -limit), limit).astype(held_as)


def setup_inputs(seed: int = 0) -> dict:
    key_of = jax.random.split(jax.random.key(seed), 12)
    velocity = jnp.clip(0.19921875 + 0.24023438 * jax.random.uniform(key_of[0], (NX, NY, NZ), jnp.float32) ** levels(key_of[0], (NX, NY, NZ), ((0, 32), (1, 8)), -0.2, 0.2), 0.19921875, 0.43945312).astype(jnp.bfloat16)
    anchors = draw_anchors(jax.random.fold_in(key_of[11], 71), 0)
    start_step = plant(jax.random.randint(key_of[2], (SHOTS,), 0, NT - STEPS + 1), jax.random.fold_in(key_of[2], 1), 0, NT - STEPS).astype(jnp.int32)
    source = draw_source(jax.random.fold_in(key_of[11], 71), 0)
    receivers = draw_receivers(jax.random.fold_in(key_of[11], 71), 0)
    traces = normal_values(key_of[5], (SHOTS, NT, REC), 1.0, 6.0, ((0, 32),), jnp.float32)
    wavelet = normal_values(key_of[6], (NT,), 1.0, 6.0, (), jnp.float32)
    fwd_prev = normal_values(key_of[7], (SHOTS, AX, AY, NZ), 1.0, 6.0, ((0, 32), (1, 8)), jnp.float32)
    fwd_now = normal_values(key_of[8], (SHOTS, AX, AY, NZ), 1.0, 6.0, ((0, 32), (1, 8)), jnp.float32)
    adj_prev = normal_values(key_of[9], (SHOTS, AX, AY, NZ), 1.0, 6.0, ((0, 32), (1, 8)), jnp.float32)
    adj_now = normal_values(key_of[10], (SHOTS, AX, AY, NZ), 1.0, 6.0, ((0, 32), (1, 8)), jnp.float32)
    return dict(velocity=velocity, anchors=anchors, start_step=start_step, source=source, receivers=receivers, traces=traces, wavelet=wavelet, fwd_prev=fwd_prev, fwd_now=fwd_now, adj_prev=adj_prev, adj_now=adj_now)


CENTER = -205.0 / 72.0
COEFFS = (8.0 / 5.0, -1.0 / 5.0, 8.0 / 315.0, -1.0 / 560.0)


def laplace_rows(extended):
    row_count = extended.shape[0] - 8
    count_y = extended.shape[1]
    count_z = extended.shape[2]
    middle = extended[4:4 + row_count]
    padded = jnp.pad(middle, ((0, 0), (4, 4), (4, 4)))
    summed = (3.0 * CENTER) * middle
    for k in range(1, 5):
        weight = COEFFS[k - 1]
        summed = summed + weight * (extended[4 + k:4 + k + row_count] + extended[4 - k:4 - k + row_count])
        summed = summed + weight * (padded[:, 4 + k:4 + k + count_y, 4:4 + count_z] + padded[:, 4 - k:4 - k + count_y, 4:4 + count_z])
        summed = summed + weight * (padded[:, 4:4 + count_y, 4 + k:4 + k + count_z] + padded[:, 4:4 + count_y, 4 - k:4 - k + count_z])
    return summed


def source_term(x_start, row_count, count_y, count_z, shot_source, amplitude):
    grid_shape = (row_count, count_y, count_z)
    cell_x = x_start + lax.broadcasted_iota(jnp.int32, grid_shape, 0)
    cell_y = lax.broadcasted_iota(jnp.int32, grid_shape, 1)
    cell_z = lax.broadcasted_iota(jnp.int32, grid_shape, 2)
    is_hit = (cell_x == shot_source[0]) & (cell_y == shot_source[1]) & (cell_z == shot_source[2])
    return jnp.where(is_hit, amplitude, jnp.zeros((), amplitude.dtype))


def receiver_term(x_start, row_count, count_y, count_z, shot_receivers, amplitudes):
    local_x = (shot_receivers[0] - x_start).astype(jnp.int32)
    valid = (local_x >= 0) & (local_x < row_count)
    local_x = jnp.where(valid, local_x, row_count).astype(jnp.int32)
    grid = jnp.zeros((row_count, count_y, count_z), amplitudes.dtype)
    return grid.at[local_x, shot_receivers[1], shot_receivers[2]].add(amplitudes, mode="drop")


def reference(velocity, anchors, start_step, source, receivers, traces, wavelet, fwd_prev, fwd_now, adj_prev, adj_now):
    def accumulate(gradient, per_shot):
        anchor, first_step, shot_source, shot_receivers, shot_traces, prev_f, now_f, prev_a, now_a = per_shot
        zero_index = jnp.zeros((), jnp.int32)
        corner = (anchor[0].astype(jnp.int32), anchor[1].astype(jnp.int32), zero_index)
        window = lax.dynamic_slice(velocity, corner, (AX, AY, NZ))
        courant = jnp.square(window.astype(jnp.float32))
        forward = [prev_f, now_f]
        adjoint = [prev_a, now_a]
        for k in range(STEPS):
            amplitude = lax.dynamic_index_in_dim(wavelet, first_step + k, 0, keepdims=False)
            injected = source_term(zero_index, AX, AY, NZ, shot_source, amplitude)
            extended = jnp.pad(forward[-1], ((4, 4), (0, 0), (0, 0)))
            forward.append(2.0 * extended[4:-4] - forward[-2] + courant * laplace_rows(extended) + injected)
        for k in range(STEPS):
            amplitudes = lax.dynamic_index_in_dim(shot_traces, first_step + STEPS - 1 - k, 0, keepdims=False)
            injected = receiver_term(zero_index, AX, AY, NZ, shot_receivers, amplitudes)
            extended = jnp.pad(adjoint[-1], ((4, 4), (0, 0), (0, 0)))
            adjoint.append(2.0 * extended[4:-4] - adjoint[-2] + courant * laplace_rows(extended) + injected)
        imaged = jnp.zeros_like(forward[1])
        for k in range(1, STEPS + 1):
            imaged = imaged + adjoint[k + 1] * (forward[STEPS - k + 2] - 2.0 * forward[STEPS - k + 1] + forward[STEPS - k])
        current = lax.dynamic_slice(gradient, corner, (AX, AY, NZ))
        gradient = lax.dynamic_update_slice(gradient, current + imaged, corner)
        return gradient, (forward[-1], adjoint[-1])

    start_grad = jnp.zeros((NX, NY, NZ), jnp.float32)
    gradient, fields = lax.scan(accumulate, start_grad, (anchors, start_step, source, receivers, traces, fwd_prev, fwd_now, adj_prev, adj_now))
    return fields[0], fields[1], gradient
```

```python
import functools

import jax
import jax.numpy as jnp
from jax import lax
from jax.experimental import pallas as pl
from jax.experimental.pallas import tpu as pltpu
from jax.sharding import PartitionSpec as P

STEPS = 2
CENTER = -205.0 / 72.0
COEFFS = (8.0 / 5.0, -1.0 / 5.0, 8.0 / 315.0, -1.0 / 560.0)

F32 = jnp.float32
BF16 = jnp.bfloat16
I16 = jnp.int16
I32 = jnp.int32

VMEM_LIMIT = 56 * 1024 * 1024
FLOOR = 1e-33
TOP = 32700.0
HALO = 4
GROUP = 32


def vmem():
    return pl.BlockSpec(memory_space=pltpu.VMEM)


def smem():
    return pl.BlockSpec(memory_space=pltpu.SMEM)


def call(kernel, outs, args, spaces, scratch=(), cost=1_000_000):
    moved = sum(a.size * a.dtype.itemsize for a in (*outs, *args))
    return pl.pallas_call(
        kernel,
        out_shape=list(outs),
        in_specs=[smem() if s == "s" else vmem() for s in spaces],
        out_specs=[vmem()] * len(outs),
        scratch_shapes=list(scratch),
        compiler_params=pltpu.CompilerParams(vmem_limit_bytes=VMEM_LIMIT),
        cost_estimate=pl.CostEstimate(flops=cost, bytes_accessed=moved, transcendentals=0),
    )(*args)


def struct(shape, dtype):
    return jax.ShapeDtypeStruct(shape, dtype)


def code_group(values):
    top = jnp.max(jnp.abs(values), axis=0, keepdims=True)
    level = jnp.ceil(jnp.log2(jnp.maximum(top, FLOOR)) * 256.0) + 1.0
    scaled = values * (TOP * jnp.exp2(level * (-1.0 / 256.0)))
    return jnp.round(scaled).astype(I32), level.astype(I32)


def code_rows(values, out_ref, base):
    band = values[0].shape[0]
    levels = []
    for n in range(0, len(values), 2):
        codes = []
        for value in values[n : n + 2]:
            code, level = code_group(value)
            codes.append(code)
            levels.append(level)
        out_ref[pl.ds(base + n * band, 2 * band), :] = jnp.concatenate(codes, axis=0).astype(I16)
    levels += [jnp.zeros((-len(levels) % 16, values[0].shape[1]), I32)]
    spot = pl.ds(base + len(values) * band, code_rows_of(len(values), band) - len(values) * band)
    out_ref[spot, :] = jnp.concatenate(levels, axis=0).astype(I16)


def code_rows_of(groups, band):
    return groups * band + groups + -groups % 16


def decode_rows(in_ref, groups, band):
    scales = decode_scale(in_ref[pl.ds(groups * band, groups + -groups % 16), :])
    for n in range(0, groups, 2):
        pair = in_ref[pl.ds(n * band, 2 * band), :].astype(I32).astype(F32)
        yield pair[:band] * scales[n : n + 1]
        yield pair[band:] * scales[n + 1 : n + 2]


def decode_scale(levels):
    return jnp.exp2(levels.astype(I32).astype(F32) * (1.0 / 256.0)) * (1.0 / TOP)


def code_halos(field, rows, out_ref, level_ref, base):
    for n, layer in enumerate(rows):
        value = field(layer)
        count = value.shape[0] // GROUP
        for g in range(count):
            code, level = code_group(value[g * GROUP : (g + 1) * GROUP])
            spot = base + n * count + g
            out_ref[pl.ds(spot * GROUP, GROUP), :] = code.astype(I16)
            level_ref[pl.ds(spot, 1), :] = level


def halo_rows(layers, count_y):
    groups = layers * count_y // GROUP
    return groups * GROUP + groups


def encode_kernel(now_f, now_a, low_ref, high_ref, level_ref):
    count_y = now_f.shape[1]
    per = HALO * count_y // GROUP
    for out_ref, first in ((low_ref, 0), (high_ref, now_f.shape[0] - HALO)):
        for f, ref in enumerate((now_f, now_a)):
            code_halos(lambda x: ref[x], range(first, first + HALO), out_ref, level_ref, f * per)
        out_ref[2 * per * GROUP :, :] = level_ref[...].astype(I16)


def decode_halo(in_ref, scale_ref, pad_ref, f, first, count_y):
    per = count_y // GROUP
    for layer in range(HALO):
        for g in range(per):
            spot = (f * HALO + layer) * per + g
            code = in_ref[pl.ds(spot * GROUP, GROUP), :].astype(I32).astype(F32)
            pad_ref[first + layer, pl.ds(PAD + g * GROUP, GROUP), :] = code * scale_ref[pl.ds(spot, 1), :]


PAD = 8


def laplace_tile(pad_ref, layer, y, rows, masks):
    middle = pad_ref[layer, pl.ds(PAD + y, rows), :]
    summed = (3.0 * CENTER) * middle
    for k in range(1, HALO + 1):
        up, down = masks[k - 1]
        count = middle.shape[1]
        part = pad_ref[layer + k, pl.ds(PAD + y, rows), :] + pad_ref[layer - k, pl.ds(PAD + y, rows), :]
        part += pad_ref[layer, pl.ds(PAD + y + k, rows), :] + pad_ref[layer, pl.ds(PAD + y - k, rows), :]
        part += jnp.where(up, pltpu.roll(middle, k, 1), 0.0)
        part += jnp.where(down, pltpu.roll(middle, count - k, 1), 0.0)
        summed += COEFFS[k - 1] * part
    return middle, summed


TILE = 32


def lane_masks(rows, count):
    lane = lax.broadcasted_iota(I32, (rows, count), 1)
    return [(lane >= k, lane < count - k) for k in range(1, HALO + 1)]


def fill(pad_ref, field_ref, low_ref, high_ref, scales, f):
    row_count, count_y = field_ref.shape[0], field_ref.shape[1]
    pad_ref[:, 0:PAD, :] = jnp.zeros((pad_ref.shape[0], PAD, pad_ref.shape[2]), F32)
    pad_ref[:, PAD + count_y :, :] = jnp.zeros((pad_ref.shape[0], PAD, pad_ref.shape[2]), F32)
    for x in range(row_count):
        pad_ref[HALO + x, PAD : PAD + count_y, :] = field_ref[x]
    decode_halo(low_ref, scales[0], pad_ref, f, 0, count_y)
    decode_halo(high_ref, scales[1], pad_ref, f, HALO + row_count, count_y)


def load_scales(in_ref, scale_ref):
    groups = scale_ref.shape[0]
    scale_ref[...] = decode_scale(in_ref[groups * GROUP :, :])


def add_source(source, start, wave, ref, k):
    x = source[0, 0] - lax.axis_index("dom") * ref.shape[0]
    lane = lax.broadcasted_iota(I32, (1, ref.shape[2]), 1)

    @pl.when((x >= 0) & (x < ref.shape[0]))
    def _():
        y = source[0, 1]
        row = ref[x, pl.ds(y, 1), :]
        ref[x, pl.ds(y, 1), :] = row + jnp.where(lane == source[0, 2], wave[start[0] + k], 0.0)


def first_kernel(groups, anchors, source, begin, wave, now_f, now_a, prev_f, prev_a, low, high, hit, *rest):
    pieces, rest = rest[:groups], rest[groups:]
    next_f, next_a, courant, send_low, send_high, slab, pad, scale_low, scale_high, level = rest
    row_count, count_y, count_z = now_f.shape
    band = pieces[0].shape[0] // row_count
    me = lax.axis_index("dom")
    for k in range(groups):
        start = pl.multiple_of(lax.rem(me + groups - k, groups) * band, 8)
        for x in range(0, row_count, 2):
            speed = pieces[k][pl.ds(x * band, 2 * band), :].astype(F32)
            slab[x, pl.ds(start, band), :] = jnp.square(speed[:band])
            slab[x + 1, pl.ds(start, band), :] = jnp.square(speed[band:])
    masks = lane_masks(TILE, count_z)
    load_scales(low, scale_low)
    load_scales(high, scale_high)
    for f, (now, prev, out) in enumerate(((now_f, prev_f, next_f), (now_a, prev_a, next_a))):
        fill(pad, now, low, high, (scale_low, scale_high), f)

        @pl.loop(0, row_count)
        def _(x):
            for y in range(0, count_y, TILE):
                if f == 0:
                    factor = slab[x, pl.ds(anchors[0, 1] + y, TILE), :]
                    courant[x, pl.ds(y, TILE), :] = factor
                else:
                    factor = courant[x, pl.ds(y, TILE), :]
                middle, summed = laplace_tile(pad, HALO + x, y, TILE, masks)
                value = 2.0 * middle - prev[x, pl.ds(y, TILE), :] + factor * summed
                if f == 1:
                    value += hit[x, pl.ds(y, TILE), :]
                out[x, pl.ds(y, TILE), :] = value

        if f == 0:
            add_source(source, begin, wave, out, 0)
    per = HALO * count_y // GROUP
    for out_ref, first in ((send_low, 0), (send_high, row_count - HALO)):
        for f, ref in enumerate((next_f, next_a)):
            code_halos(lambda x: ref[x], range(first, first + HALO), out_ref, level, f * per)
        out_ref[2 * per * GROUP :, :] = level[...].astype(I16)


def second_kernel(groups, anchors, source, begin, wave, p1, q1, p0, q0, prev_f, courant, low, high, hit, *rest):
    next_f, next_a, own = rest[:3]
    sends = rest[3 : 2 + groups]
    frame, pad, pad_a, scale_low, scale_high = rest[2 + groups :]
    row_count, count_y, count_z = p1.shape
    band = own.shape[0] // row_count
    masks = lane_masks(TILE, count_z)
    load_scales(low, scale_low)
    load_scales(high, scale_high)
    fill(pad, p1, low, high, (scale_low, scale_high), 0)
    fill(pad_a, q1, low, high, (scale_low, scale_high), 1)
    edge = (frame.shape[1] - count_y) // 2
    frame[:, 0:edge, :] = jnp.zeros((row_count, edge, count_z), F32)
    frame[:, edge + count_y :, :] = jnp.zeros((row_count, edge, count_z), F32)

    @pl.loop(0, row_count)
    def _(x):
        for y in range(0, count_y, TILE):
            spot = pl.ds(y, TILE)
            middle, summed = laplace_tile(pad, HALO + x, y, TILE, masks)
            before = p0[x, spot, :]
            next_f[x, spot, :] = 2.0 * middle - before + courant[x, spot, :] * summed
            middle_a, summed = laplace_tile(pad_a, HALO + x, y, TILE, masks)
            last = 2.0 * middle_a - q0[x, spot, :] + courant[x, spot, :] * summed + hit[x, spot, :]
            next_a[x, spot, :] = last

    add_source(source, begin, wave, next_f, 1)

    @pl.loop(0, row_count)
    def _(x):
        for y in range(0, count_y, TILE):
            spot = pl.ds(y, TILE)
            before, middle = p0[x, spot, :], p1[x, spot, :]
            image = q1[x, spot, :] * (next_f[x, spot, :] - 2.0 * middle + before)
            image += next_a[x, spot, :] * (middle - 2.0 * before + prev_f[x, spot, :])
            frame[x, pl.ds(edge + y, TILE), :] = image

    me = lax.axis_index("dom")
    for k in range(groups):
        target = lax.rem(me + k, groups)
        start = edge - anchors[0, 1] + target * band
        values = [frame[x, pl.ds(start, band), :] for x in range(row_count)]
        if k == 0:
            for x in range(row_count):
                own[pl.ds(x * band, band), :] = values[x]
        else:
            code_rows(values, sends[k - 1], 0)


def hit_kernel(begin, cells, traces, first, second):
    row_count, count_y, count_z = first.shape
    x = cells[0:1, :] - lax.axis_index("dom") * row_count
    inside = (x >= 0) & (x < row_count)
    row = jnp.where(inside, x * count_y + cells[1:2, :], -1)
    depth = lax.broadcasted_iota(I32, (count_z, row.shape[1]), 0)
    at_depth = depth == cells[2:3, :]
    parts = []
    for k in range(STEPS):
        left = traces[pl.ds(begin[0] + (STEPS - 1 - k), 1), :]
        for _ in range(3):
            part = left.astype(BF16).astype(F32)
            parts.append(jnp.where(at_depth, part, 0.0).astype(BF16))
            left = left - part
    right = jnp.concatenate(parts, axis=0)

    @pl.loop(0, row_count)
    def _(i):
        cell = i * count_y + lax.broadcasted_iota(I32, (count_y, row.shape[1]), 0)
        left = jnp.where(cell == row, 1.0, 0.0).astype(BF16)
        got = lax.dot_general(left, right, (((1,), (1,)), ((), ())), preferred_element_type=F32)
        for k, out in enumerate((first, second)):
            base = 3 * k * count_z
            high = got[:, base : base + count_z]
            middle = got[:, base + count_z : base + 2 * count_z]
            low = got[:, base + 2 * count_z : base + 3 * count_z]
            out[i] = high + (middle + low)


SIZE_X, SIZE_Z, SIZE_C = 4, 4, 2


def place_of(shot):
    return shot // (SIZE_Z * SIZE_C), lax.rem(shot // SIZE_C, SIZE_Z), lax.rem(shot, SIZE_C)


def turn(axis, k):
    pairs = []
    for shot in range(SIZE_X * SIZE_Z * SIZE_C):
        x, z, c = shot // (SIZE_Z * SIZE_C), shot // SIZE_C % SIZE_Z, shot % SIZE_C
        x = (x + k) % SIZE_X if axis == "x" else x
        z = (z + k) % SIZE_Z if axis == "z" else z
        c = (c + k) % SIZE_C if axis == "c" else c
        pairs.append((shot, (x * SIZE_Z + z) * SIZE_C + c))
    return pairs


def pick_kernel(layout, row_count, anchors, *refs):
    count = len(layout)
    ins, outs, table = refs[:count], refs[count:-1], refs[-1]
    groups = len(outs)
    per = outs[0].shape[0] // row_count
    block = ins[0].shape[0] // len(layout[0])
    own = block // per
    x, z, c = place_of(lax.axis_index("shot"))
    me = lax.axis_index("dom")
    anchor = anchors[0, 0]
    first = anchor // own
    span = table.shape[0] // block
    for ref, owners in zip(ins, layout):
        for n, (dx, dz, dc) in enumerate(owners):
            owner = lax.rem(x + dx, SIZE_X) * SIZE_Z + lax.rem(z + dz, SIZE_Z)
            place = owner * SIZE_C + lax.rem(c + dc, SIZE_C) - first

            @pl.when((place >= 0) & (place < span))
            def _():
                start = pl.multiple_of(place * block, 8)
                table[pl.ds(start, block), :] = ref[pl.ds(n * block, block), :].astype(F32)

    offset = (anchor - first * own) * per
    for k in range(groups):
        start = pl.multiple_of(offset + lax.rem(me + k, groups) * (row_count * per), 8)
        outs[k][...] = table[pl.ds(start, row_count * per), :].astype(BF16)


def band_kernel(groups, row_count, block, anchors, own, *refs):
    got, (keep, send, table) = refs[: groups - 1], refs[groups - 1 :]
    per = own.shape[0] // row_count
    c = lax.rem(lax.axis_index("shot"), SIZE_C)
    me = lax.axis_index("dom")
    anchor = anchors[0, 0]
    first = anchor // (block // per)
    table[...] = jnp.zeros(table.shape, F32)
    offset = (anchor - first * (block // per)) * per
    for k in range(groups):
        base = offset + lax.rem(me + groups - k, groups) * (row_count * per)
        if k == 0:
            table[pl.ds(pl.multiple_of(base, 8), row_count * per), :] = own[...]
        else:
            for n, value in enumerate(decode_rows(got[k - 1], row_count, per)):
                table[pl.ds(pl.multiple_of(base + n * per, 8), per), :] = value
    mine = lax.rem(c + first, SIZE_C)
    for i in range(keep.shape[0] // block):
        for out, parity in ((keep, mine), (send, 1 - mine)):
            start = pl.multiple_of((SIZE_C * i + parity) * block, 8)
            out[pl.ds(i * block, block), :] = table[pl.ds(start, block), :]


def core_kernel(block, per, anchors, other, keep, got, own, *refs):
    sends, total = refs[:-1], refs[-1]
    x, _, c = place_of(lax.axis_index("shot"))
    total[...] = jnp.zeros(total.shape, F32)
    for ref, place in ((keep, anchors), (got, other)):
        first = place[0, 0] // (block // per)
        low = (first + lax.rem(c + first, SIZE_C)) // SIZE_C
        for i in range(ref.shape[0] // block):
            spot = pl.ds(pl.multiple_of((low + i) * block, 8), block)
            total[spot, :] += ref[pl.ds(i * block, block), :]
    size = own.shape[0]
    own[...] = total[pl.ds(pl.multiple_of(x * size, 8), size), :]
    for k, send in enumerate(sends, 1):
        start = lax.rem(x + k, SIZE_X) * size
        values = [total[pl.ds(pl.multiple_of(start + n * per, 8), per), :] for n in range(size // per)]
        code_rows(values, send, 0)


def along_x_kernel(per, mine, *refs):
    got, rest = refs[: SIZE_X - 1], refs[SIZE_X - 1 :]
    own, sends, total = rest[0], rest[1:-1], rest[-1]
    total[...] = mine[...]
    for ref in got:
        for n, value in enumerate(decode_rows(ref, total.shape[0] // per, per)):
            total[pl.ds(n * per, per), :] += value
    _, z, _ = place_of(lax.axis_index("shot"))
    size = own.shape[0]
    own[...] = total[pl.ds(pl.multiple_of(z * size, 8), size), :]
    for k, send in enumerate(sends, 1):
        start = lax.rem(z + k, SIZE_Z) * size
        values = [total[pl.ds(pl.multiple_of(start + n * per, 8), per), :] for n in range(size // per)]
        code_rows(values, send, 0)


def along_z_kernel(per, mine, *refs):
    got, out = refs[:-1], refs[-1]
    for parts in zip(range(mine.shape[0] // per), *[decode_rows(r, mine.shape[0] // per, per) for r in got]):
        n, values = parts[0], parts[1:]
        total = mine[pl.ds(n * per, per), :]
        for value in values:
            total += value
        out[pl.ds(n * per, per), :] = total


def around(groups, k):
    return [(i, (i + k) % groups) for i in range(groups)]


def body(
    velocity,
    anchors,
    start_step,
    source,
    receivers,
    traces,
    wavelet,
    fwd_prev,
    fwd_now,
    adj_prev,
    adj_now,
):
    row_count, count_y, count_z = fwd_now.shape[1:]
    groups = lax.axis_size("dom")
    own_rows, band = velocity.shape[:2]
    block = own_rows * band
    piece = row_count * band
    p0, q0, p_prev, q_prev = fwd_now[0], adj_now[0], fwd_prev[0], adj_prev[0]
    scalars = (anchors, source, start_step, wavelet)
    up = [(i, i + 1) for i in range(groups - 1)]
    down = [(b, a) for a, b in up]

    local = velocity.reshape(block, count_z)
    near = [local] + [lax.ppermute(local, "shot", turn("z", k)) for k in range(1, SIZE_Z)]
    other = lax.ppermute(anchors, "shot", turn("c", 1))

    half = halo_rows(2 * HALO, count_y)
    code = struct((half, count_z), I16)
    levels = pltpu.VMEM((2 * HALO * count_y // GROUP, count_z), I32)
    low, high = call(encode_kernel, (code, code), (p0, q0), "vv", (levels,))
    from_low = lax.ppermute(high, "dom", up)
    from_high = lax.ppermute(low, "dom", down)

    field = struct((row_count, count_y, count_z), F32)
    hits = call(hit_kernel, (field, field), (start_step, receivers[0], traces[0]), "svv")

    line = jnp.concatenate(near, axis=0)
    plane = [line] + [lax.ppermute(line, "shot", turn("x", k)) for k in range(1, SIZE_X)]
    plane += [lax.ppermute(part, "shot", turn("c", 1)) for part in plane]
    layout = [
        [(-dx % SIZE_X, -dz % SIZE_Z, dc) for dz in range(SIZE_Z)]
        for dc in range(SIZE_C)
        for dx in range(SIZE_X)
    ]
    span = -(-(row_count * groups + own_rows - 1) // own_rows)
    span += span % SIZE_C
    table = pltpu.VMEM((span * block, count_z), F32)
    pieces = call(
        functools.partial(pick_kernel, layout, row_count),
        [struct((piece, count_z), BF16)] * groups,
        (anchors, *plane),
        "s" + "v" * len(plane),
        (table,),
    )
    pieces = [pieces[0]] + [lax.ppermute(pieces[k], "dom", around(groups, k)) for k in range(1, groups)]

    padded = pltpu.VMEM((row_count + 2 * HALO, count_y + 2 * PAD, count_z), F32)
    scale = pltpu.VMEM((2 * HALO * count_y // GROUP, count_z), F32)
    slab = pltpu.VMEM((row_count, groups * band, count_z), F32)
    p1, q1, courant, low, high = call(
        functools.partial(first_kernel, groups),
        (field, field, field, code, code),
        (*scalars, p0, q0, p_prev, q_prev, from_low, from_high, hits[0], *pieces),
        "ssss" + "v" * (7 + groups),
        (slab, padded, scale, scale, levels),
    )
    from_low = lax.ppermute(high, "dom", up)
    from_high = lax.ppermute(low, "dom", down)

    edge = groups * band - count_y
    coded = struct((code_rows_of(row_count, band), count_z), I16)
    frame = pltpu.VMEM((row_count, count_y + 2 * edge, count_z), F32)
    p2, q2, own, *sends = call(
        functools.partial(second_kernel, groups),
        (field, field, struct((piece, count_z), F32), *[coded] * (groups - 1)),
        (*scalars, p1, q1, p0, q0, p_prev, courant, from_low, from_high, hits[1]),
        "ssss" + "v" * 9,
        (frame, padded, padded, scale, scale),
    )
    got = [lax.ppermute(send, "dom", around(groups, k)) for k, send in enumerate(sends, 1)]

    part = struct((span // SIZE_C * block, count_z), F32)
    keep, send = call(
        functools.partial(band_kernel, groups, row_count, block),
        (part, part),
        (anchors, own, *got),
        "s" + "v" * groups,
        (table,),
    )
    got = lax.ppermute(send, "shot", turn("c", 1))

    size = SIZE_Z * block
    coded = struct((code_rows_of(size // band, band), count_z), I16)
    total = pltpu.VMEM(((SIZE_X * SIZE_Z + 1) * block, count_z), F32)
    own, *sends = call(
        functools.partial(core_kernel, block, band),
        (struct((size, count_z), F32), *[coded] * (SIZE_X - 1)),
        (anchors, other, keep, got),
        "ssvv",
        (total,),
    )
    got = [lax.ppermute(send, "shot", turn("x", k)) for k, send in enumerate(sends, 1)]

    coded = struct((code_rows_of(own_rows, band), count_z), I16)
    own, *sends = call(
        functools.partial(along_x_kernel, band),
        (struct((block, count_z), F32), *[coded] * (SIZE_Z - 1)),
        (own, *got),
        "v" * SIZE_X,
        (pltpu.VMEM((size, count_z), F32),),
    )
    got = [lax.ppermute(send, "shot", turn("z", k)) for k, send in enumerate(sends, 1)]

    (gradient,) = call(
        functools.partial(along_z_kernel, band),
        (struct((block, count_z), F32),),
        (own, *got),
        "v" * SIZE_Z,
    )
    return (p2[None], q2[None], gradient.reshape(own_rows, band, count_z))


def solution(mesh):
    placed = (
        P("shot", "dom", None),
        P("shot", None),
        P("shot"),
        P("shot", None),
        P("shot", None, None),
        P("shot", None, None),
        P(),
        P("shot", "dom", None, None),
        P("shot", "dom", None, None),
        P("shot", "dom", None, None),
        P("shot", "dom", None, None),
    )
    return jax.shard_map(
        body,
        mesh=mesh,
        in_specs=placed,
        out_specs=(
            P("shot", "dom", None, None),
            P("shot", "dom", None, None),
            P("shot", "dom", None),
        ),
        check_vma=False,
    )
```

```python
import functools

import jax
import jax.numpy as jnp
from jax import lax
from jax.experimental import pallas as pl
from jax.experimental.pallas import tpu as pltpu
from jax.sharding import PartitionSpec as P

STEPS = 2
CENTER = -205.0 / 72.0
COEFFS = (8.0 / 5.0, -1.0 / 5.0, 8.0 / 315.0, -1.0 / 560.0)

F32 = jnp.float32
BF16 = jnp.bfloat16
I16 = jnp.int16
I32 = jnp.int32

VMEM_LIMIT = 32 * 1024 * 1024
FLOOR = 1e-33
TOP = 32700.0
HALO = 4
GROUP = 32


def vmem():
    return pl.BlockSpec(memory_space=pltpu.VMEM)


def smem():
    return pl.BlockSpec(memory_space=pltpu.SMEM)


def call(kernel, outs, args, spaces, scratch=(), cost=1_000_000):
    moved = sum(a.size * a.dtype.itemsize for a in (*outs, *args))
    return pl.pallas_call(
        kernel,
        out_shape=list(outs),
        in_specs=[smem() if s == "s" else vmem() for s in spaces],
        out_specs=[vmem()] * len(outs),
        scratch_shapes=list(scratch),
        compiler_params=pltpu.CompilerParams(vmem_limit_bytes=VMEM_LIMIT),
        cost_estimate=pl.CostEstimate(flops=0, bytes_accessed=0, transcendentals=0),
    )(*args)


def struct(shape, dtype):
    return jax.ShapeDtypeStruct(shape, dtype)


def code_group(values):
    top = jnp.max(jnp.abs(values), axis=0, keepdims=True)
    level = jnp.ceil(jnp.log2(jnp.maximum(top, FLOOR)) * 256.0) + 1.0
    scaled = values * (TOP * jnp.exp2(level * (-1.0 / 256.0)))
    return jnp.round(scaled).astype(I32), level.astype(I32)


def code_rows(values, out_ref, base):
    band = values[0].shape[0]
    levels = []
    for n in range(0, len(values), 2):
        codes = []
        for value in values[n : n + 2]:
            code, level = code_group(value)
            codes.append(code)
            levels.append(level)
        out_ref[pl.ds(base + n * band, 2 * band), :] = jnp.concatenate(codes, axis=0).astype(I16)
    levels += [jnp.zeros((-len(levels) % 16, values[0].shape[1]), I32)]
    spot = pl.ds(base + len(values) * band, code_rows_of(len(values), band) - len(values) * band)
    out_ref[spot, :] = jnp.concatenate(levels, axis=0).astype(I16)


def code_rows_of(groups, band):
    return groups * band + groups + -groups % 16


def decode_rows(in_ref, groups, band):
    scales = decode_scale(in_ref[pl.ds(groups * band, groups + -groups % 16), :])
    for n in range(0, groups, 2):
        pair = in_ref[pl.ds(n * band, 2 * band), :].astype(I32).astype(F32)
        yield pair[:band] * scales[n : n + 1]
        yield pair[band:] * scales[n + 1 : n + 2]


def decode_scale(levels):
    return jnp.exp2(levels.astype(I32).astype(F32) * (1.0 / 256.0)) * (1.0 / TOP)


def code_halos(field, rows, out_ref, level_ref, base):
    for n, layer in enumerate(rows):
        value = field(layer)
        count = value.shape[0] // GROUP
        for g in range(count):
            code, level = code_group(value[g * GROUP : (g + 1) * GROUP])
            spot = base + n * count + g
            out_ref[pl.ds(spot * GROUP, GROUP), :] = code.astype(I16)
            level_ref[pl.ds(spot, 1), :] = level


def halo_rows(layers, count_y):
    groups = layers * count_y // GROUP
    return groups * GROUP + groups


def encode_kernel(now_f, now_a, low_ref, high_ref, level_ref):
    count_y = now_f.shape[1]
    per = HALO * count_y // GROUP
    for out_ref, first in ((low_ref, 0), (high_ref, now_f.shape[0] - HALO)):
        for f, ref in enumerate((now_f, now_a)):
            code_halos(lambda x: ref[x], range(first, first + HALO), out_ref, level_ref, f * per)
        out_ref[2 * per * GROUP :, :] = level_ref[...].astype(I16)


def decode_halo(in_ref, scale_ref, pad_ref, f, first, count_y):
    per = count_y // GROUP
    for layer in range(HALO):
        for g in range(per):
            spot = (f * HALO + layer) * per + g
            code = in_ref[pl.ds(spot * GROUP, GROUP), :].astype(I32).astype(F32)
            pad_ref[first + layer, pl.ds(PAD + g * GROUP, GROUP), :] = code * scale_ref[pl.ds(spot, 1), :]


PAD = 8


def laplace_tile(pad_ref, layer, y, rows, masks):
    middle = pad_ref[layer, pl.ds(PAD + y, rows), :]
    summed = (3.0 * CENTER) * middle
    for k in range(1, HALO + 1):
        up, down = masks[k - 1]
        count = middle.shape[1]
        part = pad_ref[layer + k, pl.ds(PAD + y, rows), :] + pad_ref[layer - k, pl.ds(PAD + y, rows), :]
        part += pad_ref[layer, pl.ds(PAD + y + k, rows), :] + pad_ref[layer, pl.ds(PAD + y - k, rows), :]
        part += jnp.where(up, pltpu.roll(middle, k, 1), 0.0)
        part += jnp.where(down, pltpu.roll(middle, count - k, 1), 0.0)
        summed += COEFFS[k - 1] * part
    return middle, summed


TILE = 32


def lane_masks(rows, count):
    lane = lax.broadcasted_iota(I32, (rows, count), 1)
    return [(lane >= k, lane < count - k) for k in range(1, HALO + 1)]


def fill(pad_ref, field_ref):
    row_count, count_y, count_z = field_ref.shape
    edge = jnp.zeros((pad_ref.shape[0], PAD, count_z), F32)
    pad_ref[:, 0:PAD, :] = edge
    pad_ref[:, PAD + count_y :, :] = edge
    for x in range(row_count):
        pad_ref[HALO + x, PAD : PAD + count_y, :] = field_ref[x]


def load_scales(in_ref, scale_ref):
    groups = scale_ref.shape[0]
    scale_ref[...] = decode_scale(in_ref[groups * GROUP :, :])


def add_source(source, start, wave, ref, k, edge=0):
    x = source[0, 0] - lax.axis_index("dom") * ref.shape[0]
    lane = lax.broadcasted_iota(I32, (1, ref.shape[2]), 1)

    @pl.when((x >= 0) & (x < ref.shape[0]))
    def _():
        y = source[0, 1] + edge
        row = ref[x, pl.ds(y, 1), :]
        ref[x, pl.ds(y, 1), :] = row + jnp.where(lane == source[0, 2], wave[start[0] + k], 0.0)


def before_kernel(now_f, now_a, prev_f, prev_a, low, high, hit, *rest):
    sum_f, sum_a, base_f, base_a, pad, scale_low, scale_high = rest
    row_count, count_y, count_z = now_f.shape
    masks = lane_masks(TILE, count_z)
    load_scales(low, scale_low)
    load_scales(high, scale_high)
    fields = ((now_f, prev_f, sum_f, base_f), (now_a, prev_a, sum_a, base_a))
    for f, (now, prev, total, base) in enumerate(fields):
        fill(pad, now)
        decode_halo(low, scale_low, pad, f, 0, count_y)
        decode_halo(high, scale_high, pad, f, HALO + row_count, count_y)

        @pl.loop(0, row_count)
        def _(x):
            for y in range(0, count_y, TILE):
                spot = pl.ds(y, TILE)
                middle, summed = laplace_tile(pad, HALO + x, y, TILE, masks)
                total[x, spot, :] = summed
                value = 2.0 * middle - prev[x, spot, :]
                base[x, spot, :] = value + hit[x, spot, :] if f else value


def first_kernel(groups, anchors, source, begin, wave, sum_f, sum_a, base_f, base_a, *rest):
    pieces, rest = rest[:groups], rest[groups:]
    next_f, next_a, courant, send_low, send_high, slab, level = rest
    row_count, count_y, _ = sum_f.shape
    band = pieces[0].shape[0] // row_count
    me = lax.axis_index("dom")
    for k in range(groups):
        start = pl.multiple_of((me ^ k) * band, 8)
        for x in range(0, row_count, 2):
            speed = pieces[-k][pl.ds(x * band, 2 * band), :].astype(F32)
            slab[x, pl.ds(start, band), :] = jnp.square(speed[:band])
            slab[x + 1, pl.ds(start, band), :] = jnp.square(speed[band:])

    @pl.loop(0, row_count)
    def _(x):
        for y in range(0, count_y, TILE):
            spot = pl.ds(y, TILE)
            factor = slab[x, pl.ds(anchors[0, 1] + y, TILE), :]
            courant[x, spot, :] = factor
            next_f[x, spot, :] = base_f[x, spot, :] + factor * sum_f[x, spot, :]
            next_a[x, spot, :] = base_a[x, spot, :] + factor * sum_a[x, spot, :]

    add_source(source, begin, wave, next_f, 0)
    per = HALO * count_y // GROUP
    for out_ref, first in ((send_low, 0), (send_high, row_count - HALO)):
        for f, ref in enumerate((next_f, next_a)):
            code_halos(lambda x: ref[x], range(first, first + HALO), out_ref, level, f * per)
        out_ref[2 * per * GROUP :, :] = level[...].astype(I16)


def between_kernel(p1, q1, p0, q0, prev_f, courant, hit, part_f, part_a, bend, pad):
    row_count, count_y, count_z = p1.shape
    masks = lane_masks(TILE, count_z)
    outer = jnp.zeros((HALO, pad.shape[1], count_z), F32)
    pad[0:HALO] = outer
    pad[HALO + row_count :] = outer
    for f, (now, out) in enumerate(((p1, part_f), (q1, part_a))):
        fill(pad, now)

        @pl.loop(0, row_count)
        def _(x):
            for y in range(0, count_y, TILE):
                spot = pl.ds(y, TILE)
                middle, summed = laplace_tile(pad, HALO + x, y, TILE, masks)
                value = courant[x, spot, :] * summed
                if f == 0:
                    bend[x, spot, :] = middle - 2.0 * p0[x, spot, :] + prev_f[x, spot, :]
                else:
                    value += hit[x, spot, :] + (2.0 * middle - q0[x, spot, :])
                out[x, spot, :] = value


def halo_terms(in_ref, scale_ref, f, spot_y, count_y, low):
    per = count_y // GROUP
    rows = []
    for layer in range(HALO):
        spot = (f * HALO + layer) * per + spot_y // GROUP
        code = in_ref[pl.ds(spot * GROUP, GROUP), :].astype(I32).astype(F32)
        rows.append(code * scale_ref[pl.ds(spot, 1), :])
    if low:
        rows = rows[::-1]
    return [sum(COEFFS[r + j] * rows[j] for j in range(HALO - r)) for r in range(HALO)]


def second_kernel(groups, anchors, source, begin, wave, p1, q1, p0, courant, part_f, part_a, bend, low, high, *rest):
    next_f, next_a, own = rest[:3]
    sends = rest[3 : 2 + groups]
    frame, scale_low, scale_high = rest[2 + groups :]
    row_count, count_y, count_z = p1.shape
    band = own.shape[0] // row_count
    load_scales(low, scale_low)
    load_scales(high, scale_high)
    edge = (frame.shape[1] - count_y) // 2
    frame[:, 0:edge, :] = jnp.zeros((row_count, edge, count_z), F32)
    frame[:, edge + count_y :, :] = jnp.zeros((row_count, edge, count_z), F32)
    for y in range(0, count_y, GROUP):
        spot = pl.ds(y, GROUP)
        for ref, scale, side in ((low, scale_low, True), (high, scale_high, False)):
            for f in range(2):
                for r, term in enumerate(halo_terms(ref, scale, f, y, count_y, side)):
                    x = r if side else row_count - 1 - r
                    term = courant[x, spot, :] * term
                    if f == 0:
                        frame[x, pl.ds(edge + y, GROUP), :] = part_f[x, spot, :] + term
                    else:
                        next_a[x, spot, :] = part_a[x, spot, :] + term

    add_source(source, begin, wave, frame, 1, edge)

    @pl.loop(0, row_count)
    def _(x):
        for y in range(0, count_y, TILE):
            spot = pl.ds(y, TILE)
            change = frame[x, pl.ds(edge + y, TILE), :]
            next_f[x, spot, :] = 2.0 * p1[x, spot, :] - p0[x, spot, :] + change
            image = q1[x, spot, :] * change + next_a[x, spot, :] * bend[x, spot, :]
            frame[x, pl.ds(edge + y, TILE), :] = image

    me = lax.axis_index("dom")
    for k in range(groups):
        start = edge - anchors[0, 1] + (me ^ k) * band
        values = [frame[x, pl.ds(start, band), :] for x in range(row_count)]
        if k == 0:
            for x in range(row_count):
                own[pl.ds(x * band, band), :] = values[x]
        else:
            code_rows(values, sends[k - 1], 0)


def hit_kernel(begin, cells, traces, first, second):
    row_count, count_y, count_z = first.shape
    x = cells[0:1, :] - lax.axis_index("dom") * row_count
    inside = (x >= 0) & (x < row_count)
    row = jnp.where(inside, x * count_y + cells[1:2, :], -1)
    depth = lax.broadcasted_iota(I32, (count_z, row.shape[1]), 0)
    at_depth = depth == cells[2:3, :]
    parts = []
    for k in range(STEPS):
        left = traces[pl.ds(begin[0] + (STEPS - 1 - k), 1), :]
        for _ in range(3):
            part = left.astype(BF16).astype(F32)
            parts.append(jnp.where(at_depth, part, 0.0).astype(BF16))
            left = left - part
    right = jnp.concatenate(parts, axis=0)

    @pl.loop(0, row_count)
    def _(i):
        cell = i * count_y + lax.broadcasted_iota(I32, (count_y, row.shape[1]), 0)
        left = jnp.where(cell == row, 1.0, 0.0).astype(BF16)
        got = lax.dot_general(left, right, (((1,), (1,)), ((), ())), preferred_element_type=F32)
        for k, out in enumerate((first, second)):
            base = 3 * k * count_z
            high = got[:, base : base + count_z]
            middle = got[:, base + count_z : base + 2 * count_z]
            low = got[:, base + 2 * count_z : base + 3 * count_z]
            out[i] = high + (middle + low)


SIZE_X, SIZE_Z, SIZE_C = 4, 4, 2


def place_of(shot):
    return shot // (SIZE_Z * SIZE_C), lax.rem(shot // SIZE_C, SIZE_Z), lax.rem(shot, SIZE_C)


def swap(axis, k):
    bits = k * {"x": SIZE_Z * SIZE_C, "z": SIZE_C, "c": 1}[axis]
    return [(shot, shot ^ bits) for shot in range(SIZE_X * SIZE_Z * SIZE_C)]


def pick_kernel(layout, row_count, anchors, *refs):
    count = len(layout)
    ins, outs, table = refs[:count], refs[count:-1], refs[-1]
    groups = len(outs)
    per = outs[0].shape[0] // row_count
    block = ins[0].shape[0] // len(layout[0])
    own = block // per
    x, z, c = place_of(lax.axis_index("shot"))
    me = lax.axis_index("dom")
    anchor = anchors[0, 0]
    first = anchor // own
    span = table.shape[0] // block
    for ref, owners in zip(ins, layout):
        for n, (dx, dz, dc) in enumerate(owners):
            place = ((x ^ dx) * SIZE_Z + (z ^ dz)) * SIZE_C + (c ^ dc) - first

            @pl.when((place >= 0) & (place < span))
            def _():
                start = pl.multiple_of(place * block, 8)
                table[pl.ds(start, block), :] = ref[pl.ds(n * block, block), :].astype(F32)

    offset = (anchor - first * own) * per
    for k in range(groups):
        start = pl.multiple_of(offset + (me ^ k) * (row_count * per), 8)
        outs[k][...] = table[pl.ds(start, row_count * per), :].astype(BF16)


def band_kernel(groups, row_count, block, anchors, own, *refs):
    got, (keep, send, table) = refs[: groups - 1], refs[groups - 1 :]
    per = own.shape[0] // row_count
    c = lax.rem(lax.axis_index("shot"), SIZE_C)
    me = lax.axis_index("dom")
    anchor = anchors[0, 0]
    first = anchor // (block // per)
    table[...] = jnp.zeros(table.shape, F32)
    offset = (anchor - first * (block // per)) * per
    for k in range(groups):
        base = offset + (me ^ k) * (row_count * per)
        if k == 0:
            table[pl.ds(pl.multiple_of(base, 8), row_count * per), :] = own[...]
        else:
            for n, value in enumerate(decode_rows(got[-k], row_count, per)):
                table[pl.ds(pl.multiple_of(base + n * per, 8), per), :] = value
    mine = lax.rem(c + first, SIZE_C)
    for i in range(keep.shape[0] // block):
        for out, parity in ((keep, mine), (send, 1 - mine)):
            start = pl.multiple_of((SIZE_C * i + parity) * block, 8)
            out[pl.ds(i * block, block), :] = table[pl.ds(start, block), :]


def core_kernel(block, per, anchors, other, keep, got, own, *refs):
    sends, total = refs[:-1], refs[-1]
    x, _, c = place_of(lax.axis_index("shot"))
    total[...] = jnp.zeros(total.shape, F32)
    for ref, place in ((keep, anchors), (got, other)):
        first = place[0, 0] // (block // per)
        low = (first + lax.rem(c + first, SIZE_C)) // SIZE_C
        for i in range(ref.shape[0] // block):
            spot = pl.ds(pl.multiple_of((low + i) * block, 8), block)
            total[spot, :] += ref[pl.ds(i * block, block), :]
    size = own.shape[0]
    own[...] = total[pl.ds(pl.multiple_of(x * size, 8), size), :]
    for k, send in enumerate(sends, 1):
        start = (x ^ k) * size
        values = [total[pl.ds(pl.multiple_of(start + n * per, 8), per), :] for n in range(size // per)]
        code_rows(values, send, 0)


def along_x_kernel(per, mine, *refs):
    got, rest = refs[: SIZE_X - 1], refs[SIZE_X - 1 :]
    own, sends, total = rest[0], rest[1:-1], rest[-1]
    total[...] = mine[...]
    for ref in got:
        for n, value in enumerate(decode_rows(ref, total.shape[0] // per, per)):
            total[pl.ds(n * per, per), :] += value
    _, z, _ = place_of(lax.axis_index("shot"))
    size = own.shape[0]
    own[...] = total[pl.ds(pl.multiple_of(z * size, 8), size), :]
    for k, send in enumerate(sends, 1):
        start = (z ^ k) * size
        values = [total[pl.ds(pl.multiple_of(start + n * per, 8), per), :] for n in range(size // per)]
        code_rows(values, send, 0)


def along_z_kernel(per, mine, *refs):
    got, out = refs[:-1], refs[-1]
    for parts in zip(range(mine.shape[0] // per), *[decode_rows(r, mine.shape[0] // per, per) for r in got]):
        n, values = parts[0], parts[1:]
        total = mine[pl.ds(n * per, per), :]
        for value in values:
            total += value
        out[pl.ds(n * per, per), :] = total


def across(groups, k):
    return [(i, i ^ k) for i in range(groups)]


def far_first(values):
    return sorted(values, reverse=True)


def exchange(parts, axis, pairs):
    got = {}
    for k in far_first(range(1, len(parts) + 1)):
        got[k] = lax.ppermute(parts[k - 1], axis, pairs(k))
    return [got[k] for k in sorted(got)]


def body(
    velocity,
    anchors,
    start_step,
    source,
    receivers,
    traces,
    wavelet,
    fwd_prev,
    fwd_now,
    adj_prev,
    adj_now,
):
    row_count, count_y, count_z = fwd_now.shape[1:]
    groups = lax.axis_size("dom")
    own_rows, band = velocity.shape[:2]
    block = own_rows * band
    piece = row_count * band
    p0, q0, p_prev, q_prev = fwd_now[0], adj_now[0], fwd_prev[0], adj_prev[0]
    scalars = (anchors, source, start_step, wavelet)
    up = [(i, i + 1) for i in range(groups - 1)]
    down = [(b, a) for a, b in up]

    along = {axis: functools.partial(swap, axis) for axis in "xzc"}
    between = functools.partial(across, groups)

    local = velocity.reshape(block, count_z)
    other = lax.ppermute(anchors, "shot", swap("c", 1))
    near = [local] + exchange([local] * (SIZE_Z - 1), "shot", along["z"])

    half = halo_rows(2 * HALO, count_y)
    code = struct((half, count_z), I16)
    levels = pltpu.VMEM((2 * HALO * count_y // GROUP, count_z), I32)
    low, high = call(encode_kernel, (code, code), (p0, q0), "vv", (levels,))
    from_low = lax.ppermute(high, "dom", up)
    from_high = lax.ppermute(low, "dom", down)

    line = jnp.concatenate(near, axis=0)
    line, other, low = lax.optimization_barrier((line, other, low))
    field = struct((row_count, count_y, count_z), F32)
    hits = call(hit_kernel, (field, field), (start_step, receivers[0], traces[0]), "svv")
    plane = [line] + exchange([line] * (SIZE_X - 1), "shot", along["x"])
    plane = list(lax.optimization_barrier((*plane, hits[0])))[:SIZE_X]
    plane += [lax.ppermute(part, "shot", swap("c", 1)) for part in plane]
    *plane, from_low, from_high = lax.optimization_barrier((*plane, from_low, from_high))
    layout = [[(dx, dz, dc) for dz in range(SIZE_Z)] for dc in range(SIZE_C) for dx in range(SIZE_X)]
    span = -(-(row_count * groups + own_rows - 1) // own_rows)
    span += span % SIZE_C
    table = pltpu.VMEM((span * block, count_z), F32)
    pieces = call(
        functools.partial(pick_kernel, layout, row_count),
        [struct((piece, count_z), BF16)] * groups,
        (anchors, *plane),
        "s" + "v" * len(plane),
        (table,),
    )
    pieces = [pieces[0]] + exchange(pieces[1:], "dom", between)[::-1]

    padded = pltpu.VMEM((row_count + 2 * HALO, count_y + 2 * PAD, count_z), F32)
    scale = pltpu.VMEM((2 * HALO * count_y // GROUP, count_z), F32)
    slab = pltpu.VMEM((row_count, groups * band, count_z), F32)
    sums = call(
        before_kernel,
        (field,) * 4,
        (p0, q0, p_prev, q_prev, from_low, from_high, hits[0]),
        "v" * 7,
        (padded, scale, scale),
    )
    p1, q1, courant, low, high = call(
        functools.partial(first_kernel, groups),
        (field, field, field, code, code),
        (*scalars, *sums, *pieces),
        "ssss" + "v" * (4 + groups),
        (slab, levels),
    )
    from_low = lax.ppermute(high, "dom", up)
    from_high = lax.ppermute(low, "dom", down)
    part_f, part_a, bend = call(
        between_kernel,
        (field,) * 3,
        (p1, q1, p0, q0, p_prev, courant, hits[1]),
        "v" * 7,
        (padded,),
    )

    edge = groups * band - count_y
    coded = struct((code_rows_of(row_count, band), count_z), I16)
    frame = pltpu.VMEM((row_count, count_y + 2 * edge, count_z), F32)
    p2, q2, own, *sends = call(
        functools.partial(second_kernel, groups),
        (field, field, struct((piece, count_z), F32), *[coded] * (groups - 1)),
        (*scalars, p1, q1, p0, courant, part_f, part_a, bend, from_low, from_high),
        "ssss" + "v" * 9,
        (frame, scale, scale),
    )
    got = exchange(sends, "dom", between)[::-1]

    part = struct((span // SIZE_C * block, count_z), F32)
    keep, send = call(
        functools.partial(band_kernel, groups, row_count, block),
        (part, part),
        (anchors, own, *got),
        "s" + "v" * groups,
        (table,),
    )
    got = lax.ppermute(send, "shot", swap("c", 1))

    size = SIZE_Z * block
    coded = struct((code_rows_of(size // band, band), count_z), I16)
    total = pltpu.VMEM(((SIZE_X * SIZE_Z + 1) * block, count_z), F32)
    own, *sends = call(
        functools.partial(core_kernel, block, band),
        (struct((size, count_z), F32), *[coded] * (SIZE_X - 1)),
        (anchors, other, keep, got),
        "ssvv",
        (total,),
    )
    got = exchange(sends, "shot", along["x"])[::-1]

    coded = struct((code_rows_of(own_rows, band), count_z), I16)
    own, *sends = call(
        functools.partial(along_x_kernel, band),
        (struct((block, count_z), F32), *[coded] * (SIZE_Z - 1)),
        (own, *got),
        "v" * SIZE_X,
        (pltpu.VMEM((size, count_z), F32),),
    )
    got = exchange(sends, "shot", along["z"])[::-1]

    (gradient,) = call(
        functools.partial(along_z_kernel, band),
        (struct((block, count_z), F32),),
        (own, *got),
        "v" * SIZE_Z,
    )
    return (p2[None], q2[None], gradient.reshape(own_rows, band, count_z))


def solution(mesh):
    placed = (
        P("shot", "dom", None),
        P("shot", None),
        P("shot"),
        P("shot", None),
        P("shot", None, None),
        P("shot", None, None),
        P(),
        P("shot", "dom", None, None),
        P("shot", "dom", None, None),
        P("shot", "dom", None, None),
        P("shot", "dom", None, None),
    )
    return jax.shard_map(
        body,
        mesh=mesh,
        in_specs=placed,
        out_specs=(
            P("shot", "dom", None, None),
            P("shot", "dom", None, None),
            P("shot", "dom", None),
        ),
        check_vma=False,
    )
```

```python
import functools

import jax
import jax.numpy as jnp
from jax import lax
from jax.experimental import pallas as pl
from jax.experimental.pallas import tpu as pltpu
from jax.sharding import PartitionSpec as P

STEPS = 2
CENTER = -205.0 / 72.0
COEFFS = (8.0 / 5.0, -1.0 / 5.0, 8.0 / 315.0, -1.0 / 560.0)

F32 = jnp.float32
BF16 = jnp.bfloat16
I16 = jnp.int16
I32 = jnp.int32

VMEM_LIMIT = 32 * 1024 * 1024
FLOOR = 1e-33
TOP = 32700.0
HALO = 4
GROUP = 32


def vmem():
    return pl.BlockSpec(memory_space=pltpu.VMEM)


def smem():
    return pl.BlockSpec(memory_space=pltpu.SMEM)


def call(kernel, outs, args, spaces, scratch=(), cost=1_000_000):
    moved = sum(a.size * a.dtype.itemsize for a in (*outs, *args))
    return pl.pallas_call(
        kernel,
        out_shape=list(outs),
        in_specs=[smem() if s == "s" else vmem() for s in spaces],
        out_specs=[vmem()] * len(outs),
        scratch_shapes=list(scratch),
        compiler_params=pltpu.CompilerParams(vmem_limit_bytes=VMEM_LIMIT),
        cost_estimate=pl.CostEstimate(flops=0, bytes_accessed=0, transcendentals=0),
    )(*args)


def struct(shape, dtype):
    return jax.ShapeDtypeStruct(shape, dtype)


def code_group(values):
    top = jnp.max(jnp.abs(values), axis=0, keepdims=True)
    level = jnp.ceil(jnp.log2(jnp.maximum(top, FLOOR)) * 256.0) + 1.0
    scaled = values * (TOP * jnp.exp2(level * (-1.0 / 256.0)))
    return jnp.round(scaled).astype(I32), level.astype(I32)


def code_rows(values, out_ref, base):
    band = values[0].shape[0]
    levels = []
    for n in range(0, len(values), 2):
        codes = []
        for value in values[n : n + 2]:
            code, level = code_group(value)
            codes.append(code)
            levels.append(level)
        out_ref[pl.ds(base + n * band, 2 * band), :] = jnp.concatenate(codes, axis=0).astype(I16)
    levels += [jnp.zeros((-len(levels) % 16, values[0].shape[1]), I32)]
    spot = pl.ds(base + len(values) * band, code_rows_of(len(values), band) - len(values) * band)
    out_ref[spot, :] = jnp.concatenate(levels, axis=0).astype(I16)


def code_rows_of(groups, band):
    return groups * band + groups + -groups % 16


def decode_rows(in_ref, groups, band):
    scales = decode_scale(in_ref[pl.ds(groups * band, groups + -groups % 16), :])
    for n in range(0, groups, 2):
        pair = in_ref[pl.ds(n * band, 2 * band), :].astype(I32).astype(F32)
        yield pair[:band] * scales[n : n + 1]
        yield pair[band:] * scales[n + 1 : n + 2]


def decode_scale(levels):
    return jnp.exp2(levels.astype(I32).astype(F32) * (1.0 / 256.0)) * (1.0 / TOP)


def code_halos(field, rows, out_ref, level_ref, base):
    for n, layer in enumerate(rows):
        value = field(layer)
        count = value.shape[0] // GROUP
        for g in range(count):
            code, level = code_group(value[g * GROUP : (g + 1) * GROUP])
            spot = base + n * count + g
            out_ref[pl.ds(spot * GROUP, GROUP), :] = code.astype(I16)
            level_ref[pl.ds(spot, 1), :] = level


def halo_rows(layers, count_y):
    groups = layers * count_y // GROUP
    return groups * GROUP + groups


def odd_place():
    return lax.rem(lax.axis_index("dom"), 2)


def code_edges(fields, out_refs, level_ref):
    row_count, count_y, _ = fields[0].shape
    per = HALO * count_y // GROUP
    odd = odd_place()
    for out_ref, high in zip(out_refs, (1 - odd, odd)):
        first = high * (row_count - HALO)
        for f, ref in enumerate(fields):
            code_halos(lambda x: ref[x], [first + n for n in range(HALO)], out_ref, level_ref, f * per)
        out_ref[2 * per * GROUP :, :] = level_ref[...].astype(I16)


def encode_kernel(now_f, now_a, one, two, level_ref):
    code_edges((now_f, now_a), (one, two), level_ref)


def decode_halo(in_ref, scale_ref, pad_ref, f, first, count_y):
    per = count_y // GROUP
    for layer in range(HALO):
        for g in range(per):
            spot = (f * HALO + layer) * per + g
            code = in_ref[pl.ds(spot * GROUP, GROUP), :].astype(I32).astype(F32)
            pad_ref[first + layer, pl.ds(PAD + g * GROUP, GROUP), :] = code * scale_ref[pl.ds(spot, 1), :]


PAD = 8


def laplace_tile(pad_ref, layer, y, rows, masks):
    middle = pad_ref[layer, pl.ds(PAD + y, rows), :]
    summed = (3.0 * CENTER) * middle
    for k in range(1, HALO + 1):
        up, down = masks[k - 1]
        count = middle.shape[1]
        part = pad_ref[layer + k, pl.ds(PAD + y, rows), :] + pad_ref[layer - k, pl.ds(PAD + y, rows), :]
        part += pad_ref[layer, pl.ds(PAD + y + k, rows), :] + pad_ref[layer, pl.ds(PAD + y - k, rows), :]
        part += jnp.where(up, pltpu.roll(middle, k, 1), 0.0)
        part += jnp.where(down, pltpu.roll(middle, count - k, 1), 0.0)
        summed += COEFFS[k - 1] * part
    return middle, summed


TILE = 32


def lane_masks(rows, count):
    lane = lax.broadcasted_iota(I32, (rows, count), 1)
    return [(lane >= k, lane < count - k) for k in range(1, HALO + 1)]


def fill(pad_ref, field_ref):
    row_count, count_y, count_z = field_ref.shape
    edge = jnp.zeros((pad_ref.shape[0], PAD, count_z), F32)
    pad_ref[:, 0:PAD, :] = edge
    pad_ref[:, PAD + count_y :, :] = edge
    for x in range(row_count):
        pad_ref[HALO + x, PAD : PAD + count_y, :] = field_ref[x]


def load_scales(in_ref, scale_ref):
    groups = scale_ref.shape[0]
    scale_ref[...] = decode_scale(in_ref[groups * GROUP :, :])


def add_source(source, start, wave, ref, k, edge=0):
    x = source[0, 0] - lax.axis_index("dom") * ref.shape[0]
    lane = lax.broadcasted_iota(I32, (1, ref.shape[2]), 1)

    @pl.when((x >= 0) & (x < ref.shape[0]))
    def _():
        y = source[0, 1] + edge
        row = ref[x, pl.ds(y, 1), :]
        ref[x, pl.ds(y, 1), :] = row + jnp.where(lane == source[0, 2], wave[start[0] + k], 0.0)


def before_kernel(now_f, now_a, prev_f, prev_a, one, two, hit, *rest):
    sum_f, sum_a, base_f, base_a, pad, scale_one, scale_two = rest
    row_count, count_y, count_z = now_f.shape
    masks = lane_masks(TILE, count_z)
    load_scales(one, scale_one)
    load_scales(two, scale_two)
    odd = odd_place()
    fields = ((now_f, prev_f, sum_f, base_f), (now_a, prev_a, sum_a, base_a))
    for f, (now, prev, total, base) in enumerate(fields):
        fill(pad, now)
        decode_halo(one, scale_one, pad, f, (1 - odd) * (HALO + row_count), count_y)
        decode_halo(two, scale_two, pad, f, odd * (HALO + row_count), count_y)

        @pl.loop(0, row_count)
        def _(x):
            for y in range(0, count_y, TILE):
                spot = pl.ds(y, TILE)
                middle, summed = laplace_tile(pad, HALO + x, y, TILE, masks)
                total[x, spot, :] = summed
                value = 2.0 * middle - prev[x, spot, :]
                base[x, spot, :] = value + hit[x, spot, :] if f else value


def first_kernel(halves, anchors, source, begin, wave, sum_f, sum_a, base_f, base_a, *rest):
    next_f, next_a, courant, one, two, slab, level = rest[-7:]
    pieces = rest[:-7]
    row_count, count_y, _ = sum_f.shape
    band = pieces[0].shape[0] // (row_count * halves)
    side = len(pieces)
    me = lax.rem(lax.axis_index("dom"), side)
    for k in range(side):
        for half in range(halves):
            start = pl.multiple_of((half * side + (me ^ k)) * band, 8)
            for x in range(0, row_count, 2):
                speed = pieces[-k][pl.ds((half * row_count + x) * band, 2 * band), :].astype(F32)
                slab[x, pl.ds(start, band), :] = jnp.square(speed[:band])
                slab[x + 1, pl.ds(start, band), :] = jnp.square(speed[band:])

    @pl.loop(0, row_count)
    def _(x):
        for y in range(0, count_y, TILE):
            spot = pl.ds(y, TILE)
            factor = slab[x, pl.ds(anchors[0, 1] + y, TILE), :]
            courant[x, spot, :] = factor
            next_f[x, spot, :] = base_f[x, spot, :] + factor * sum_f[x, spot, :]
            next_a[x, spot, :] = base_a[x, spot, :] + factor * sum_a[x, spot, :]

    add_source(source, begin, wave, next_f, 0)
    code_edges((next_f, next_a), (one, two), level)


def between_kernel(p1, q1, p0, q0, prev_f, courant, hit, part_f, part_a, bend, pad):
    row_count, count_y, count_z = p1.shape
    masks = lane_masks(TILE, count_z)
    outer = jnp.zeros((HALO, pad.shape[1], count_z), F32)
    pad[0:HALO] = outer
    pad[HALO + row_count :] = outer
    for f, (now, out) in enumerate(((p1, part_f), (q1, part_a))):
        fill(pad, now)

        @pl.loop(0, row_count)
        def _(x):
            for y in range(0, count_y, TILE):
                spot = pl.ds(y, TILE)
                middle, summed = laplace_tile(pad, HALO + x, y, TILE, masks)
                value = courant[x, spot, :] * summed
                if f == 0:
                    bend[x, spot, :] = middle - 2.0 * p0[x, spot, :] + prev_f[x, spot, :]
                else:
                    value += hit[x, spot, :] + (2.0 * middle - q0[x, spot, :])
                out[x, spot, :] = value


def halo_terms(in_ref, scale_ref, f, spot_y, count_y, low):
    per = count_y // GROUP
    rows = []
    for j in range(HALO):
        layer = j + low * (HALO - 1 - 2 * j)
        spot = (f * HALO + layer) * per + spot_y // GROUP
        code = in_ref[pl.ds(pl.multiple_of(spot * GROUP, GROUP), GROUP), :].astype(I32).astype(F32)
        rows.append(code * scale_ref[pl.ds(spot, 1), :])
    return [sum(COEFFS[r + j] * rows[j] for j in range(HALO - r)) for r in range(HALO)]


def second_kernel(groups, anchors, source, begin, wave, p1, q1, p0, courant, part_f, part_a, bend, one, two, *rest):
    next_f, next_a, own = rest[:3]
    sends = rest[3 : 2 + groups]
    frame, scale_one, scale_two = rest[2 + groups :]
    row_count, count_y, count_z = p1.shape
    band = own.shape[0] // row_count
    load_scales(one, scale_one)
    load_scales(two, scale_two)
    odd = odd_place()
    edge = (frame.shape[1] - count_y) // 2
    frame[:, 0:edge, :] = jnp.zeros((row_count, edge, count_z), F32)
    frame[:, edge + count_y :, :] = jnp.zeros((row_count, edge, count_z), F32)
    for y in range(0, count_y, GROUP):
        spot = pl.ds(y, GROUP)
        for ref, scale, low in ((one, scale_one, odd), (two, scale_two, 1 - odd)):
            for f in range(2):
                for r, term in enumerate(halo_terms(ref, scale, f, y, count_y, low)):
                    x = row_count - 1 - r + low * (2 * r + 1 - row_count)
                    term = courant[x, spot, :] * term
                    if f == 0:
                        frame[x, pl.ds(edge + y, GROUP), :] = part_f[x, spot, :] + term
                    else:
                        next_a[x, spot, :] = part_a[x, spot, :] + term

    add_source(source, begin, wave, frame, 1, edge)

    @pl.loop(0, row_count)
    def _(x):
        for y in range(0, count_y, TILE):
            spot = pl.ds(y, TILE)
            change = frame[x, pl.ds(edge + y, TILE), :]
            next_f[x, spot, :] = 2.0 * p1[x, spot, :] - p0[x, spot, :] + change
            image = q1[x, spot, :] * change + next_a[x, spot, :] * bend[x, spot, :]
            frame[x, pl.ds(edge + y, TILE), :] = image

    me = lax.axis_index("dom")
    for k in range(groups):
        start = edge - anchors[0, 1] + (me ^ k) * band
        values = [frame[x, pl.ds(start, band), :] for x in range(row_count)]
        if k == 0:
            for x in range(row_count):
                own[pl.ds(x * band, band), :] = values[x]
        else:
            code_rows(values, sends[k - 1], 0)


def hit_kernel(begin, cells, traces, first, second):
    row_count, count_y, count_z = first.shape
    x = cells[0:1, :] - lax.axis_index("dom") * row_count
    inside = (x >= 0) & (x < row_count)
    row = jnp.where(inside, x * count_y + cells[1:2, :], -1)
    depth = lax.broadcasted_iota(I32, (count_z, row.shape[1]), 0)
    at_depth = depth == cells[2:3, :]
    parts = []
    for k in range(STEPS):
        left = traces[pl.ds(begin[0] + (STEPS - 1 - k), 1), :]
        for _ in range(3):
            part = left.astype(BF16).astype(F32)
            parts.append(jnp.where(at_depth, part, 0.0).astype(BF16))
            left = left - part
    right = jnp.concatenate(parts, axis=0)

    @pl.loop(0, row_count)
    def _(i):
        cell = i * count_y + lax.broadcasted_iota(I32, (count_y, row.shape[1]), 0)
        left = jnp.where(cell == row, 1.0, 0.0).astype(BF16)
        got = lax.dot_general(left, right, (((1,), (1,)), ((), ())), preferred_element_type=F32)
        for k, out in enumerate((first, second)):
            base = 3 * k * count_z
            high = got[:, base : base + count_z]
            middle = got[:, base + count_z : base + 2 * count_z]
            low = got[:, base + 2 * count_z : base + 3 * count_z]
            out[i] = high + (middle + low)


SIZE_X, SIZE_Z, SIZE_C = 4, 4, 2
HALVES = 2


def place_of(shot):
    return shot // (SIZE_Z * SIZE_C), lax.rem(shot // SIZE_C, SIZE_Z), lax.rem(shot, SIZE_C)


def swap(axis, k):
    bits = k * {"x": SIZE_Z * SIZE_C, "z": SIZE_C, "c": 1}[axis]
    return [(shot, shot ^ bits) for shot in range(SIZE_X * SIZE_Z * SIZE_C)]


def join_kernel(*refs):
    size = refs[0].shape[0]
    for n, ref in enumerate(refs[:-1]):
        refs[-1][pl.ds(n * size, size), :] = ref[...]


def pick_kernel(layout, row_count, halves, anchors, *refs):
    count = len(layout)
    ins, outs, table = refs[:count], refs[count:-1], refs[-1]
    side = len(outs)
    piece = outs[0].shape[0] // halves
    per = piece // row_count
    block = ins[0].shape[0] // len(layout[0])
    own = block // per
    x, z, c = place_of(lax.axis_index("shot"))
    half, me = lax.axis_index("dom") // side, lax.rem(lax.axis_index("dom"), side)
    anchor = anchors[0, 0] + half * (side * row_count)
    first = anchor // own
    span = table.shape[1] // block
    for ref, owners in zip(ins, layout):
        for n, (dx, dz, dc, dh) in enumerate(owners):
            place = ((x ^ dx) * SIZE_Z + (z ^ dz)) * SIZE_C + (c ^ dc) - first

            @pl.when((place >= 0) & (place < span))
            def _():
                start = pl.multiple_of(place * block, 8)
                table[half ^ dh, pl.ds(start, block), :] = ref[pl.ds(n * block, block), :].astype(F32)

    offset = (anchor - first * own) * per
    for k in range(side):
        start = pl.multiple_of(offset + (me ^ k) * piece, 8)
        for h in range(halves):
            outs[k][pl.ds(h * piece, piece), :] = table[h, pl.ds(start, piece), :].astype(BF16)


def band_kernel(groups, row_count, block, anchors, own, *refs):
    got, (keep, send, table) = refs[: groups - 1], refs[groups - 1 :]
    per = own.shape[0] // row_count
    c = lax.rem(lax.axis_index("shot"), SIZE_C)
    me = lax.axis_index("dom")
    anchor = anchors[0, 0]
    first = anchor // (block // per)
    table[...] = jnp.zeros(table.shape, F32)
    offset = (anchor - first * (block // per)) * per
    for k in range(groups):
        base = offset + (me ^ k) * (row_count * per)
        if k == 0:
            table[pl.ds(pl.multiple_of(base, 8), row_count * per), :] = own[...]
        else:
            for n, value in enumerate(decode_rows(got[-k], row_count, per)):
                table[pl.ds(pl.multiple_of(base + n * per, 8), per), :] = value
    mine = lax.rem(c + first, SIZE_C)
    for i in range(keep.shape[0] // block):
        for out, parity in ((keep, mine), (send, 1 - mine)):
            start = pl.multiple_of((SIZE_C * i + parity) * block, 8)
            out[pl.ds(i * block, block), :] = table[pl.ds(start, block), :]


def core_kernel(block, per, anchors, other, keep, got, own, *refs):
    sends, total = refs[:-1], refs[-1]
    x, _, c = place_of(lax.axis_index("shot"))
    total[...] = jnp.zeros(total.shape, F32)
    for ref, place in ((keep, anchors), (got, other)):
        first = place[0, 0] // (block // per)
        low = (first + lax.rem(c + first, SIZE_C)) // SIZE_C
        for i in range(ref.shape[0] // block):
            spot = pl.ds(pl.multiple_of((low + i) * block, 8), block)
            total[spot, :] += ref[pl.ds(i * block, block), :]
    size = own.shape[0]
    own[...] = total[pl.ds(pl.multiple_of(x * size, 8), size), :]
    for k, send in enumerate(sends, 1):
        start = (x ^ k) * size
        values = [total[pl.ds(pl.multiple_of(start + n * per, 8), per), :] for n in range(size // per)]
        code_rows(values, send, 0)


def along_x_kernel(per, mine, *refs):
    got, rest = refs[: SIZE_X - 1], refs[SIZE_X - 1 :]
    own, sends, total = rest[0], rest[1:-1], rest[-1]
    total[...] = mine[...]
    for ref in got:
        for n, value in enumerate(decode_rows(ref, total.shape[0] // per, per)):
            total[pl.ds(n * per, per), :] += value
    _, z, _ = place_of(lax.axis_index("shot"))
    size = own.shape[0]
    own[...] = total[pl.ds(pl.multiple_of(z * size, 8), size), :]
    for k, send in enumerate(sends, 1):
        start = (z ^ k) * size
        values = [total[pl.ds(pl.multiple_of(start + n * per, 8), per), :] for n in range(size // per)]
        code_rows(values, send, 0)


def along_z_kernel(per, mine, *refs):
    got, out = refs[:-1], refs[-1]
    for parts in zip(range(mine.shape[0] // per), *[decode_rows(r, mine.shape[0] // per, per) for r in got]):
        n, values = parts[0], parts[1:]
        total = mine[pl.ds(n * per, per), :]
        for value in values:
            total += value
        out[pl.ds(n * per, per), :] = total


def swap_z(groups, k):
    shots, doms = (k % SIZE_Z) * SIZE_C, (k // SIZE_Z) * (groups // HALVES)
    return [
        (shot * groups + dom, (shot ^ shots) * groups + (dom ^ doms))
        for shot in range(SIZE_X * SIZE_Z * SIZE_C)
        for dom in range(groups)
    ]


def across(groups, k):
    return [(i, i ^ k) for i in range(groups)]


def far_first(values):
    return sorted(values, reverse=True)


def exchange(parts, axis, pairs):
    got = {}
    for k in far_first(range(1, len(parts) + 1)):
        got[k] = lax.ppermute(parts[k - 1], axis, pairs(k))
    return [got[k] for k in sorted(got)]


def body(
    velocity,
    anchors,
    start_step,
    source,
    receivers,
    traces,
    wavelet,
    fwd_prev,
    fwd_now,
    adj_prev,
    adj_now,
):
    row_count, count_y, count_z = fwd_now.shape[1:]
    groups = lax.axis_size("dom")
    own_rows, band = velocity.shape[:2]
    block = own_rows * band
    piece = row_count * band
    p0, q0, p_prev, q_prev = fwd_now[0], adj_now[0], fwd_prev[0], adj_prev[0]
    scalars = (anchors, source, start_step, wavelet)
    one_pairs = [(i, i ^ 1) for i in range(groups)]
    two_pairs = [(i, i + 1) for i in range(1, groups - 1, 2)]
    two_pairs += [(b, a) for a, b in two_pairs]

    along = {axis: functools.partial(swap, axis) for axis in "xzc"}
    between = functools.partial(across, groups)

    local = velocity.reshape(block, count_z)
    other = lax.ppermute(anchors, "shot", swap("c", 1))
    near = [local] + exchange([local] * (HALVES * SIZE_Z - 1), ("shot", "dom"), functools.partial(swap_z, groups))

    half = halo_rows(2 * HALO, count_y)
    code = struct((half, count_z), I16)
    levels = pltpu.VMEM((2 * HALO * count_y // GROUP, count_z), I32)
    one, two = call(encode_kernel, (code, code), (p0, q0), "vv", (levels,))
    from_one = lax.ppermute(one, "dom", one_pairs)
    from_two = lax.ppermute(two, "dom", two_pairs)

    (line,) = call(join_kernel, (struct((len(near) * block, count_z), BF16),), near, "v" * len(near))
    line, other, one = lax.optimization_barrier((line, other, one))
    field = struct((row_count, count_y, count_z), F32)
    hits = call(hit_kernel, (field, field), (start_step, receivers[0], traces[0]), "svv")
    plane = [line] + exchange([line] * (SIZE_X - 1), "shot", along["x"])
    plane = list(lax.optimization_barrier((*plane, hits[0])))[:SIZE_X]
    plane += [lax.ppermute(part, "shot", swap("c", 1)) for part in plane]
    *plane, from_one, from_two = lax.optimization_barrier((*plane, from_one, from_two))
    layout = [
        [(dx, k % SIZE_Z, dc, k // SIZE_Z) for k in range(HALVES * SIZE_Z)]
        for dc in range(SIZE_C)
        for dx in range(SIZE_X)
    ]
    span = -(-(row_count * groups + own_rows - 1) // own_rows)
    span += span % SIZE_C
    table = pltpu.VMEM((span * block, count_z), F32)
    side = groups // HALVES
    pieces = call(
        functools.partial(pick_kernel, layout, row_count, HALVES),
        [struct((HALVES * piece, count_z), BF16)] * side,
        (anchors, *plane),
        "s" + "v" * len(plane),
        (pltpu.VMEM((HALVES, -(-(row_count * side + own_rows - 1) // own_rows) * block, count_z), F32),),
    )
    pieces = [pieces[0]] + exchange(pieces[1:], "dom", between)[::-1]

    padded = pltpu.VMEM((row_count + 2 * HALO, count_y + 2 * PAD, count_z), F32)
    scale = pltpu.VMEM((2 * HALO * count_y // GROUP, count_z), F32)
    slab = pltpu.VMEM((row_count, groups * band, count_z), F32)
    sums = call(
        before_kernel,
        (field,) * 4,
        (p0, q0, p_prev, q_prev, from_one, from_two, hits[0]),
        "v" * 7,
        (padded, scale, scale),
    )
    p1, q1, courant, one, two = call(
        functools.partial(first_kernel, HALVES),
        (field, field, field, code, code),
        (*scalars, *sums, *pieces),
        "ssss" + "v" * (4 + side),
        (slab, levels),
    )
    from_one = lax.ppermute(one, "dom", one_pairs)
    from_two = lax.ppermute(two, "dom", two_pairs)
    part_f, part_a, bend = call(
        between_kernel,
        (field,) * 3,
        (p1, q1, p0, q0, p_prev, courant, hits[1]),
        "v" * 7,
        (padded,),
    )

    edge = groups * band - count_y
    coded = struct((code_rows_of(row_count, band), count_z), I16)
    frame = pltpu.VMEM((row_count, count_y + 2 * edge, count_z), F32)
    p2, q2, own, *sends = call(
        functools.partial(second_kernel, groups),
        (field, field, struct((piece, count_z), F32), *[coded] * (groups - 1)),
        (*scalars, p1, q1, p0, courant, part_f, part_a, bend, from_one, from_two),
        "ssss" + "v" * 9,
        (frame, scale, scale),
    )
    got = exchange(sends, "dom", between)[::-1]

    part = struct((span // SIZE_C * block, count_z), F32)
    keep, send = call(
        functools.partial(band_kernel, groups, row_count, block),
        (part, part),
        (anchors, own, *got),
        "s" + "v" * groups,
        (table,),
    )
    got = lax.ppermute(send, "shot", swap("c", 1))

    size = SIZE_Z * block
    coded = struct((code_rows_of(size // band, band), count_z), I16)
    total = pltpu.VMEM(((SIZE_X * SIZE_Z + 1) * block, count_z), F32)
    own, *sends = call(
        functools.partial(core_kernel, block, band),
        (struct((size, count_z), F32), *[coded] * (SIZE_X - 1)),
        (anchors, other, keep, got),
        "ssvv",
        (total,),
    )
    got = exchange(sends, "shot", along["x"])[::-1]

    coded = struct((code_rows_of(own_rows, band), count_z), I16)
    own, *sends = call(
        functools.partial(along_x_kernel, band),
        (struct((block, count_z), F32), *[coded] * (SIZE_Z - 1)),
        (own, *got),
        "v" * SIZE_X,
        (pltpu.VMEM((size, count_z), F32),),
    )
    got = exchange(sends, "shot", along["z"])[::-1]

    (gradient,) = call(
        functools.partial(along_z_kernel, band),
        (struct((block, count_z), F32),),
        (own, *got),
        "v" * SIZE_Z,
    )
    return (p2[None], q2[None], gradient.reshape(own_rows, band, count_z))


def solution(mesh):
    placed = (
        P("shot", "dom", None),
        P("shot", None),
        P("shot"),
        P("shot", None),
        P("shot", None, None),
        P("shot", None, None),
        P(),
        P("shot", "dom", None, None),
        P("shot", "dom", None, None),
        P("shot", "dom", None, None),
        P("shot", "dom", None, None),
    )
    return jax.shard_map(
        body,
        mesh=mesh,
        in_specs=placed,
        out_specs=(
            P("shot", "dom", None, None),
            P("shot", "dom", None, None),
            P("shot", "dom", None),
        ),
        check_vma=False,
    )
```

```python
import functools

import jax
import jax.numpy as jnp
from jax import lax
from jax.experimental import pallas as pl
from jax.experimental.pallas import tpu as pltpu
from jax.sharding import PartitionSpec as P

STEPS = 2
CENTER = -205.0 / 72.0
COEFFS = (8.0 / 5.0, -1.0 / 5.0, 8.0 / 315.0, -1.0 / 560.0)

F32 = jnp.float32
BF16 = jnp.bfloat16
I16 = jnp.int16
I32 = jnp.int32

VMEM_LIMIT = 32 * 1024 * 1024
FLOOR = 1e-33
TOP = 32700.0
HALO = 4
GROUP = 32


def vmem():
    return pl.BlockSpec(memory_space=pltpu.VMEM)


def smem():
    return pl.BlockSpec(memory_space=pltpu.SMEM)


def call(kernel, outs, args, spaces, scratch=(), cost=1_000_000):
    moved = sum(a.size * a.dtype.itemsize for a in (*outs, *args))
    return pl.pallas_call(
        kernel,
        out_shape=list(outs),
        in_specs=[smem() if s == "s" else vmem() for s in spaces],
        out_specs=[vmem()] * len(outs),
        scratch_shapes=list(scratch),
        compiler_params=pltpu.CompilerParams(vmem_limit_bytes=VMEM_LIMIT),
        cost_estimate=pl.CostEstimate(flops=0, bytes_accessed=0, transcendentals=0),
    )(*args)


def struct(shape, dtype):
    return jax.ShapeDtypeStruct(shape, dtype)


def code_group(values):
    top = jnp.max(jnp.abs(values), axis=0, keepdims=True)
    level = jnp.ceil(jnp.log2(jnp.maximum(top, FLOOR)) * 256.0) + 1.0
    scaled = values * (TOP * jnp.exp2(level * (-1.0 / 256.0)))
    return jnp.round(scaled).astype(I32), level.astype(I32)


def code_rows(values, out_ref, base):
    band = values[0].shape[0]
    levels = []
    for n in range(0, len(values), 2):
        codes = []
        for value in values[n : n + 2]:
            code, level = code_group(value)
            codes.append(code)
            levels.append(level)
        out_ref[pl.ds(base + n * band, 2 * band), :] = jnp.concatenate(codes, axis=0).astype(I16)
    levels += [jnp.zeros((-len(levels) % 16, values[0].shape[1]), I32)]
    spot = pl.ds(base + len(values) * band, code_rows_of(len(values), band) - len(values) * band)
    out_ref[spot, :] = jnp.concatenate(levels, axis=0).astype(I16)


def code_rows_of(groups, band):
    return groups * band + groups + -groups % 16


def decode_rows(in_ref, groups, band):
    scales = decode_scale(in_ref[pl.ds(groups * band, groups + -groups % 16), :])
    for n in range(0, groups, 2):
        pair = in_ref[pl.ds(n * band, 2 * band), :].astype(I32).astype(F32)
        yield pair[:band] * scales[n : n + 1]
        yield pair[band:] * scales[n + 1 : n + 2]


def decode_scale(levels):
    return jnp.exp2(levels.astype(I32).astype(F32) * (1.0 / 256.0)) * (1.0 / TOP)


def code_halos(field, rows, out_ref, level_ref, base):
    for n, layer in enumerate(rows):
        value = field(layer)
        count = value.shape[0] // GROUP
        for g in range(count):
            code, level = code_group(value[g * GROUP : (g + 1) * GROUP])
            spot = base + n * count + g
            out_ref[pl.ds(spot * GROUP, GROUP), :] = code.astype(I16)
            level_ref[pl.ds(spot, 1), :] = level


def halo_rows(layers, count_y):
    groups = layers * count_y // GROUP
    return groups * GROUP + groups


def odd_place():
    return lax.rem(lax.axis_index("dom"), 2)


def code_edges(fields, out_refs, level_ref):
    row_count, count_y, _ = fields[0].shape
    per = HALO * count_y // GROUP
    odd = odd_place()
    for out_ref, high in zip(out_refs, (1 - odd, odd)):
        first = high * (row_count - HALO)
        for f, ref in enumerate(fields):
            code_halos(lambda x: ref[x], [first + n for n in range(HALO)], out_ref, level_ref, f * per)
        out_ref[2 * per * GROUP :, :] = level_ref[...].astype(I16)


def encode_kernel(now_f, now_a, one, two, level_ref):
    code_edges((now_f, now_a), (one, two), level_ref)


PAD = 8


def laplace_tile(pad_ref, layer, y, rows, masks):
    middle = pad_ref[layer, pl.ds(PAD + y, rows), :]
    summed = (3.0 * CENTER) * middle
    for k in range(1, HALO + 1):
        up, down = masks[k - 1]
        count = middle.shape[1]
        part = pad_ref[layer + k, pl.ds(PAD + y, rows), :] + pad_ref[layer - k, pl.ds(PAD + y, rows), :]
        part += pad_ref[layer, pl.ds(PAD + y + k, rows), :] + pad_ref[layer, pl.ds(PAD + y - k, rows), :]
        part += jnp.where(up, pltpu.roll(middle, k, 1), 0.0)
        part += jnp.where(down, pltpu.roll(middle, count - k, 1), 0.0)
        summed += COEFFS[k - 1] * part
    return middle, summed


TILE = 32


def lane_masks(rows, count):
    lane = lax.broadcasted_iota(I32, (rows, count), 1)
    return [(lane >= k, lane < count - k) for k in range(1, HALO + 1)]


def fill(pad_ref, field_ref):
    row_count, count_y, count_z = field_ref.shape
    edge = jnp.zeros((pad_ref.shape[0], PAD, count_z), F32)
    pad_ref[:, 0:PAD, :] = edge
    pad_ref[:, PAD + count_y :, :] = edge
    for x in range(row_count):
        pad_ref[HALO + x, PAD : PAD + count_y, :] = field_ref[x]


def clear_outer(pad_ref):
    outer = jnp.zeros((HALO, *pad_ref.shape[1:]), F32)
    pad_ref[0:HALO] = outer
    pad_ref[pad_ref.shape[0] - HALO :] = outer


def load_scales(in_ref, scale_ref):
    groups = scale_ref.shape[0]
    scale_ref[...] = decode_scale(in_ref[groups * GROUP :, :])


def add_source(source, start, wave, ref, k, edge=0):
    x = source[0, 0] - lax.axis_index("dom") * ref.shape[0]
    lane = lax.broadcasted_iota(I32, (1, ref.shape[2]), 1)

    @pl.when((x >= 0) & (x < ref.shape[0]))
    def _():
        y = source[0, 1] + edge
        row = ref[x, pl.ds(y, 1), :]
        ref[x, pl.ds(y, 1), :] = row + jnp.where(lane == source[0, 2], wave[start[0] + k], 0.0)


def before_kernel(now_f, now_a, prev_f, prev_a, hit, sum_f, sum_a, base_f, base_a, pad):
    row_count, count_y, count_z = now_f.shape
    masks = lane_masks(TILE, count_z)
    clear_outer(pad)
    fields = ((now_f, prev_f, sum_f, base_f), (now_a, prev_a, sum_a, base_a))
    for f, (now, prev, total, base) in enumerate(fields):
        fill(pad, now)

        @pl.loop(0, row_count)
        def _(x):
            for y in range(0, count_y, TILE):
                spot = pl.ds(y, TILE)
                middle, summed = laplace_tile(pad, HALO + x, y, TILE, masks)
                total[x, spot, :] = summed
                value = 2.0 * middle - prev[x, spot, :]
                base[x, spot, :] = value + hit[x, spot, :] if f else value


def halo_terms(in_ref, scale_ref, f, spot_y, count_y, low):
    per = count_y // GROUP
    rows = []
    for j in range(HALO):
        layer = j + low * (HALO - 1 - 2 * j)
        spot = (f * HALO + layer) * per + spot_y // GROUP
        code = in_ref[pl.ds(pl.multiple_of(spot * GROUP, GROUP), GROUP), :].astype(I32).astype(F32)
        rows.append(code * scale_ref[pl.ds(spot, 1), :])
    return [sum(COEFFS[r + j] * rows[j] for j in range(HALO - r)) for r in range(HALO)]


def halo_tiles(refs, scales, row_count, count_y):
    for ref, scale in zip(refs, scales):
        load_scales(ref, scale)
    odd = odd_place()
    for y in range(0, count_y, GROUP):
        for ref, scale, low in zip(refs, scales, (odd, 1 - odd)):
            terms = [halo_terms(ref, scale, f, y, count_y, low) for f in range(2)]
            for r in range(HALO):
                yield row_count - 1 - r + low * (2 * r + 1 - row_count), y, terms[0][r], terms[1][r]


def first_kernel(halves, anchors, source, begin, wave, sum_f, sum_a, base_f, base_a, *rest):
    next_f, next_a, courant, one, two, slab, level, scale_one, scale_two = rest[-9:]
    halos, pieces = rest[:2], rest[2:-9]
    row_count, count_y, _ = sum_f.shape
    band = pieces[0].shape[0] // (row_count * halves)
    side = len(pieces)
    me = lax.rem(lax.axis_index("dom"), side)
    for k in range(side):
        for half in range(halves):
            start = pl.multiple_of((half * side + (me ^ k)) * band, 8)
            for x in range(0, row_count, 2):
                speed = pieces[-k][pl.ds((half * row_count + x) * band, 2 * band), :].astype(F32)
                slab[x, pl.ds(start, band), :] = jnp.square(speed[:band])
                slab[x + 1, pl.ds(start, band), :] = jnp.square(speed[band:])

    for x, y, term_f, term_a in halo_tiles(halos, (scale_one, scale_two), row_count, count_y):
        spot = pl.ds(y, GROUP)
        factor = slab[x, pl.ds(anchors[0, 1] + y, GROUP), :]
        courant[x, spot, :] = factor
        next_f[x, spot, :] = base_f[x, spot, :] + factor * (sum_f[x, spot, :] + term_f)
        next_a[x, spot, :] = base_a[x, spot, :] + factor * (sum_a[x, spot, :] + term_a)

    add_source(source, begin, wave, next_f, 0)
    code_edges((next_f, next_a), (one, two), level)


def between_kernel(p1, q1, p0, q0, prev_f, courant, hit, part_f, part_a, bend, pad):
    row_count, count_y, count_z = p1.shape
    masks = lane_masks(TILE, count_z)
    clear_outer(pad)
    for f, (now, out) in enumerate(((p1, part_f), (q1, part_a))):
        fill(pad, now)

        @pl.loop(0, row_count)
        def _(x):
            for y in range(0, count_y, TILE):
                spot = pl.ds(y, TILE)
                middle, summed = laplace_tile(pad, HALO + x, y, TILE, masks)
                value = courant[x, spot, :] * summed
                if f == 0:
                    bend[x, spot, :] = middle - 2.0 * p0[x, spot, :] + prev_f[x, spot, :]
                else:
                    value += hit[x, spot, :] + (2.0 * middle - q0[x, spot, :])
                out[x, spot, :] = value


def second_kernel(groups, anchors, source, begin, wave, p1, q1, p0, courant, part_f, part_a, bend, one, two, *rest):
    next_f, next_a, own = rest[:3]
    sends = rest[3 : 2 + groups]
    frame, scale_one, scale_two = rest[2 + groups :]
    row_count, count_y, count_z = p1.shape
    band = own.shape[0] // row_count
    edge = (frame.shape[1] - count_y) // 2
    frame[:, 0:edge, :] = jnp.zeros((row_count, edge, count_z), F32)
    frame[:, edge + count_y :, :] = jnp.zeros((row_count, edge, count_z), F32)
    for x, y, term_f, term_a in halo_tiles((one, two), (scale_one, scale_two), row_count, count_y):
        spot = pl.ds(y, GROUP)
        factor = courant[x, spot, :]
        frame[x, pl.ds(edge + y, GROUP), :] = part_f[x, spot, :] + factor * term_f
        next_a[x, spot, :] = part_a[x, spot, :] + factor * term_a

    add_source(source, begin, wave, frame, 1, edge)

    @pl.loop(0, row_count)
    def _(x):
        for y in range(0, count_y, TILE):
            spot = pl.ds(y, TILE)
            change = frame[x, pl.ds(edge + y, TILE), :]
            next_f[x, spot, :] = 2.0 * p1[x, spot, :] - p0[x, spot, :] + change
            image = q1[x, spot, :] * change + next_a[x, spot, :] * bend[x, spot, :]
            frame[x, pl.ds(edge + y, TILE), :] = image

    me = lax.axis_index("dom")
    for k in range(groups):
        start = edge - anchors[0, 1] + (me ^ k) * band
        values = [frame[x, pl.ds(start, band), :] for x in range(row_count)]
        if k == 0:
            for x in range(row_count):
                own[pl.ds(x * band, band), :] = values[x]
        else:
            code_rows(values, sends[k - 1], 0)


def hit_kernel(begin, cells, traces, first, second):
    row_count, count_y, count_z = first.shape
    x = cells[0:1, :] - lax.axis_index("dom") * row_count
    inside = (x >= 0) & (x < row_count)
    row = jnp.where(inside, x * count_y + cells[1:2, :], -1)
    depth = lax.broadcasted_iota(I32, (count_z, row.shape[1]), 0)
    at_depth = depth == cells[2:3, :]
    parts = []
    for k in range(STEPS):
        left = traces[pl.ds(begin[0] + (STEPS - 1 - k), 1), :]
        for _ in range(3):
            part = left.astype(BF16).astype(F32)
            parts.append(jnp.where(at_depth, part, 0.0).astype(BF16))
            left = left - part
    right = jnp.concatenate(parts, axis=0)

    @pl.loop(0, row_count)
    def _(i):
        cell = i * count_y + lax.broadcasted_iota(I32, (count_y, row.shape[1]), 0)
        left = jnp.where(cell == row, 1.0, 0.0).astype(BF16)
        got = lax.dot_general(left, right, (((1,), (1,)), ((), ())), preferred_element_type=F32)
        for k, out in enumerate((first, second)):
            base = 3 * k * count_z
            high = got[:, base : base + count_z]
            middle = got[:, base + count_z : base + 2 * count_z]
            low = got[:, base + 2 * count_z : base + 3 * count_z]
            out[i] = high + (middle + low)


SIZE_X, SIZE_Z, SIZE_C = 4, 4, 2
HALVES = 2


def place_of(shot):
    return shot // (SIZE_Z * SIZE_C), lax.rem(shot // SIZE_C, SIZE_Z), lax.rem(shot, SIZE_C)


def swap(axis, k):
    bits = k * {"x": SIZE_Z * SIZE_C, "z": SIZE_C, "c": 1}[axis]
    return [(shot, shot ^ bits) for shot in range(SIZE_X * SIZE_Z * SIZE_C)]


def join_kernel(*refs):
    size = refs[0].shape[0]
    for n, ref in enumerate(refs[:-1]):
        refs[-1][pl.ds(n * size, size), :] = ref[...]


def pick_kernel(layout, row_count, halves, anchors, *refs):
    count = len(layout)
    ins, outs, table = refs[:count], refs[count:-1], refs[-1]
    side = len(outs)
    piece = outs[0].shape[0] // halves
    per = piece // row_count
    block = ins[0].shape[0] // len(layout[0])
    own = block // per
    x, z, c = place_of(lax.axis_index("shot"))
    half, me = lax.axis_index("dom") // side, lax.rem(lax.axis_index("dom"), side)
    anchor = anchors[0, 0] + half * (side * row_count)
    first = anchor // own
    span = table.shape[1] // block
    for ref, owners in zip(ins, layout):
        for n, (dx, dz, dc, dh) in enumerate(owners):
            place = ((x ^ dx) * SIZE_Z + (z ^ dz)) * SIZE_C + (c ^ dc) - first

            @pl.when((place >= 0) & (place < span))
            def _():
                start = pl.multiple_of(place * block, 8)
                table[half ^ dh, pl.ds(start, block), :] = ref[pl.ds(n * block, block), :].astype(F32)

    offset = (anchor - first * own) * per
    for k in range(side):
        start = pl.multiple_of(offset + (me ^ k) * piece, 8)
        for h in range(halves):
            outs[k][pl.ds(h * piece, piece), :] = table[h, pl.ds(start, piece), :].astype(BF16)


def band_kernel(groups, row_count, block, anchors, own, *refs):
    got, (keep, send, table) = refs[: groups - 1], refs[groups - 1 :]
    per = own.shape[0] // row_count
    c = lax.rem(lax.axis_index("shot"), SIZE_C)
    me = lax.axis_index("dom")
    anchor = anchors[0, 0]
    first = anchor // (block // per)
    table[...] = jnp.zeros(table.shape, F32)
    offset = (anchor - first * (block // per)) * per
    for k in range(groups):
        base = offset + (me ^ k) * (row_count * per)
        if k == 0:
            table[pl.ds(pl.multiple_of(base, 8), row_count * per), :] = own[...]
        else:
            for n, value in enumerate(decode_rows(got[-k], row_count, per)):
                table[pl.ds(pl.multiple_of(base + n * per, 8), per), :] = value
    mine = lax.rem(c + first, SIZE_C)
    for i in range(keep.shape[0] // block):
        for out, parity in ((keep, mine), (send, 1 - mine)):
            start = pl.multiple_of((SIZE_C * i + parity) * block, 8)
            out[pl.ds(i * block, block), :] = table[pl.ds(start, block), :]


def core_kernel(block, per, anchors, other, keep, got, own, *refs):
    sends, total = refs[:-1], refs[-1]
    x, _, c = place_of(lax.axis_index("shot"))
    total[...] = jnp.zeros(total.shape, F32)
    for ref, place in ((keep, anchors), (got, other)):
        first = place[0, 0] // (block // per)
        low = (first + lax.rem(c + first, SIZE_C)) // SIZE_C
        for i in range(ref.shape[0] // block):
            spot = pl.ds(pl.multiple_of((low + i) * block, 8), block)
            total[spot, :] += ref[pl.ds(i * block, block), :]
    size = own.shape[0]
    own[...] = total[pl.ds(pl.multiple_of(x * size, 8), size), :]
    for k, send in enumerate(sends, 1):
        start = (x ^ k) * size
        values = [total[pl.ds(pl.multiple_of(start + n * per, 8), per), :] for n in range(size // per)]
        code_rows(values, send, 0)


def along_x_kernel(per, mine, *refs):
    got, rest = refs[: SIZE_X - 1], refs[SIZE_X - 1 :]
    own, sends, total = rest[0], rest[1:-1], rest[-1]
    total[...] = mine[...]
    for ref in got:
        for n, value in enumerate(decode_rows(ref, total.shape[0] // per, per)):
            total[pl.ds(n * per, per), :] += value
    _, z, _ = place_of(lax.axis_index("shot"))
    size = own.shape[0]
    own[...] = total[pl.ds(pl.multiple_of(z * size, 8), size), :]
    for k, send in enumerate(sends, 1):
        start = (z ^ k) * size
        values = [total[pl.ds(pl.multiple_of(start + n * per, 8), per), :] for n in range(size // per)]
        code_rows(values, send, 0)


def along_z_kernel(per, mine, *refs):
    got, out = refs[:-1], refs[-1]
    for parts in zip(range(mine.shape[0] // per), *[decode_rows(r, mine.shape[0] // per, per) for r in got]):
        n, values = parts[0], parts[1:]
        total = mine[pl.ds(n * per, per), :]
        for value in values:
            total += value
        out[pl.ds(n * per, per), :] = total


def swap_z(groups, k):
    shots, doms = (k % SIZE_Z) * SIZE_C, (k // SIZE_Z) * (groups // HALVES)
    return [
        (shot * groups + dom, (shot ^ shots) * groups + (dom ^ doms))
        for shot in range(SIZE_X * SIZE_Z * SIZE_C)
        for dom in range(groups)
    ]


def across(groups, k):
    return [(i, i ^ k) for i in range(groups)]


def far_first(values):
    return sorted(values, reverse=True)


def exchange(parts, axis, pairs):
    got = {}
    for k in far_first(range(1, len(parts) + 1)):
        got[k] = lax.ppermute(parts[k - 1], axis, pairs(k))
    return [got[k] for k in sorted(got)]


def body(
    velocity,
    anchors,
    start_step,
    source,
    receivers,
    traces,
    wavelet,
    fwd_prev,
    fwd_now,
    adj_prev,
    adj_now,
):
    row_count, count_y, count_z = fwd_now.shape[1:]
    groups = lax.axis_size("dom")
    own_rows, band = velocity.shape[:2]
    block = own_rows * band
    piece = row_count * band
    p0, q0, p_prev, q_prev = fwd_now[0], adj_now[0], fwd_prev[0], adj_prev[0]
    scalars = (anchors, source, start_step, wavelet)
    one_pairs = [(i, i ^ 1) for i in range(groups)]
    two_pairs = [(i, i + 1) for i in range(1, groups - 1, 2)]
    two_pairs += [(b, a) for a, b in two_pairs]

    along = {axis: functools.partial(swap, axis) for axis in "xzc"}
    between = functools.partial(across, groups)

    local = velocity.reshape(block, count_z)
    other = lax.ppermute(anchors, "shot", swap("c", 1))
    near = [local] + exchange([local] * (HALVES * SIZE_Z - 1), ("shot", "dom"), functools.partial(swap_z, groups))

    half = halo_rows(2 * HALO, count_y)
    code = struct((half, count_z), I16)
    levels = pltpu.VMEM((2 * HALO * count_y // GROUP, count_z), I32)
    one, two = call(encode_kernel, (code, code), (p0, q0), "vv", (levels,))
    from_one = lax.ppermute(one, "dom", one_pairs)
    from_two = lax.ppermute(two, "dom", two_pairs)

    lines = []
    for part in range(HALVES):
        blocks = near[part * SIZE_Z : (part + 1) * SIZE_Z]
        lines += call(join_kernel, (struct((SIZE_Z * block, count_z), BF16),), blocks, "v" * SIZE_Z)
    lines[1], other, one = lax.optimization_barrier((lines[1], other, one))
    field = struct((row_count, count_y, count_z), F32)
    hits = call(hit_kernel, (field, field), (start_step, receivers[0], traces[0]), "svv")
    padded = pltpu.VMEM((row_count + 2 * HALO, count_y + 2 * PAD, count_z), F32)
    sums = call(before_kernel, (field,) * 4, (p0, q0, p_prev, q_prev, hits[0]), "v" * 5, (padded,))
    planes = [[line] + exchange([line] * (SIZE_X - 1), "shot", along["x"]) for line in lines]
    planes[1] = list(lax.optimization_barrier((*planes[1], sums[0])))[:SIZE_X]
    plane = planes[0] + planes[1]
    plane += [lax.ppermute(part, "shot", swap("c", 1)) for part in plane]
    *plane, from_one, from_two = lax.optimization_barrier((*plane, from_one, from_two))
    layout = [
        [(dx, dz, dc, dh) for dz in range(SIZE_Z)]
        for dc in range(SIZE_C)
        for dh in range(HALVES)
        for dx in range(SIZE_X)
    ]
    side = groups // HALVES
    pieces = call(
        functools.partial(pick_kernel, layout, row_count, HALVES),
        [struct((HALVES * piece, count_z), BF16)] * side,
        (anchors, *plane),
        "s" + "v" * len(plane),
        (pltpu.VMEM((HALVES, -(-(row_count * side + own_rows - 1) // own_rows) * block, count_z), F32),),
    )
    pieces = [pieces[0]] + exchange(pieces[1:], "dom", between)[::-1]

    scale = pltpu.VMEM((2 * HALO * count_y // GROUP, count_z), F32)
    slab = pltpu.VMEM((row_count, groups * band, count_z), F32)
    p1, q1, courant, one, two = call(
        functools.partial(first_kernel, HALVES),
        (field, field, field, code, code),
        (*scalars, *sums, from_one, from_two, *pieces),
        "ssss" + "v" * (6 + side),
        (slab, levels, scale, scale),
    )
    from_one = lax.ppermute(one, "dom", one_pairs)
    from_two = lax.ppermute(two, "dom", two_pairs)
    part_f, part_a, bend = call(
        between_kernel,
        (field,) * 3,
        (p1, q1, p0, q0, p_prev, courant, hits[1]),
        "v" * 7,
        (padded,),
    )

    span = -(-(row_count * groups + own_rows - 1) // own_rows)
    span += span % SIZE_C
    table = pltpu.VMEM((span * block, count_z), F32)
    edge = groups * band - count_y
    coded = struct((code_rows_of(row_count, band), count_z), I16)
    frame = pltpu.VMEM((row_count, count_y + 2 * edge, count_z), F32)
    p2, q2, own, *sends = call(
        functools.partial(second_kernel, groups),
        (field, field, struct((piece, count_z), F32), *[coded] * (groups - 1)),
        (*scalars, p1, q1, p0, courant, part_f, part_a, bend, from_one, from_two),
        "ssss" + "v" * 9,
        (frame, scale, scale),
    )
    got = exchange(sends, "dom", between)[::-1]

    part = struct((span // SIZE_C * block, count_z), F32)
    keep, send = call(
        functools.partial(band_kernel, groups, row_count, block),
        (part, part),
        (anchors, own, *got),
        "s" + "v" * groups,
        (table,),
    )
    got = lax.ppermute(send, "shot", swap("c", 1))

    size = SIZE_Z * block
    coded = struct((code_rows_of(size // band, band), count_z), I16)
    total = pltpu.VMEM(((SIZE_X * SIZE_Z + 1) * block, count_z), F32)
    own, *sends = call(
        functools.partial(core_kernel, block, band),
        (struct((size, count_z), F32), *[coded] * (SIZE_X - 1)),
        (anchors, other, keep, got),
        "ssvv",
        (total,),
    )
    got = exchange(sends, "shot", along["x"])[::-1]

    coded = struct((code_rows_of(own_rows, band), count_z), I16)
    own, *sends = call(
        functools.partial(along_x_kernel, band),
        (struct((block, count_z), F32), *[coded] * (SIZE_Z - 1)),
        (own, *got),
        "v" * SIZE_X,
        (pltpu.VMEM((size, count_z), F32),),
    )
    got = exchange(sends, "shot", along["z"])[::-1]

    (gradient,) = call(
        functools.partial(along_z_kernel, band),
        (struct((block, count_z), F32),),
        (own, *got),
        "v" * SIZE_Z,
    )
    return (p2[None], q2[None], gradient.reshape(own_rows, band, count_z))


def solution(mesh):
    placed = (
        P("shot", "dom", None),
        P("shot", None),
        P("shot"),
        P("shot", None),
        P("shot", None, None),
        P("shot", None, None),
        P(),
        P("shot", "dom", None, None),
        P("shot", "dom", None, None),
        P("shot", "dom", None, None),
        P("shot", "dom", None, None),
    )
    return jax.shard_map(
        body,
        mesh=mesh,
        in_specs=placed,
        out_specs=(
            P("shot", "dom", None, None),
            P("shot", "dom", None, None),
            P("shot", "dom", None),
        ),
        check_vma=False,
    )
```

```python
import functools

import jax
import jax.numpy as jnp
from jax import lax
from jax.experimental import pallas as pl
from jax.experimental.pallas import tpu as pltpu
from jax.sharding import PartitionSpec as P

STEPS = 2
CENTER = -205.0 / 72.0
COEFFS = (8.0 / 5.0, -1.0 / 5.0, 8.0 / 315.0, -1.0 / 560.0)

F32 = jnp.float32
BF16 = jnp.bfloat16
I16 = jnp.int16
I32 = jnp.int32

VMEM_LIMIT = 32 * 1024 * 1024
FLOOR = 1e-33
TOP = 32700.0
MICROSECOND = 3_690_000
HALO = 4
GROUP = 32


def vmem():
    return pl.BlockSpec(memory_space=pltpu.VMEM)


def smem():
    return pl.BlockSpec(memory_space=pltpu.SMEM)


def call(kernel, outs, args, spaces, scratch=(), work=0):
    return pl.pallas_call(
        kernel,
        out_shape=list(outs),
        in_specs=[smem() if s == "s" else vmem() for s in spaces],
        out_specs=[vmem()] * len(outs),
        scratch_shapes=list(scratch),
        compiler_params=pltpu.CompilerParams(vmem_limit_bytes=VMEM_LIMIT),
        cost_estimate=pl.CostEstimate(flops=0, bytes_accessed=work * MICROSECOND, transcendentals=0),
    )(*args)


def struct(shape, dtype):
    return jax.ShapeDtypeStruct(shape, dtype)


def code_group(values):
    top = jnp.max(jnp.abs(values), axis=0, keepdims=True)
    level = jnp.ceil(jnp.log2(jnp.maximum(top, FLOOR)) * 256.0) + 1.0
    scaled = values * (TOP * jnp.exp2(level * (-1.0 / 256.0)))
    return jnp.round(scaled).astype(I32), level.astype(I32)


def code_rows(values, out_ref, base):
    band = values[0].shape[0]
    levels = []
    for n in range(0, len(values), 2):
        codes = []
        for value in values[n : n + 2]:
            code, level = code_group(value)
            codes.append(code)
            levels.append(level)
        out_ref[pl.ds(base + n * band, 2 * band), :] = jnp.concatenate(codes, axis=0).astype(I16)
    levels += [jnp.zeros((-len(levels) % 16, values[0].shape[1]), I32)]
    spot = pl.ds(base + len(values) * band, code_rows_of(len(values), band) - len(values) * band)
    out_ref[spot, :] = jnp.concatenate(levels, axis=0).astype(I16)


def code_rows_of(groups, band):
    return groups * band + groups + -groups % 16


def decode_rows(in_ref, groups, band):
    scales = decode_scale(in_ref[pl.ds(groups * band, groups + -groups % 16), :])
    for n in range(0, groups, 2):
        pair = in_ref[pl.ds(n * band, 2 * band), :].astype(I32).astype(F32)
        yield pair[:band] * scales[n : n + 1]
        yield pair[band:] * scales[n + 1 : n + 2]


def decode_scale(levels):
    return jnp.exp2(levels.astype(I32).astype(F32) * (1.0 / 256.0)) * (1.0 / TOP)


def code_halos(field, rows, out_ref, level_ref, base):
    for n, layer in enumerate(rows):
        value = field(layer)
        count = value.shape[0] // GROUP
        for g in range(count):
            code, level = code_group(value[g * GROUP : (g + 1) * GROUP])
            spot = base + n * count + g
            out_ref[pl.ds(spot * GROUP, GROUP), :] = code.astype(I16)
            level_ref[pl.ds(spot, 1), :] = level


def halo_rows(layers, count_y):
    groups = layers * count_y // GROUP
    return groups * GROUP + groups


def odd_place():
    return lax.rem(lax.axis_index("dom"), 2)


def code_edges(fields, out_refs, level_ref):
    row_count, count_y, _ = fields[0].shape
    per = HALO * count_y // GROUP
    odd = odd_place()
    for out_ref, high in zip(out_refs, (1 - odd, odd)):
        first = high * (row_count - HALO)
        for f, ref in enumerate(fields):
            code_halos(lambda x: ref[x], [first + n for n in range(HALO)], out_ref, level_ref, f * per)
        out_ref[2 * per * GROUP :, :] = level_ref[...].astype(I16)


def encode_kernel(now_f, now_a, one, two, level_ref):
    code_edges((now_f, now_a), (one, two), level_ref)


PAD = 8


def laplace_tile(pad_ref, layer, y, rows, masks):
    middle = pad_ref[layer, pl.ds(PAD + y, rows), :]
    summed = (3.0 * CENTER) * middle
    for k in range(1, HALO + 1):
        up, down = masks[k - 1]
        count = middle.shape[1]
        part = pad_ref[layer + k, pl.ds(PAD + y, rows), :] + pad_ref[layer - k, pl.ds(PAD + y, rows), :]
        part += pad_ref[layer, pl.ds(PAD + y + k, rows), :] + pad_ref[layer, pl.ds(PAD + y - k, rows), :]
        part += jnp.where(up, pltpu.roll(middle, k, 1), 0.0)
        part += jnp.where(down, pltpu.roll(middle, count - k, 1), 0.0)
        summed += COEFFS[k - 1] * part
    return middle, summed


TILE = 32


def lane_masks(rows, count):
    lane = lax.broadcasted_iota(I32, (rows, count), 1)
    return [(lane >= k, lane < count - k) for k in range(1, HALO + 1)]


def fill(pad_ref, field_ref):
    row_count, count_y, count_z = field_ref.shape
    edge = jnp.zeros((pad_ref.shape[0], PAD, count_z), F32)
    pad_ref[:, 0:PAD, :] = edge
    pad_ref[:, PAD + count_y :, :] = edge
    for x in range(row_count):
        pad_ref[HALO + x, PAD : PAD + count_y, :] = field_ref[x]


def clear_outer(pad_ref):
    outer = jnp.zeros((HALO, *pad_ref.shape[1:]), F32)
    pad_ref[0:HALO] = outer
    pad_ref[pad_ref.shape[0] - HALO :] = outer


def load_scales(in_ref, scale_ref):
    groups = scale_ref.shape[0]
    scale_ref[...] = decode_scale(in_ref[groups * GROUP :, :])


def add_source(source, start, wave, ref, k, edge=0):
    x = source[0, 0] - lax.axis_index("dom") * ref.shape[0]
    lane = lax.broadcasted_iota(I32, (1, ref.shape[2]), 1)

    @pl.when((x >= 0) & (x < ref.shape[0]))
    def _():
        y = source[0, 1] + edge
        row = ref[x, pl.ds(y, 1), :]
        ref[x, pl.ds(y, 1), :] = row + jnp.where(lane == source[0, 2], wave[start[0] + k], 0.0)


def before_kernel(now_f, now_a, prev_f, prev_a, hit, sum_f, sum_a, base_f, base_a, pad):
    row_count, count_y, count_z = now_f.shape
    masks = lane_masks(TILE, count_z)
    clear_outer(pad)
    fields = ((now_f, prev_f, sum_f, base_f), (now_a, prev_a, sum_a, base_a))
    for f, (now, prev, total, base) in enumerate(fields):
        fill(pad, now)

        @pl.loop(0, row_count)
        def _(x):
            for y in range(0, count_y, TILE):
                spot = pl.ds(y, TILE)
                middle, summed = laplace_tile(pad, HALO + x, y, TILE, masks)
                total[x, spot, :] = summed
                value = 2.0 * middle - prev[x, spot, :]
                base[x, spot, :] = value + hit[x, spot, :] if f else value


def halo_terms(in_ref, scale_ref, f, spot_y, count_y, low):
    per = count_y // GROUP
    rows = []
    for j in range(HALO):
        layer = j + low * (HALO - 1 - 2 * j)
        spot = (f * HALO + layer) * per + spot_y // GROUP
        code = in_ref[pl.ds(pl.multiple_of(spot * GROUP, GROUP), GROUP), :].astype(I32).astype(F32)
        rows.append(code * scale_ref[pl.ds(spot, 1), :])
    return [sum(COEFFS[r + j] * rows[j] for j in range(HALO - r)) for r in range(HALO)]


def halo_tiles(refs, scales, row_count, count_y):
    for ref, scale in zip(refs, scales):
        load_scales(ref, scale)
    odd = odd_place()
    for y in range(0, count_y, GROUP):
        for ref, scale, low in zip(refs, scales, (odd, 1 - odd)):
            terms = [halo_terms(ref, scale, f, y, count_y, low) for f in range(2)]
            for r in range(HALO):
                yield row_count - 1 - r + low * (2 * r + 1 - row_count), y, terms[0][r], terms[1][r]


def first_kernel(halves, anchors, source, begin, wave, sum_f, sum_a, base_f, base_a, *rest):
    next_f, next_a, courant, one, two, slab, level, scale_one, scale_two = rest[-9:]
    halos, pieces = rest[:2], rest[2:-9]
    row_count, count_y, _ = sum_f.shape
    band = pieces[0].shape[0] // (row_count * halves)
    side = len(pieces)
    me = lax.rem(lax.axis_index("dom"), side)
    for k in range(side):
        for half in range(halves):
            start = pl.multiple_of((half * side + (me ^ k)) * band, 8)
            for x in range(0, row_count, 2):
                speed = pieces[-k][pl.ds((half * row_count + x) * band, 2 * band), :].astype(F32)
                slab[x, pl.ds(start, band), :] = jnp.square(speed[:band])
                slab[x + 1, pl.ds(start, band), :] = jnp.square(speed[band:])

    for x, y, term_f, term_a in halo_tiles(halos, (scale_one, scale_two), row_count, count_y):
        spot = pl.ds(y, GROUP)
        factor = slab[x, pl.ds(anchors[0, 1] + y, GROUP), :]
        courant[x, spot, :] = factor
        next_f[x, spot, :] = base_f[x, spot, :] + factor * (sum_f[x, spot, :] + term_f)
        next_a[x, spot, :] = base_a[x, spot, :] + factor * (sum_a[x, spot, :] + term_a)

    add_source(source, begin, wave, next_f, 0)
    code_edges((next_f, next_a), (one, two), level)


def between_kernel(p1, q1, p0, q0, prev_f, courant, hit, part_f, part_a, bend, pad):
    row_count, count_y, count_z = p1.shape
    masks = lane_masks(TILE, count_z)
    clear_outer(pad)
    for f, (now, out) in enumerate(((p1, part_f), (q1, part_a))):
        fill(pad, now)

        @pl.loop(0, row_count)
        def _(x):
            for y in range(0, count_y, TILE):
                spot = pl.ds(y, TILE)
                middle, summed = laplace_tile(pad, HALO + x, y, TILE, masks)
                value = courant[x, spot, :] * summed
                if f == 0:
                    bend[x, spot, :] = middle - 2.0 * p0[x, spot, :] + prev_f[x, spot, :]
                else:
                    value += hit[x, spot, :] + (2.0 * middle - q0[x, spot, :])
                out[x, spot, :] = value


def second_kernel(groups, anchors, source, begin, wave, p1, q1, p0, courant, part_f, part_a, bend, one, two, *rest):
    next_f, next_a, own = rest[:3]
    sends = rest[3 : 2 + groups]
    frame, scale_one, scale_two = rest[2 + groups :]
    row_count, count_y, count_z = p1.shape
    band = own.shape[0] // row_count
    edge = (frame.shape[1] - count_y) // 2
    frame[:, 0:edge, :] = jnp.zeros((row_count, edge, count_z), F32)
    frame[:, edge + count_y :, :] = jnp.zeros((row_count, edge, count_z), F32)
    for x, y, term_f, term_a in halo_tiles((one, two), (scale_one, scale_two), row_count, count_y):
        spot = pl.ds(y, GROUP)
        factor = courant[x, spot, :]
        frame[x, pl.ds(edge + y, GROUP), :] = part_f[x, spot, :] + factor * term_f
        next_a[x, spot, :] = part_a[x, spot, :] + factor * term_a

    add_source(source, begin, wave, frame, 1, edge)

    @pl.loop(0, row_count)
    def _(x):
        for y in range(0, count_y, TILE):
            spot = pl.ds(y, TILE)
            change = frame[x, pl.ds(edge + y, TILE), :]
            next_f[x, spot, :] = 2.0 * p1[x, spot, :] - p0[x, spot, :] + change
            image = q1[x, spot, :] * change + next_a[x, spot, :] * bend[x, spot, :]
            frame[x, pl.ds(edge + y, TILE), :] = image

    me = lax.axis_index("dom")
    for k in range(groups):
        start = edge - anchors[0, 1] + (me ^ k) * band
        values = [frame[x, pl.ds(start, band), :] for x in range(row_count)]
        if k == 0:
            for x in range(row_count):
                own[pl.ds(x * band, band), :] = values[x]
        else:
            code_rows(values, sends[k - 1], 0)


def hit_kernel(begin, cells, traces, first, second):
    row_count, count_y, count_z = first.shape
    x = cells[0:1, :] - lax.axis_index("dom") * row_count
    inside = (x >= 0) & (x < row_count)
    row = jnp.where(inside, x * count_y + cells[1:2, :], -1)
    depth = lax.broadcasted_iota(I32, (count_z, row.shape[1]), 0)
    at_depth = depth == cells[2:3, :]
    parts = []
    for k in range(STEPS):
        left = traces[pl.ds(begin[0] + (STEPS - 1 - k), 1), :]
        for _ in range(3):
            part = left.astype(BF16).astype(F32)
            parts.append(jnp.where(at_depth, part, 0.0).astype(BF16))
            left = left - part
    right = jnp.concatenate(parts, axis=0)

    @pl.loop(0, row_count)
    def _(i):
        cell = i * count_y + lax.broadcasted_iota(I32, (count_y, row.shape[1]), 0)
        left = jnp.where(cell == row, 1.0, 0.0).astype(BF16)
        got = lax.dot_general(left, right, (((1,), (1,)), ((), ())), preferred_element_type=F32)
        for k, out in enumerate((first, second)):
            base = 3 * k * count_z
            high = got[:, base : base + count_z]
            middle = got[:, base + count_z : base + 2 * count_z]
            low = got[:, base + 2 * count_z : base + 3 * count_z]
            out[i] = high + (middle + low)


SIZE_X, SIZE_Z, SIZE_C = 4, 4, 2
HALVES = 2


def place_of(shot):
    return shot // (SIZE_Z * SIZE_C), lax.rem(shot // SIZE_C, SIZE_Z), lax.rem(shot, SIZE_C)


def swap(axis, k):
    bits = k * {"x": SIZE_Z * SIZE_C, "z": SIZE_C, "c": 1}[axis]
    return [(shot, shot ^ bits) for shot in range(SIZE_X * SIZE_Z * SIZE_C)]


def join_kernel(*refs):
    size = refs[0].shape[0]
    for n, ref in enumerate(refs[:-1]):
        refs[-1][pl.ds(n * size, size), :] = ref[...]


def pick_kernel(layout, row_count, halves, anchors, *refs):
    count = len(layout)
    ins, outs, table = refs[:count], refs[count:-1], refs[-1]
    side = len(outs)
    piece = outs[0].shape[0] // halves
    per = piece // row_count
    block = ins[0].shape[0] // len(layout[0])
    own = block // per
    x, z, c = place_of(lax.axis_index("shot"))
    half, me = lax.axis_index("dom") // side, lax.rem(lax.axis_index("dom"), side)
    anchor = anchors[0, 0] + half * (side * row_count)
    first = anchor // own
    span = table.shape[1] // block
    for ref, owners in zip(ins, layout):
        for n, (dx, dz, dc, dh) in enumerate(owners):
            place = ((x ^ dx) * SIZE_Z + (z ^ dz)) * SIZE_C + (c ^ dc) - first

            @pl.when((place >= 0) & (place < span))
            def _():
                start = pl.multiple_of(place * block, 8)
                table[half ^ dh, pl.ds(start, block), :] = ref[pl.ds(n * block, block), :].astype(F32)

    offset = (anchor - first * own) * per
    for k in range(side):
        start = pl.multiple_of(offset + (me ^ k) * piece, 8)
        for h in range(halves):
            outs[k][pl.ds(h * piece, piece), :] = table[h, pl.ds(start, piece), :].astype(BF16)


def band_kernel(groups, row_count, block, anchors, own, *refs):
    got, (keep, send, table) = refs[: groups - 1], refs[groups - 1 :]
    per = own.shape[0] // row_count
    c = lax.rem(lax.axis_index("shot"), SIZE_C)
    me = lax.axis_index("dom")
    anchor = anchors[0, 0]
    first = anchor // (block // per)
    table[...] = jnp.zeros(table.shape, F32)
    offset = (anchor - first * (block // per)) * per
    for k in range(groups):
        base = offset + (me ^ k) * (row_count * per)
        if k == 0:
            table[pl.ds(pl.multiple_of(base, 8), row_count * per), :] = own[...]
        else:
            for n, value in enumerate(decode_rows(got[-k], row_count, per)):
                table[pl.ds(pl.multiple_of(base + n * per, 8), per), :] = value
    mine = lax.rem(c + first, SIZE_C)
    for i in range(keep.shape[0] // block):
        for out, parity in ((keep, mine), (send, 1 - mine)):
            start = pl.multiple_of((SIZE_C * i + parity) * block, 8)
            out[pl.ds(i * block, block), :] = table[pl.ds(start, block), :]


def core_kernel(block, per, anchors, other, keep, got, own, *refs):
    sends, total = refs[:-1], refs[-1]
    x, _, c = place_of(lax.axis_index("shot"))
    total[...] = jnp.zeros(total.shape, F32)
    for ref, place in ((keep, anchors), (got, other)):
        first = place[0, 0] // (block // per)
        low = (first + lax.rem(c + first, SIZE_C)) // SIZE_C
        for i in range(ref.shape[0] // block):
            spot = pl.ds(pl.multiple_of((low + i) * block, 8), block)
            total[spot, :] += ref[pl.ds(i * block, block), :]
    size = own.shape[0]
    own[...] = total[pl.ds(pl.multiple_of(x * size, 8), size), :]
    for k, send in enumerate(sends, 1):
        start = (x ^ k) * size
        values = [total[pl.ds(pl.multiple_of(start + n * per, 8), per), :] for n in range(size // per)]
        code_rows(values, send, 0)


def along_x_kernel(per, mine, *refs):
    got, rest = refs[: SIZE_X - 1], refs[SIZE_X - 1 :]
    own, sends, total = rest[0], rest[1:-1], rest[-1]
    total[...] = mine[...]
    for ref in got:
        for n, value in enumerate(decode_rows(ref, total.shape[0] // per, per)):
            total[pl.ds(n * per, per), :] += value
    _, z, _ = place_of(lax.axis_index("shot"))
    size = own.shape[0]
    own[...] = total[pl.ds(pl.multiple_of(z * size, 8), size), :]
    for k, send in enumerate(sends, 1):
        start = (z ^ k) * size
        values = [total[pl.ds(pl.multiple_of(start + n * per, 8), per), :] for n in range(size // per)]
        code_rows(values, send, 0)


def along_z_kernel(per, mine, *refs):
    got, out = refs[:-1], refs[-1]
    for parts in zip(range(mine.shape[0] // per), *[decode_rows(r, mine.shape[0] // per, per) for r in got]):
        n, values = parts[0], parts[1:]
        total = mine[pl.ds(n * per, per), :]
        for value in values:
            total += value
        out[pl.ds(n * per, per), :] = total


def swap_z(groups, k):
    shots, doms = (k % SIZE_Z) * SIZE_C, (k // SIZE_Z) * (groups // HALVES)
    return [
        (shot * groups + dom, (shot ^ shots) * groups + (dom ^ doms))
        for shot in range(SIZE_X * SIZE_Z * SIZE_C)
        for dom in range(groups)
    ]


def across(groups, k):
    return [(i, i ^ k) for i in range(groups)]


def far_first(values):
    return sorted(values, reverse=True)


def exchange(parts, axis, pairs):
    got = {}
    for k in far_first(range(1, len(parts) + 1)):
        got[k] = lax.ppermute(parts[k - 1], axis, pairs(k))
    return [got[k] for k in sorted(got)]


def body(
    velocity,
    anchors,
    start_step,
    source,
    receivers,
    traces,
    wavelet,
    fwd_prev,
    fwd_now,
    adj_prev,
    adj_now,
):
    row_count, count_y, count_z = fwd_now.shape[1:]
    groups = lax.axis_size("dom")
    own_rows, band = velocity.shape[:2]
    block = own_rows * band
    piece = row_count * band
    p0, q0, p_prev, q_prev = fwd_now[0], adj_now[0], fwd_prev[0], adj_prev[0]
    scalars = (anchors, source, start_step, wavelet)
    one_pairs = [(i, i ^ 1) for i in range(groups)]
    two_pairs = [(i, i + 1) for i in range(1, groups - 1, 2)]
    two_pairs += [(b, a) for a, b in two_pairs]

    along = {axis: functools.partial(swap, axis) for axis in "xzc"}
    between = functools.partial(across, groups)

    local = velocity.reshape(block, count_z)
    near = [local] + exchange([local] * (HALVES * SIZE_Z - 1), ("shot", "dom"), functools.partial(swap_z, groups))

    half = halo_rows(2 * HALO, count_y)
    code = struct((half, count_z), I16)
    levels = pltpu.VMEM((2 * HALO * count_y // GROUP, count_z), I32)
    (line,) = call(join_kernel, (struct((len(near) * block, count_z), BF16),), near, "v" * len(near))

    p0, line = lax.optimization_barrier((p0, line))
    one, two = call(encode_kernel, (code, code), (p0, q0), "vv", (levels,))
    from_one = lax.ppermute(one, "dom", one_pairs)
    from_two = lax.ppermute(two, "dom", two_pairs)
    anchors, line = lax.optimization_barrier((anchors, line))
    other = lax.ppermute(anchors, "shot", swap("c", 1))
    field = struct((row_count, count_y, count_z), F32)
    hits = call(hit_kernel, (field, field), (start_step, receivers[0], traces[0]), "svv", work=4)
    padded = pltpu.VMEM((row_count + 2 * HALO, count_y + 2 * PAD, count_z), F32)
    sums = call(before_kernel, (field,) * 4, (p0, q0, p_prev, q_prev, hits[0]), "v" * 5, (padded,), work=6)
    plane = [line] + exchange([line] * (SIZE_X - 1), "shot", along["x"])
    plane, other = lax.optimization_barrier((plane, sums[0], other))[::2]
    plane += [lax.ppermute(part, "shot", swap("c", 1)) for part in plane]
    *plane, from_two, from_one = lax.optimization_barrier((*plane, from_two, from_one))
    layout = [
        [(dx, k % SIZE_Z, dc, k // SIZE_Z) for k in range(HALVES * SIZE_Z)]
        for dc in range(SIZE_C)
        for dx in range(SIZE_X)
    ]
    side = groups // HALVES
    pieces = call(
        functools.partial(pick_kernel, layout, row_count, HALVES),
        [struct((HALVES * piece, count_z), BF16)] * side,
        (anchors, *plane),
        "s" + "v" * len(plane),
        (pltpu.VMEM((HALVES, -(-(row_count * side + own_rows - 1) // own_rows) * block, count_z), F32),),
    )
    pieces = [pieces[0]] + exchange(pieces[1:], "dom", between)[::-1]

    scale = pltpu.VMEM((2 * HALO * count_y // GROUP, count_z), F32)
    slab = pltpu.VMEM((row_count, groups * band, count_z), F32)
    p1, q1, courant, one, two = call(
        functools.partial(first_kernel, HALVES),
        (field, field, field, code, code),
        (*scalars, *sums, from_one, from_two, *pieces),
        "ssss" + "v" * (6 + side),
        (slab, levels, scale, scale),
    )
    from_one = lax.ppermute(one, "dom", one_pairs)
    from_two = lax.ppermute(two, "dom", two_pairs)
    part_f, part_a, bend = call(
        between_kernel,
        (field,) * 3,
        (p1, q1, p0, q0, p_prev, courant, hits[1]),
        "v" * 7,
        (padded,),
        work=6,
    )

    span = -(-(row_count * groups + own_rows - 1) // own_rows)
    span += span % SIZE_C
    table = pltpu.VMEM((span * block, count_z), F32)
    edge = groups * band - count_y
    coded = struct((code_rows_of(row_count, band), count_z), I16)
    frame = pltpu.VMEM((row_count, count_y + 2 * edge, count_z), F32)
    p2, q2, own, *sends = call(
        functools.partial(second_kernel, groups),
        (field, field, struct((piece, count_z), F32), *[coded] * (groups - 1)),
        (*scalars, p1, q1, p0, courant, part_f, part_a, bend, from_one, from_two),
        "ssss" + "v" * 9,
        (frame, scale, scale),
    )
    got = exchange(sends, "dom", between)[::-1]

    part = struct((span // SIZE_C * block, count_z), F32)
    keep, send = call(
        functools.partial(band_kernel, groups, row_count, block),
        (part, part),
        (anchors, own, *got),
        "s" + "v" * groups,
        (table,),
    )
    got = lax.ppermute(send, "shot", swap("c", 1))

    size = SIZE_Z * block
    coded = struct((code_rows_of(size // band, band), count_z), I16)
    total = pltpu.VMEM(((SIZE_X * SIZE_Z + 1) * block, count_z), F32)
    own, *sends = call(
        functools.partial(core_kernel, block, band),
        (struct((size, count_z), F32), *[coded] * (SIZE_X - 1)),
        (anchors, other, keep, got),
        "ssvv",
        (total,),
    )
    got = exchange(sends, "shot", along["x"])[::-1]

    coded = struct((code_rows_of(own_rows, band), count_z), I16)
    own, *sends = call(
        functools.partial(along_x_kernel, band),
        (struct((block, count_z), F32), *[coded] * (SIZE_Z - 1)),
        (own, *got),
        "v" * SIZE_X,
        (pltpu.VMEM((size, count_z), F32),),
    )
    got = exchange(sends, "shot", along["z"])[::-1]

    (gradient,) = call(
        functools.partial(along_z_kernel, band),
        (struct((block, count_z), F32),),
        (own, *got),
        "v" * SIZE_Z,
    )
    return (p2[None], q2[None], gradient.reshape(own_rows, band, count_z))


def solution(mesh):
    placed = (
        P("shot", "dom", None),
        P("shot", None),
        P("shot"),
        P("shot", None),
        P("shot", None, None),
        P("shot", None, None),
        P(),
        P("shot", "dom", None, None),
        P("shot", "dom", None, None),
        P("shot", "dom", None, None),
        P("shot", "dom", None, None),
    )
    return jax.shard_map(
        body,
        mesh=mesh,
        in_specs=placed,
        out_specs=(
            P("shot", "dom", None, None),
            P("shot", "dom", None, None),
            P("shot", "dom", None),
        ),
        check_vma=False,
    )
```

```python
import functools

import jax
import jax.numpy as jnp
from jax import lax
from jax.experimental import pallas as pl
from jax.experimental.pallas import tpu as pltpu
from jax.sharding import PartitionSpec as P

STEPS = 2
CENTER = -205.0 / 72.0
COEFFS = (8.0 / 5.0, -1.0 / 5.0, 8.0 / 315.0, -1.0 / 560.0)

F32 = jnp.float32
BF16 = jnp.bfloat16
I16 = jnp.int16
I32 = jnp.int32

VMEM_LIMIT = 32 * 1024 * 1024
FLOOR = 1e-33
TOP = 32700.0
MICROSECOND = 3_690_000
HALO = 4
GROUP = 32


def vmem():
    return pl.BlockSpec(memory_space=pltpu.VMEM)


def smem():
    return pl.BlockSpec(memory_space=pltpu.SMEM)


def call(kernel, outs, args, spaces, scratch=(), work=0):
    return pl.pallas_call(
        kernel,
        out_shape=list(outs),
        in_specs=[smem() if s == "s" else vmem() for s in spaces],
        out_specs=[vmem()] * len(outs),
        scratch_shapes=list(scratch),
        compiler_params=pltpu.CompilerParams(vmem_limit_bytes=VMEM_LIMIT),
        cost_estimate=pl.CostEstimate(flops=0, bytes_accessed=work * MICROSECOND, transcendentals=0),
    )(*args)


def struct(shape, dtype):
    return jax.ShapeDtypeStruct(shape, dtype)


def code_group(values):
    top = jnp.max(jnp.abs(values), axis=0, keepdims=True)
    level = jnp.ceil(jnp.log2(jnp.maximum(top, FLOOR)) * 256.0) + 1.0
    scaled = values * (TOP * jnp.exp2(level * (-1.0 / 256.0)))
    return jnp.round(scaled).astype(I32), level.astype(I32)


def code_rows(values, out_ref, base):
    band = values[0].shape[0]
    levels = []
    for n in range(0, len(values), 2):
        codes = []
        for value in values[n : n + 2]:
            code, level = code_group(value)
            codes.append(code)
            levels.append(level)
        out_ref[pl.ds(base + n * band, 2 * band), :] = jnp.concatenate(codes, axis=0).astype(I16)
    levels += [jnp.zeros((-len(levels) % 16, values[0].shape[1]), I32)]
    spot = pl.ds(base + len(values) * band, code_rows_of(len(values), band) - len(values) * band)
    out_ref[spot, :] = jnp.concatenate(levels, axis=0).astype(I16)


def code_rows_of(groups, band):
    return groups * band + groups + -groups % 16


def decode_rows(in_ref, groups, band):
    scales = decode_scale(in_ref[pl.ds(groups * band, groups + -groups % 16), :])
    for n in range(0, groups, 2):
        pair = in_ref[pl.ds(n * band, 2 * band), :].astype(I32).astype(F32)
        yield pair[:band] * scales[n : n + 1]
        yield pair[band:] * scales[n + 1 : n + 2]


def decode_scale(levels):
    return jnp.exp2(levels.astype(I32).astype(F32) * (1.0 / 256.0)) * (1.0 / TOP)


def code_halos(field, rows, out_ref, level_ref, base):
    for n, layer in enumerate(rows):
        value = field(layer)
        count = value.shape[0] // GROUP
        for g in range(count):
            code, level = code_group(value[g * GROUP : (g + 1) * GROUP])
            spot = base + n * count + g
            out_ref[pl.ds(spot * GROUP, GROUP), :] = code.astype(I16)
            level_ref[pl.ds(spot, 1), :] = level


def halo_rows(layers, count_y):
    groups = layers * count_y // GROUP
    return groups * GROUP + groups


def odd_place():
    return lax.rem(lax.axis_index("dom"), 2)


def code_edges(fields, out_refs, level_ref):
    row_count, count_y, _ = fields[0].shape
    per = HALO * count_y // GROUP
    odd = odd_place()
    for out_ref, high in zip(out_refs, (1 - odd, odd)):
        first = high * (row_count - HALO)
        for f, ref in enumerate(fields):
            code_halos(lambda x: ref[x], [first + n for n in range(HALO)], out_ref, level_ref, f * per)
        out_ref[2 * per * GROUP :, :] = level_ref[...].astype(I16)


def encode_kernel(now_f, now_a, one, two, level_ref):
    code_edges((now_f, now_a), (one, two), level_ref)


PAD = 8


def laplace_tile(pad_ref, layer, y, rows, masks):
    middle = pad_ref[layer, pl.ds(PAD + y, rows), :]
    summed = (3.0 * CENTER) * middle
    for k in range(1, HALO + 1):
        up, down = masks[k - 1]
        count = middle.shape[1]
        part = pad_ref[layer + k, pl.ds(PAD + y, rows), :] + pad_ref[layer - k, pl.ds(PAD + y, rows), :]
        part += pad_ref[layer, pl.ds(PAD + y + k, rows), :] + pad_ref[layer, pl.ds(PAD + y - k, rows), :]
        part += jnp.where(up, pltpu.roll(middle, k, 1), 0.0)
        part += jnp.where(down, pltpu.roll(middle, count - k, 1), 0.0)
        summed += COEFFS[k - 1] * part
    return middle, summed


TILE = 32


def lane_masks(rows, count):
    lane = lax.broadcasted_iota(I32, (rows, count), 1)
    return [(lane >= k, lane < count - k) for k in range(1, HALO + 1)]


def fill(pad_ref, field_ref):
    row_count, count_y, count_z = field_ref.shape
    edge = jnp.zeros((pad_ref.shape[0], PAD, count_z), F32)
    pad_ref[:, 0:PAD, :] = edge
    pad_ref[:, PAD + count_y :, :] = edge
    for x in range(row_count):
        pad_ref[HALO + x, PAD : PAD + count_y, :] = field_ref[x]


def clear_outer(pad_ref):
    outer = jnp.zeros((HALO, *pad_ref.shape[1:]), F32)
    pad_ref[0:HALO] = outer
    pad_ref[pad_ref.shape[0] - HALO :] = outer


def load_scales(in_ref, scale_ref):
    groups = scale_ref.shape[0]
    scale_ref[...] = decode_scale(in_ref[groups * GROUP :, :])


def add_source(source, start, wave, ref, k, edge=0):
    x = source[0, 0] - lax.axis_index("dom") * ref.shape[0]
    lane = lax.broadcasted_iota(I32, (1, ref.shape[2]), 1)

    @pl.when((x >= 0) & (x < ref.shape[0]))
    def _():
        y = source[0, 1] + edge
        row = ref[x, pl.ds(y, 1), :]
        ref[x, pl.ds(y, 1), :] = row + jnp.where(lane == source[0, 2], wave[start[0] + k], 0.0)


def before_kernel(now_f, now_a, prev_f, prev_a, hit, sum_f, sum_a, base_f, base_a, pad):
    row_count, count_y, count_z = now_f.shape
    masks = lane_masks(TILE, count_z)
    clear_outer(pad)
    fields = ((now_f, prev_f, sum_f, base_f), (now_a, prev_a, sum_a, base_a))
    for f, (now, prev, total, base) in enumerate(fields):
        fill(pad, now)

        @pl.loop(0, row_count)
        def _(x):
            for y in range(0, count_y, TILE):
                spot = pl.ds(y, TILE)
                middle, summed = laplace_tile(pad, HALO + x, y, TILE, masks)
                total[x, spot, :] = summed
                value = 2.0 * middle - prev[x, spot, :]
                base[x, spot, :] = value + hit[x, spot, :] if f else value


def halo_terms(in_ref, scale_ref, f, spot_y, count_y, low):
    per = count_y // GROUP
    rows = []
    for j in range(HALO):
        layer = j + low * (HALO - 1 - 2 * j)
        spot = (f * HALO + layer) * per + spot_y // GROUP
        code = in_ref[pl.ds(pl.multiple_of(spot * GROUP, GROUP), GROUP), :].astype(I32).astype(F32)
        rows.append(code * scale_ref[pl.ds(spot, 1), :])
    return [sum(COEFFS[r + j] * rows[j] for j in range(HALO - r)) for r in range(HALO)]


def halo_tiles(refs, scales, row_count, count_y):
    for ref, scale in zip(refs, scales):
        load_scales(ref, scale)
    odd = odd_place()
    for y in range(0, count_y, GROUP):
        for ref, scale, low in zip(refs, scales, (odd, 1 - odd)):
            terms = [halo_terms(ref, scale, f, y, count_y, low) for f in range(2)]
            for r in range(HALO):
                yield row_count - 1 - r + low * (2 * r + 1 - row_count), y, terms[0][r], terms[1][r]


def first_kernel(halves, anchors, source, begin, wave, sum_f, sum_a, base_f, base_a, *rest):
    next_f, next_a, courant, one, two, slab, level, scale_one, scale_two = rest[-9:]
    halos, pieces = rest[:2], rest[2:-9]
    row_count, count_y, _ = sum_f.shape
    band = pieces[0].shape[0] // (row_count * halves)
    side = len(pieces)
    me = lax.rem(lax.axis_index("dom"), side)
    for k in range(side):
        for half in range(halves):
            start = pl.multiple_of((half * side + (me ^ k)) * band, 8)
            for x in range(0, row_count, 2):
                speed = pieces[-k][pl.ds((half * row_count + x) * band, 2 * band), :].astype(F32)
                slab[x, pl.ds(start, band), :] = jnp.square(speed[:band])
                slab[x + 1, pl.ds(start, band), :] = jnp.square(speed[band:])

    for x, y, term_f, term_a in halo_tiles(halos, (scale_one, scale_two), row_count, count_y):
        spot = pl.ds(y, GROUP)
        factor = slab[x, pl.ds(anchors[0, 1] + y, GROUP), :]
        courant[x, spot, :] = factor
        next_f[x, spot, :] = base_f[x, spot, :] + factor * (sum_f[x, spot, :] + term_f)
        next_a[x, spot, :] = base_a[x, spot, :] + factor * (sum_a[x, spot, :] + term_a)

    add_source(source, begin, wave, next_f, 0)
    code_edges((next_f, next_a), (one, two), level)


def between_kernel(p1, q1, p0, q0, prev_f, courant, hit, part_f, part_a, bend, pad):
    row_count, count_y, count_z = p1.shape
    masks = lane_masks(TILE, count_z)
    clear_outer(pad)
    for f, (now, out) in enumerate(((p1, part_f), (q1, part_a))):
        fill(pad, now)

        @pl.loop(0, row_count)
        def _(x):
            for y in range(0, count_y, TILE):
                spot = pl.ds(y, TILE)
                middle, summed = laplace_tile(pad, HALO + x, y, TILE, masks)
                value = courant[x, spot, :] * summed
                if f == 0:
                    bend[x, spot, :] = middle - 2.0 * p0[x, spot, :] + prev_f[x, spot, :]
                else:
                    value += hit[x, spot, :] + (2.0 * middle - q0[x, spot, :])
                out[x, spot, :] = value


def second_kernel(groups, anchors, source, begin, wave, p1, q1, p0, courant, part_f, part_a, bend, one, two, *rest):
    next_f, next_a, own = rest[:3]
    sends = rest[3 : 2 + groups]
    frame, scale_one, scale_two = rest[2 + groups :]
    row_count, count_y, count_z = p1.shape
    band = own.shape[0] // row_count
    edge = (frame.shape[1] - count_y) // 2
    frame[:, 0:edge, :] = jnp.zeros((row_count, edge, count_z), F32)
    frame[:, edge + count_y :, :] = jnp.zeros((row_count, edge, count_z), F32)
    for x, y, term_f, term_a in halo_tiles((one, two), (scale_one, scale_two), row_count, count_y):
        spot = pl.ds(y, GROUP)
        factor = courant[x, spot, :]
        frame[x, pl.ds(edge + y, GROUP), :] = part_f[x, spot, :] + factor * term_f
        next_a[x, spot, :] = part_a[x, spot, :] + factor * term_a

    add_source(source, begin, wave, frame, 1, edge)

    @pl.loop(0, row_count)
    def _(x):
        for y in range(0, count_y, TILE):
            spot = pl.ds(y, TILE)
            change = frame[x, pl.ds(edge + y, TILE), :]
            next_f[x, spot, :] = 2.0 * p1[x, spot, :] - p0[x, spot, :] + change
            image = q1[x, spot, :] * change + next_a[x, spot, :] * bend[x, spot, :]
            frame[x, pl.ds(edge + y, TILE), :] = image

    me = lax.axis_index("dom")
    for k in range(groups):
        start = edge - anchors[0, 1] + (me ^ k) * band
        values = [frame[x, pl.ds(start, band), :] for x in range(row_count)]
        if k == 0:
            for x in range(row_count):
                own[pl.ds(x * band, band), :] = values[x]
        else:
            code_rows(values, sends[k - 1], 0)


def hit_kernel(begin, cells, traces, first, second):
    row_count, count_y, count_z = first.shape
    x = cells[0:1, :] - lax.axis_index("dom") * row_count
    inside = (x >= 0) & (x < row_count)
    row = jnp.where(inside, x * count_y + cells[1:2, :], -1)
    depth = lax.broadcasted_iota(I32, (count_z, row.shape[1]), 0)
    at_depth = depth == cells[2:3, :]
    parts = []
    for k in range(STEPS):
        left = traces[pl.ds(begin[0] + (STEPS - 1 - k), 1), :]
        for _ in range(3):
            part = left.astype(BF16).astype(F32)
            parts.append(jnp.where(at_depth, part, 0.0).astype(BF16))
            left = left - part
    right = jnp.concatenate(parts, axis=0)

    @pl.loop(0, row_count)
    def _(i):
        cell = i * count_y + lax.broadcasted_iota(I32, (count_y, row.shape[1]), 0)
        left = jnp.where(cell == row, 1.0, 0.0).astype(BF16)
        got = lax.dot_general(left, right, (((1,), (1,)), ((), ())), preferred_element_type=F32)
        for k, out in enumerate((first, second)):
            base = 3 * k * count_z
            high = got[:, base : base + count_z]
            middle = got[:, base + count_z : base + 2 * count_z]
            low = got[:, base + 2 * count_z : base + 3 * count_z]
            out[i] = high + (middle + low)


SIZE_X, SIZE_Z, SIZE_C = 4, 4, 2
HALVES = 2


def place_of(shot):
    return shot // (SIZE_Z * SIZE_C), lax.rem(shot // SIZE_C, SIZE_Z), lax.rem(shot, SIZE_C)


def swap(axis, k):
    bits = k * {"x": SIZE_Z * SIZE_C, "z": SIZE_C, "c": 1}[axis]
    return [(shot, shot ^ bits) for shot in range(SIZE_X * SIZE_Z * SIZE_C)]


def join_kernel(*refs):
    size = refs[0].shape[0]
    for n, ref in enumerate(refs[:-1]):
        refs[-1][pl.ds(n * size, size), :] = ref[...]


def pick_kernel(layout, row_count, halves, anchors, *refs):
    count = len(layout)
    ins, outs, table = refs[:count], refs[count:-1], refs[-1]
    side = len(outs)
    piece = outs[0].shape[0] // halves
    per = piece // row_count
    block = ins[0].shape[0] // len(layout[0])
    own = block // per
    x, z, c = place_of(lax.axis_index("shot"))
    half, me = lax.axis_index("dom") // side, lax.rem(lax.axis_index("dom"), side)
    anchor = anchors[0, 0] + half * (side * row_count)
    first = anchor // own
    span = table.shape[1] // block
    for ref, owners in zip(ins, layout):
        for n, (dx, dz, dc, dh) in enumerate(owners):
            place = ((x ^ dx) * SIZE_Z + (z ^ dz)) * SIZE_C + (c ^ dc) - first

            @pl.when((place >= 0) & (place < span))
            def _():
                start = pl.multiple_of(place * block, 8)
                table[half ^ dh, pl.ds(start, block), :] = ref[pl.ds(n * block, block), :].astype(F32)

    offset = (anchor - first * own) * per
    for k in range(side):
        start = pl.multiple_of(offset + (me ^ k) * piece, 8)
        for h in range(halves):
            outs[k][pl.ds(h * piece, piece), :] = table[h, pl.ds(start, piece), :].astype(BF16)


def band_kernel(groups, row_count, block, anchors, own, *refs):
    got, (keep, send, table) = refs[: groups - 1], refs[groups - 1 :]
    per = own.shape[0] // row_count
    c = lax.rem(lax.axis_index("shot"), SIZE_C)
    me = lax.axis_index("dom")
    anchor = anchors[0, 0]
    first = anchor // (block // per)
    table[...] = jnp.zeros(table.shape, F32)
    offset = (anchor - first * (block // per)) * per
    for k in range(groups):
        base = offset + (me ^ k) * (row_count * per)
        if k == 0:
            table[pl.ds(pl.multiple_of(base, 8), row_count * per), :] = own[...]
        else:
            for n, value in enumerate(decode_rows(got[-k], row_count, per)):
                table[pl.ds(pl.multiple_of(base + n * per, 8), per), :] = value
    mine = lax.rem(c + first, SIZE_C)
    for i in range(keep.shape[0] // block):
        for out, parity in ((keep, mine), (send, 1 - mine)):
            start = pl.multiple_of((SIZE_C * i + parity) * block, 8)
            out[pl.ds(i * block, block), :] = table[pl.ds(start, block), :]


def core_kernel(block, per, anchors, other, keep, got, own, *refs):
    sends, total = refs[:-1], refs[-1]
    x, _, c = place_of(lax.axis_index("shot"))
    total[...] = jnp.zeros(total.shape, F32)
    for ref, place in ((keep, anchors), (got, other)):
        first = place[0, 0] // (block // per)
        low = (first + lax.rem(c + first, SIZE_C)) // SIZE_C
        for i in range(ref.shape[0] // block):
            spot = pl.ds(pl.multiple_of((low + i) * block, 8), block)
            total[spot, :] += ref[pl.ds(i * block, block), :]
    size = own.shape[0]
    own[...] = total[pl.ds(pl.multiple_of(x * size, 8), size), :]
    for k, send in enumerate(sends, 1):
        start = (x ^ k) * size
        values = [total[pl.ds(pl.multiple_of(start + n * per, 8), per), :] for n in range(size // per)]
        code_rows(values, send, 0)


def along_x_kernel(per, mine, *refs):
    got, rest = refs[: SIZE_X - 1], refs[SIZE_X - 1 :]
    own, sends, total = rest[0], rest[1:-1], rest[-1]
    total[...] = mine[...]
    for ref in got:
        for n, value in enumerate(decode_rows(ref, total.shape[0] // per, per)):
            total[pl.ds(n * per, per), :] += value
    _, z, _ = place_of(lax.axis_index("shot"))
    size = own.shape[0]
    own[...] = total[pl.ds(pl.multiple_of(z * size, 8), size), :]
    for k, send in enumerate(sends, 1):
        start = (z ^ k) * size
        values = [total[pl.ds(pl.multiple_of(start + n * per, 8), per), :] for n in range(size // per)]
        code_rows(values, send, 0)


def along_z_kernel(per, mine, *refs):
    got, out = refs[:-1], refs[-1]
    for parts in zip(range(mine.shape[0] // per), *[decode_rows(r, mine.shape[0] // per, per) for r in got]):
        n, values = parts[0], parts[1:]
        total = mine[pl.ds(n * per, per), :]
        for value in values:
            total += value
        out[pl.ds(n * per, per), :] = total


def swap_z(groups, k):
    shots, doms = (k % SIZE_Z) * SIZE_C, (k // SIZE_Z) * (groups // HALVES)
    return [
        (shot * groups + dom, (shot ^ shots) * groups + (dom ^ doms))
        for shot in range(SIZE_X * SIZE_Z * SIZE_C)
        for dom in range(groups)
    ]


def across(groups, k):
    return [(i, i ^ k) for i in range(groups)]


def far_first(values):
    return sorted(values, reverse=True)


def exchange(parts, axis, pairs):
    got = {}
    for k in far_first(range(1, len(parts) + 1)):
        got[k] = lax.ppermute(parts[k - 1], axis, pairs(k))
    return [got[k] for k in sorted(got)]


def body(
    velocity,
    anchors,
    start_step,
    source,
    receivers,
    traces,
    wavelet,
    fwd_prev,
    fwd_now,
    adj_prev,
    adj_now,
):
    row_count, count_y, count_z = fwd_now.shape[1:]
    groups = lax.axis_size("dom")
    own_rows, band = velocity.shape[:2]
    block = own_rows * band
    piece = row_count * band
    p0, q0, p_prev, q_prev = fwd_now[0], adj_now[0], fwd_prev[0], adj_prev[0]
    scalars = (anchors, source, start_step, wavelet)
    one_pairs = [(i, i ^ 1) for i in range(groups)]
    two_pairs = [(i, i + 1) for i in range(1, groups - 1, 2)]
    two_pairs += [(b, a) for a, b in two_pairs]

    along = {axis: functools.partial(swap, axis) for axis in "xzc"}
    between = functools.partial(across, groups)

    local = velocity.reshape(block, count_z)
    side = groups // HALVES
    far = lax.ppermute(local, "dom", between(side))
    lines = []
    for mine in (local, far):
        blocks = [mine] + exchange([mine] * (SIZE_Z - 1), "shot", along["z"])
        lines += call(join_kernel, (struct((SIZE_Z * block, count_z), BF16),), blocks, "v" * SIZE_Z)

    half = halo_rows(2 * HALO, count_y)
    code = struct((half, count_z), I16)
    levels = pltpu.VMEM((2 * HALO * count_y // GROUP, count_z), I32)
    one, two = call(encode_kernel, (code, code), (p0, q0), "vv", (levels,))
    from_one = lax.ppermute(one, "dom", one_pairs)
    from_two = lax.ppermute(two, "dom", two_pairs)
    near_anchors, _ = lax.optimization_barrier((anchors, lines[0]))
    other = lax.ppermute(near_anchors, "shot", swap("c", 1))
    field = struct((row_count, count_y, count_z), F32)
    hits = call(hit_kernel, (field, field), (start_step, receivers[0], traces[0]), "svv", work=4)
    padded = pltpu.VMEM((row_count + 2 * HALO, count_y + 2 * PAD, count_z), F32)
    sums = call(before_kernel, (field,) * 4, (p0, q0, p_prev, q_prev, hits[0]), "v" * 5, (padded,), work=6)
    plane = []
    for line in lines:
        plane += [line] + exchange([line] * (SIZE_X - 1), "shot", along["x"])
    plane, _, other, from_two, from_one = lax.optimization_barrier((plane, sums[0], other, from_two, from_one))
    plane += [lax.ppermute(part, "shot", swap("c", 1)) for part in plane]
    layout = [
        [(dx, dz, dc, dh) for dz in range(SIZE_Z)]
        for dc in range(SIZE_C)
        for dh in range(HALVES)
        for dx in range(SIZE_X)
    ]
    pieces = call(
        functools.partial(pick_kernel, layout, row_count, HALVES),
        [struct((HALVES * piece, count_z), BF16)] * side,
        (anchors, *plane),
        "s" + "v" * len(plane),
        (pltpu.VMEM((HALVES, -(-(row_count * side + own_rows - 1) // own_rows) * block, count_z), F32),),
    )
    pieces = [pieces[0]] + exchange(pieces[1:], "dom", between)[::-1]

    scale = pltpu.VMEM((2 * HALO * count_y // GROUP, count_z), F32)
    slab = pltpu.VMEM((row_count, groups * band, count_z), F32)
    p1, q1, courant, one, two = call(
        functools.partial(first_kernel, HALVES),
        (field, field, field, code, code),
        (*scalars, *sums, from_one, from_two, *pieces),
        "ssss" + "v" * (6 + side),
        (slab, levels, scale, scale),
    )
    from_one = lax.ppermute(one, "dom", one_pairs)
    from_two = lax.ppermute(two, "dom", two_pairs)
    part_f, part_a, bend = call(
        between_kernel,
        (field,) * 3,
        (p1, q1, p0, q0, p_prev, courant, hits[1]),
        "v" * 7,
        (padded,),
        work=6,
    )

    span = -(-(row_count * groups + own_rows - 1) // own_rows)
    span += span % SIZE_C
    table = pltpu.VMEM((span * block, count_z), F32)
    edge = groups * band - count_y
    coded = struct((code_rows_of(row_count, band), count_z), I16)
    frame = pltpu.VMEM((row_count, count_y + 2 * edge, count_z), F32)
    p2, q2, own, *sends = call(
        functools.partial(second_kernel, groups),
        (field, field, struct((piece, count_z), F32), *[coded] * (groups - 1)),
        (*scalars, p1, q1, p0, courant, part_f, part_a, bend, from_one, from_two),
        "ssss" + "v" * 9,
        (frame, scale, scale),
    )
    got = exchange(sends, "dom", between)[::-1]

    part = struct((span // SIZE_C * block, count_z), F32)
    keep, send = call(
        functools.partial(band_kernel, groups, row_count, block),
        (part, part),
        (anchors, own, *got),
        "s" + "v" * groups,
        (table,),
    )
    got = lax.ppermute(send, "shot", swap("c", 1))

    size = SIZE_Z * block
    coded = struct((code_rows_of(size // band, band), count_z), I16)
    total = pltpu.VMEM(((SIZE_X * SIZE_Z + 1) * block, count_z), F32)
    own, *sends = call(
        functools.partial(core_kernel, block, band),
        (struct((size, count_z), F32), *[coded] * (SIZE_X - 1)),
        (anchors, other, keep, got),
        "ssvv",
        (total,),
    )
    got = exchange(sends, "shot", along["x"])[::-1]

    coded = struct((code_rows_of(own_rows, band), count_z), I16)
    own, *sends = call(
        functools.partial(along_x_kernel, band),
        (struct((block, count_z), F32), *[coded] * (SIZE_Z - 1)),
        (own, *got),
        "v" * SIZE_X,
        (pltpu.VMEM((size, count_z), F32),),
    )
    got = exchange(sends, "shot", along["z"])[::-1]

    (gradient,) = call(
        functools.partial(along_z_kernel, band),
        (struct((block, count_z), F32),),
        (own, *got),
        "v" * SIZE_Z,
    )
    return (p2[None], q2[None], gradient.reshape(own_rows, band, count_z))


def solution(mesh):
    placed = (
        P("shot", "dom", None),
        P("shot", None),
        P("shot"),
        P("shot", None),
        P("shot", None, None),
        P("shot", None, None),
        P(),
        P("shot", "dom", None, None),
        P("shot", "dom", None, None),
        P("shot", "dom", None, None),
        P("shot", "dom", None, None),
    )
    return jax.shard_map(
        body,
        mesh=mesh,
        in_specs=placed,
        out_specs=(
            P("shot", "dom", None, None),
            P("shot", "dom", None, None),
            P("shot", "dom", None),
        ),
        check_vma=False,
    )
```

```python
import functools

import jax
import jax.numpy as jnp
from jax import lax
from jax.experimental import pallas as pl
from jax.experimental.pallas import tpu as pltpu
from jax.sharding import PartitionSpec as P

STEPS = 2
CENTER = -205.0 / 72.0
COEFFS = (8.0 / 5.0, -1.0 / 5.0, 8.0 / 315.0, -1.0 / 560.0)

F32 = jnp.float32
BF16 = jnp.bfloat16
I16 = jnp.int16
I32 = jnp.int32

VMEM_LIMIT = 32 * 1024 * 1024
FLOOR = 1e-33
TOP = 32700.0
HALO = 4
GROUP = 32


SPACES = {
    "v": pl.BlockSpec(memory_space=pltpu.VMEM),
    "s": pl.BlockSpec(memory_space=pltpu.SMEM),
    "a": pl.BlockSpec(memory_space=pl.ANY),
}


def call(kernel, outs, args, spaces, scratch=()):
    return pl.pallas_call(
        kernel,
        out_shape=list(outs),
        in_specs=[SPACES[s] for s in spaces],
        out_specs=[SPACES["v"]] * len(outs),
        scratch_shapes=list(scratch),
        compiler_params=pltpu.CompilerParams(vmem_limit_bytes=VMEM_LIMIT),
        cost_estimate=pl.CostEstimate(flops=0, bytes_accessed=0, transcendentals=0),
    )(*args)


def struct(shape, dtype):
    return jax.ShapeDtypeStruct(shape, dtype)


def code_group(values):
    top = jnp.max(jnp.abs(values), axis=0, keepdims=True)
    level = jnp.ceil(jnp.log2(jnp.maximum(top, FLOOR)) * 256.0) + 1.0
    scaled = values * (TOP * jnp.exp2(level * (-1.0 / 256.0)))
    return jnp.round(scaled).astype(I32), level.astype(I32)


def code_rows(values, out_ref, base):
    band = values[0].shape[0]
    levels = []
    for n in range(0, len(values), 2):
        codes = []
        for value in values[n : n + 2]:
            code, level = code_group(value)
            codes.append(code)
            levels.append(level)
        out_ref[pl.ds(base + n * band, 2 * band), :] = jnp.concatenate(codes, axis=0).astype(I16)
    levels += [jnp.zeros((-len(levels) % 16, values[0].shape[1]), I32)]
    spot = pl.ds(base + len(values) * band, code_rows_of(len(values), band) - len(values) * band)
    out_ref[spot, :] = jnp.concatenate(levels, axis=0).astype(I16)


def code_rows_of(groups, band):
    return groups * band + groups + -groups % 16


def decode_rows(in_ref, groups, band):
    scales = decode_scale(in_ref[pl.ds(groups * band, groups + -groups % 16), :])
    for n in range(0, groups, 2):
        pair = in_ref[pl.ds(n * band, 2 * band), :].astype(I32).astype(F32)
        yield pair[:band] * scales[n : n + 1]
        yield pair[band:] * scales[n + 1 : n + 2]


def decode_scale(levels):
    return jnp.exp2(levels.astype(I32).astype(F32) * (1.0 / 256.0)) * (1.0 / TOP)


def code_layers(layers, out_ref, level_ref):
    for n, (ref, layer) in enumerate(layers):
        value = ref[layer]
        count = value.shape[0] // GROUP
        for g in range(count):
            code, level = code_group(value[g * GROUP : (g + 1) * GROUP])
            out_ref[pl.ds((n * count + g) * GROUP, GROUP), :] = code.astype(I16)
            level_ref[pl.ds(n * count + g, 1), :] = level
    groups = len(layers) * count
    out_ref[groups * GROUP :, :] = level_ref[0:groups, :].astype(I16)


def halo_rows(layers, count_y):
    groups = layers * count_y // GROUP
    return groups * GROUP + groups


def odd_place():
    return lax.rem(lax.axis_index("dom"), 2)


def at_border():
    me, middle = lax.axis_index("dom"), lax.axis_size("dom") // 2
    return (me == middle) | (me == middle - 1)


def encode_kernel(now_f, now_a, prev_f, prev_a, one, two, wide, hold_f, hold_a, past_f, past_a, level_ref, arrived):
    odd = odd_place()
    edge = pl.ds(odd * HALO, HALO)
    loads = [
        pltpu.make_async_copy(source, target, arrived.at[n])
        for n, (source, target) in enumerate(
            ((now_f, hold_f), (now_a, hold_a), (prev_f.at[edge], past_f), (prev_a.at[edge], past_a))
        )
    ]
    for load in loads:
        load.start()
    for load in loads:
        load.wait()
    near_one = [(ref, (1 - odd) * HALO + n) for ref in (hold_f, hold_a) for n in range(HALO)]
    near_two = [(ref, odd * HALO + n) for ref in (hold_f, hold_a) for n in range(HALO)]
    past_two = [(ref, n) for ref in (past_f, past_a) for n in range(HALO)]

    @pl.when(at_border())
    def _():
        code_layers(near_two + near_one + past_two, wide, level_ref)

    @pl.when(jnp.logical_not(at_border()))
    def _():
        code_layers(near_two, two, level_ref)

    code_layers(near_one, one, level_ref)


PAD = 8


def laplace_tile(pad_ref, layer, y, rows, masks):
    middle = pad_ref[layer, pl.ds(PAD + y, rows), :]
    summed = (3.0 * CENTER) * middle
    for k in range(1, HALO + 1):
        up, down = masks[k - 1]
        count = middle.shape[1]
        part = pad_ref[layer + k, pl.ds(PAD + y, rows), :] + pad_ref[layer - k, pl.ds(PAD + y, rows), :]
        part += pad_ref[layer, pl.ds(PAD + y + k, rows), :] + pad_ref[layer, pl.ds(PAD + y - k, rows), :]
        part += jnp.where(up, pltpu.roll(middle, k, 1), 0.0)
        part += jnp.where(down, pltpu.roll(middle, count - k, 1), 0.0)
        summed += COEFFS[k - 1] * part
    return middle, summed


TILE = 32


def lane_masks(rows, count):
    lane = lax.broadcasted_iota(I32, (rows, count), 1)
    return [(lane >= k, lane < count - k) for k in range(1, HALO + 1)]


def fill(pad_ref, field_ref):
    row_count, count_y, count_z = field_ref.shape
    edge = jnp.zeros((pad_ref.shape[0], PAD, count_z), F32)
    pad_ref[:, 0:PAD, :] = edge
    pad_ref[:, PAD + count_y :, :] = edge
    for x in range(row_count):
        pad_ref[HALO + x, PAD : PAD + count_y, :] = field_ref[x]


def clear_outer(pad_ref):
    outer = jnp.zeros((HALO, *pad_ref.shape[1:]), F32)
    pad_ref[0:HALO] = outer
    pad_ref[pad_ref.shape[0] - HALO :] = outer


def load_scales(in_ref, scale_ref):
    groups = scale_ref.shape[0]
    base = in_ref.shape[0] // (GROUP + 1) * GROUP
    scale_ref[...] = decode_scale(in_ref[base : base + groups, :])


def load_codes(in_ref, code_ref, scale_ref):
    code_ref[...] = in_ref[0 : code_ref.shape[0], :]
    load_scales(in_ref, scale_ref)


def load_second(two, wide, code_ref, scale_ref):
    @pl.when(jnp.logical_not(at_border()))
    def _():
        load_codes(two, code_ref, scale_ref)

    @pl.when(at_border())
    def _():
        load_codes(wide, code_ref, scale_ref)


def add_source(source, start, wave, ref, k, first, edge=0):
    x = source[0, 0] - first
    lane = lax.broadcasted_iota(I32, (1, ref.shape[2]), 1)

    @pl.when((x >= 0) & (x < ref.shape[0]))
    def _():
        y = source[0, 1] + edge
        row = ref[x, pl.ds(y, 1), :]
        ref[x, pl.ds(y, 1), :] = row + jnp.where(lane == source[0, 2], wave[start[0] + k], 0.0)


def before_kernel(now_f, now_a, prev_f, prev_a, hit, sum_f, sum_a, base_f, base_a, pad):
    row_count, count_y, count_z = now_f.shape
    masks = lane_masks(TILE, count_z)
    clear_outer(pad)
    fields = ((now_f, prev_f, sum_f, base_f), (now_a, prev_a, sum_a, base_a))
    for f, (now, prev, total, base) in enumerate(fields):
        fill(pad, now)

        @pl.loop(0, row_count)
        def _(x):
            for y in range(0, count_y, TILE):
                spot = pl.ds(y, TILE)
                middle, summed = laplace_tile(pad, HALO + x, y, TILE, masks)
                total[x, spot, :] = summed
                value = 2.0 * middle - prev[x, spot, :]
                base[x, spot, :] = value + hit[x, spot, :] if f else value


def halo_terms(in_ref, scale_ref, f, spot_y, count_y, low):
    per = count_y // GROUP
    rows = []
    for j in range(HALO):
        layer = j + low * (HALO - 1 - 2 * j)
        spot = (f * HALO + layer) * per + spot_y // GROUP
        code = in_ref[pl.ds(pl.multiple_of(spot * GROUP, GROUP), GROUP), :].astype(I32).astype(F32)
        rows.append(code * scale_ref[pl.ds(spot, 1), :])
    return [sum(COEFFS[r + j] * rows[j] for j in range(HALO - r)) for r in range(HALO)]


def halo_tiles(ref, scale, low, row_count, count_y):
    for y in range(0, count_y, GROUP):
        terms = [halo_terms(ref, scale, f, y, count_y, low) for f in range(2)]
        for r in range(HALO):
            yield row_count - 1 - r + low * (2 * r + 1 - row_count), y, terms[0][r], terms[1][r]


def square_speed(pieces, halves, slab):
    row_count = slab.shape[0]
    band = pieces[0].shape[0] // (row_count * halves)
    side = len(pieces)
    me = lax.rem(lax.axis_index("dom"), side)
    for k in range(side):
        for half in range(halves):
            start = pl.multiple_of((half * side + (me ^ k)) * band, 8)
            for x in range(0, row_count, 2):
                speed = pieces[-k][pl.ds((half * row_count + x) * band, 2 * band), :].astype(F32)
                slab[x, pl.ds(start, band), :] = jnp.square(speed[:band])
                slab[x + 1, pl.ds(start, band), :] = jnp.square(speed[band:])


def step_rows(ref, scale, low, anchors, slab, terms, nexts, courant, shift):
    sum_f, sum_a, base_f, base_a = terms
    row_count, count_y, _ = sum_f.shape
    for x, y, term_f, term_a in halo_tiles(ref, scale, low, row_count, count_y):
        spot = pl.ds(y, GROUP)
        factor = slab[x, pl.ds(anchors[0, 1] + y, GROUP), :]
        courant[x - shift, spot, :] = factor
        nexts[0][x - shift, spot, :] = base_f[x, spot, :] + factor * (sum_f[x, spot, :] + term_f)
        nexts[1][x - shift, spot, :] = base_a[x, spot, :] + factor * (sum_a[x, spot, :] + term_a)


def first_kernel(halves, anchors, source, begin, wave, *rest):
    next_f, next_a, courant, one, slab, level, scale = rest[-7:]
    terms, halo, pieces = rest[:4], rest[4], rest[5:-7]
    row_count = terms[0].shape[0]
    square_speed(pieces, halves, slab)
    load_scales(halo, scale)
    odd = odd_place()
    shift = (1 - odd) * HALO
    step_rows(halo, scale, odd, anchors, slab, terms, (next_f, next_a), courant, shift)
    add_source(source, begin, wave, next_f, 0, lax.axis_index("dom") * row_count + shift)
    code_layers([(ref, n) for ref in (next_f, next_a) for n in range(HALO)], one, level)


def other_kernel(halves, side, anchors, source, begin, wave, *rest):
    (sum_f, sum_a, base_f, base_a, two, wide, now_f, now_a, edge_f, edge_a, edge_c, hit), rest = rest[:12], rest[12:]
    pieces, extra, rest = rest[:side], rest[side : 2 * side], rest[2 * side :]
    next_f, next_a, courant, send, beyond, slab, extra_slab, pad, out_f, out_a, codes, scale, far_scale, level = rest
    row_count, count_y, count_z = sum_f.shape
    odd = odd_place()
    me = lax.axis_index("dom")
    square_speed(pieces, halves, slab)
    load_second(two, wide, codes, scale)
    step_rows(codes, scale, 1 - odd, anchors, slab, (sum_f, sum_a, base_f, base_a), (next_f, next_a), courant, 0)
    add_source(source, begin, wave, next_f, 0, me * row_count)
    for n in range(HALO):
        x = (1 - odd) * HALO + n
        next_f[x] = edge_f[n]
        next_a[x] = edge_a[n]
        courant[x] = edge_c[n]
    near = [(ref, odd * HALO + n) for ref in (next_f, next_a) for n in range(HALO)]

    @pl.when(jnp.logical_not(at_border()))
    def _():
        code_layers(near, send, level)

    @pl.when(at_border())
    def _():
        square_speed(extra, halves, extra_slab)
        load_scales(wide, far_scale)
        masks = lane_masks(TILE, count_z)
        per = count_y // GROUP
        ends = jnp.zeros((pad.shape[0], PAD, count_z), F32)
        pad[:, 0:PAD, :] = ends
        pad[:, PAD + count_y :, :] = ends
        first = me * row_count + odd * (row_count + HALO) - HALO

        def decoded(n, y):
            spot = n * per + y // GROUP
            code = wide[pl.ds(spot * GROUP, GROUP), :].astype(I32).astype(F32)
            return code * far_scale[pl.ds(spot, 1), :]

        for f, (now, out) in enumerate(((now_f, out_f), (now_a, out_a))):
            for n in range(HALO):
                pad[(1 - odd) * 2 * HALO + n, PAD : PAD + count_y, :] = now[odd * HALO + n]
                for y in range(0, count_y, GROUP):
                    pad[HALO + n, pl.ds(PAD + y, GROUP), :] = decoded(f * HALO + n, y)
                    pad[odd * 2 * HALO + n, pl.ds(PAD + y, GROUP), :] = decoded((2 + f) * HALO + n, y)
            for n in range(HALO):
                for y in range(0, count_y, TILE):
                    spot = pl.ds(y, TILE)
                    middle, summed = laplace_tile(pad, HALO + n, y, TILE, masks)
                    value = 2.0 * middle - decoded((4 + f) * HALO + n, y)
                    value += extra_slab[n, pl.ds(anchors[0, 1] + y, TILE), :] * summed
                    out[n, spot, :] = value + hit[n, spot, :] if f else value
        add_source(source, begin, wave, out_f, 0, first)
        code_layers([(ref, n) for ref in (out_f, out_a) for n in range(HALO)], beyond, level)


def between_kernel(p1, q1, p0, q0, prev_f, courant, hit, part_f, part_a, bend, pad):
    row_count, count_y, count_z = p1.shape
    masks = lane_masks(TILE, count_z)
    clear_outer(pad)
    for f, (now, out) in enumerate(((p1, part_f), (q1, part_a))):
        fill(pad, now)

        @pl.loop(0, row_count)
        def _(x):
            for y in range(0, count_y, TILE):
                spot = pl.ds(y, TILE)
                middle, summed = laplace_tile(pad, HALO + x, y, TILE, masks)
                value = courant[x, spot, :] * summed
                if f == 0:
                    bend[x, spot, :] = middle - 2.0 * p0[x, spot, :] + prev_f[x, spot, :]
                else:
                    value += hit[x, spot, :] + (2.0 * middle - q0[x, spot, :])
                out[x, spot, :] = value


def second_kernel(groups, anchors, source, begin, wave, p1, q1, p0, courant, part_f, part_a, bend, one, two, beyond, *rest):
    next_f, next_a, own = rest[:3]
    sends = rest[3 : 2 + groups]
    frame, codes, scale_one, scale_two = rest[2 + groups :]
    row_count, count_y, count_z = p1.shape
    band = own.shape[0] // row_count
    edge = (frame.shape[1] - count_y) // 2
    frame[:, 0:edge, :] = jnp.zeros((row_count, edge, count_z), F32)
    frame[:, edge + count_y :, :] = jnp.zeros((row_count, edge, count_z), F32)
    odd = odd_place()
    load_scales(one, scale_one)
    load_second(two, beyond, codes, scale_two)
    for ref, scale, low in ((one, scale_one, odd), (codes, scale_two, 1 - odd)):
        for x, y, term_f, term_a in halo_tiles(ref, scale, low, row_count, count_y):
            spot = pl.ds(y, GROUP)
            factor = courant[x, spot, :]
            frame[x, pl.ds(edge + y, GROUP), :] = part_f[x, spot, :] + factor * term_f
            next_a[x, spot, :] = part_a[x, spot, :] + factor * term_a

    add_source(source, begin, wave, frame, 1, lax.axis_index("dom") * row_count, edge)

    @pl.loop(0, row_count)
    def _(x):
        for y in range(0, count_y, TILE):
            spot = pl.ds(y, TILE)
            change = frame[x, pl.ds(edge + y, TILE), :]
            next_f[x, spot, :] = 2.0 * p1[x, spot, :] - p0[x, spot, :] + change
            image = q1[x, spot, :] * change + next_a[x, spot, :] * bend[x, spot, :]
            frame[x, pl.ds(edge + y, TILE), :] = image

    me = lax.axis_index("dom")
    for k in range(groups):
        start = edge - anchors[0, 1] + (me ^ k) * band
        values = [frame[x, pl.ds(start, band), :] for x in range(row_count)]
        if k == 0:
            for x in range(row_count):
                own[pl.ds(x * band, band), :] = values[x]
        else:
            code_rows(values, sends[k - 1], 0)


def hit_kernel(begin, cells, traces, first, second, beyond):
    row_count, count_y, count_z = first.shape
    depth = lax.broadcasted_iota(I32, (count_z, cells.shape[1]), 0)
    at_depth = depth == cells[2:3, :]
    parts = []
    for k in range(STEPS):
        left = traces[pl.ds(begin[0] + (STEPS - 1 - k), 1), :]
        for _ in range(3):
            part = left.astype(BF16).astype(F32)
            parts.append(jnp.where(at_depth, part, 0.0).astype(BF16))
            left = left - part

    def add_up(start, outs):
        right = jnp.concatenate(parts[: 3 * len(outs)], axis=0)

        @pl.loop(0, outs[0].shape[0])
        def _(i):
            row = jnp.where(cells[0:1, :] == start + i, cells[1:2, :], -1)
            cell = lax.broadcasted_iota(I32, (count_y, cells.shape[1]), 0)
            left = jnp.where(cell == row, 1.0, 0.0).astype(BF16)
            got = lax.dot_general(left, right, (((1,), (1,)), ((), ())), preferred_element_type=F32)
            for k, out in enumerate(outs):
                base = 3 * k * count_z
                high = got[:, base : base + count_z]
                middle = got[:, base + count_z : base + 2 * count_z]
                low = got[:, base + 2 * count_z : base + 3 * count_z]
                out[i] = high + (middle + low)

    start = lax.axis_index("dom") * row_count
    add_up(start, (first, second))

    @pl.when(at_border())
    def _():
        add_up(start + odd_place() * (row_count + HALO) - HALO, (beyond,))


SIZE_X, SIZE_Z, SIZE_C = 4, 4, 2
HALVES = 2


def place_of(shot):
    return shot // (SIZE_Z * SIZE_C), lax.rem(shot // SIZE_C, SIZE_Z), lax.rem(shot, SIZE_C)


def swap(axis, k):
    bits = k * {"x": SIZE_Z * SIZE_C, "z": SIZE_C, "c": 1}[axis]
    return [(shot, shot ^ bits) for shot in range(SIZE_X * SIZE_Z * SIZE_C)]


def join_kernel(*refs):
    size = refs[0].shape[0]
    for n, ref in enumerate(refs[:-1]):
        refs[-1][pl.ds(n * size, size), :] = ref[...]


def pick_kernel(layout, row_count, halves, anchors, *refs):
    count = len(layout)
    ins, outs, extra, table = refs[:count], refs[count:-2], refs[-2], refs[-1]
    side = len(outs)
    piece = outs[0].shape[0] // halves
    per = piece // row_count
    block = ins[0].shape[0] // len(layout[0])
    own = block // per
    x, z, c = place_of(lax.axis_index("shot"))
    half, me = lax.axis_index("dom") // side, lax.rem(lax.axis_index("dom"), side)
    anchor = anchors[0, 0] + half * (side * row_count - HALO)
    first = anchor // own
    span = table.shape[1] // block
    for ref, owners in zip(ins, layout):
        for n, (dx, dz, dc, dh) in enumerate(owners):
            place = ((x ^ dx) * SIZE_Z + (z ^ dz)) * SIZE_C + (c ^ dc) - first

            @pl.when((place >= 0) & (place < span))
            def _():
                start = pl.multiple_of(place * block, 8)
                table[half ^ dh, pl.ds(start, block), :] = ref[pl.ds(n * block, block), :].astype(F32)

    offset = (anchor - first * own) * per
    starts = [offset + half * (HALO * per) + (me ^ k) * piece for k in range(side)]
    starts.append(offset + (1 - half) * (side * piece))
    for start, out in zip(starts, (*outs, extra)):
        size = out.shape[0] // halves
        for h in range(halves):
            out[pl.ds(h * size, size), :] = table[h, pl.ds(pl.multiple_of(start, 8), size), :].astype(BF16)


def band_kernel(groups, row_count, block, anchors, own, *refs):
    got, (keep, send, table) = refs[: groups - 1], refs[groups - 1 :]
    per = own.shape[0] // row_count
    c = lax.rem(lax.axis_index("shot"), SIZE_C)
    me = lax.axis_index("dom")
    anchor = anchors[0, 0]
    first = anchor // (block // per)
    table[...] = jnp.zeros(table.shape, F32)
    offset = (anchor - first * (block // per)) * per
    for k in range(groups):
        base = offset + (me ^ k) * (row_count * per)
        if k == 0:
            table[pl.ds(pl.multiple_of(base, 8), row_count * per), :] = own[...]
        else:
            for n, value in enumerate(decode_rows(got[-k], row_count, per)):
                table[pl.ds(pl.multiple_of(base + n * per, 8), per), :] = value
    mine = lax.rem(c + first, SIZE_C)
    for i in range(keep.shape[0] // block):
        for out, parity in ((keep, mine), (send, 1 - mine)):
            start = pl.multiple_of((SIZE_C * i + parity) * block, 8)
            out[pl.ds(i * block, block), :] = table[pl.ds(start, block), :]


def core_kernel(block, per, anchors, other, keep, got, own, *refs):
    sends, total = refs[:-1], refs[-1]
    x, _, c = place_of(lax.axis_index("shot"))
    total[...] = jnp.zeros(total.shape, F32)
    for ref, place in ((keep, anchors), (got, other)):
        first = place[0, 0] // (block // per)
        low = (first + lax.rem(c + first, SIZE_C)) // SIZE_C
        for i in range(ref.shape[0] // block):
            spot = pl.ds(pl.multiple_of((low + i) * block, 8), block)
            total[spot, :] += ref[pl.ds(i * block, block), :]
    size = own.shape[0]
    own[...] = total[pl.ds(pl.multiple_of(x * size, 8), size), :]
    for k, send in enumerate(sends, 1):
        start = (x ^ k) * size
        values = [total[pl.ds(pl.multiple_of(start + n * per, 8), per), :] for n in range(size // per)]
        code_rows(values, send, 0)


def along_x_kernel(per, mine, *refs):
    got, rest = refs[: SIZE_X - 1], refs[SIZE_X - 1 :]
    own, sends, total = rest[0], rest[1:-1], rest[-1]
    total[...] = mine[...]
    for ref in got:
        for n, value in enumerate(decode_rows(ref, total.shape[0] // per, per)):
            total[pl.ds(n * per, per), :] += value
    _, z, _ = place_of(lax.axis_index("shot"))
    size = own.shape[0]
    own[...] = total[pl.ds(pl.multiple_of(z * size, 8), size), :]
    for k, send in enumerate(sends, 1):
        start = (z ^ k) * size
        values = [total[pl.ds(pl.multiple_of(start + n * per, 8), per), :] for n in range(size // per)]
        code_rows(values, send, 0)


def along_z_kernel(per, mine, *refs):
    got, out = refs[:-1], refs[-1]
    for parts in zip(range(mine.shape[0] // per), *[decode_rows(r, mine.shape[0] // per, per) for r in got]):
        n, values = parts[0], parts[1:]
        total = mine[pl.ds(n * per, per), :]
        for value in values:
            total += value
        out[pl.ds(n * per, per), :] = total


def swap_z(groups, k):
    shots, doms = (k % SIZE_Z) * SIZE_C, (k // SIZE_Z) * (groups // HALVES)
    return [
        (shot * groups + dom, (shot ^ shots) * groups + (dom ^ doms))
        for shot in range(SIZE_X * SIZE_Z * SIZE_C)
        for dom in range(groups)
    ]


def across(groups, k):
    return [(i, i ^ k) for i in range(groups)]


def far_first(values):
    return sorted(values, reverse=True)


def exchange(parts, axis, pairs):
    got = {}
    for k in far_first(range(1, len(parts) + 1)):
        got[k] = lax.ppermute(parts[k - 1], axis, pairs(k))
    return [got[k] for k in sorted(got)]


def body(
    velocity,
    anchors,
    start_step,
    source,
    receivers,
    traces,
    wavelet,
    fwd_prev,
    fwd_now,
    adj_prev,
    adj_now,
):
    row_count, count_y, count_z = fwd_now.shape[1:]
    groups = lax.axis_size("dom")
    own_rows, band = velocity.shape[:2]
    block = own_rows * band
    piece = row_count * band
    p0, q0, p_prev, q_prev = fwd_now[0], adj_now[0], fwd_prev[0], adj_prev[0]
    scalars = (anchors, source, start_step, wavelet)
    one_pairs = [(i, i ^ 1) for i in range(groups)]
    two_pairs = [(i, i + 1) for i in range(1, groups - 1, 2)]
    side = groups // HALVES
    border = [(side - 1, side), (side, side - 1)]
    two_pairs = [(a, b) for a, b in two_pairs if a != side - 1]
    two_pairs += [(b, a) for a, b in two_pairs]

    along = {axis: functools.partial(swap, axis) for axis in "xzc"}
    between = functools.partial(across, groups)

    local = velocity.reshape(block, count_z)
    near = [local] + exchange([local] * (HALVES * SIZE_Z - 1), ("shot", "dom"), functools.partial(swap_z, groups))

    code = struct((halo_rows(2 * HALO, count_y), count_z), I16)
    wide = struct((halo_rows(6 * HALO, count_y), count_z), I16)
    groups_of = lambda layers: layers * count_y // GROUP
    levels = pltpu.VMEM((groups_of(2 * HALO), count_z), I32)
    scale = pltpu.VMEM((groups_of(2 * HALO), count_z), F32)
    wide_levels = pltpu.VMEM((groups_of(6 * HALO), count_z), I32)
    wide_scale = pltpu.VMEM((groups_of(6 * HALO), count_z), F32)
    codes = pltpu.VMEM((groups_of(2 * HALO) * GROUP, count_z), I16)
    fields = (p0, q0, p_prev, q_prev)
    strip = struct((HALO, count_y, count_z), F32)
    strips = pltpu.VMEM(strip.shape, F32)
    hold = pltpu.VMEM(p0.shape, F32)
    scratch = (hold, hold, strips, strips, wide_levels, pltpu.SemaphoreType.DMA((4,)))
    one, two, wide = call(encode_kernel, (code, code, wide), fields, "aaaa", scratch)
    from_wide = lax.ppermute(wide, "dom", border)
    from_one = lax.ppermute(one, "dom", one_pairs)
    from_two = lax.ppermute(two, "dom", two_pairs)

    (line,) = call(join_kernel, (struct((len(near) * block, count_z), BF16),), near, "v" * len(near))

    anchors, line = lax.optimization_barrier((anchors, line))
    other = lax.ppermute(anchors, "shot", swap("c", 1))
    field = struct((row_count, count_y, count_z), F32)
    hits = call(hit_kernel, (field, field, strip), (start_step, receivers[0], traces[0]), "svv")
    padded = pltpu.VMEM((row_count + 2 * HALO, count_y + 2 * PAD, count_z), F32)
    sums = call(before_kernel, (field,) * 4, (p0, q0, p_prev, q_prev, hits[0]), "v" * 5, (padded,))
    plane = [line] + exchange([line] * (SIZE_X - 1), "shot", along["x"])
    plane, other = lax.optimization_barrier((plane, sums[0], other))[::2]
    plane += [lax.ppermute(part, "shot", swap("c", 1)) for part in plane]
    layout = [
        [(dx, k % SIZE_Z, dc, k // SIZE_Z) for k in range(HALVES * SIZE_Z)]
        for dc in range(SIZE_C)
        for dx in range(SIZE_X)
    ]
    *pieces, extra = call(
        functools.partial(pick_kernel, layout, row_count, HALVES),
        (*[struct((HALVES * piece, count_z), BF16)] * side, struct((HALVES * HALO * band, count_z), BF16)),
        (anchors, *plane),
        "s" + "v" * len(plane),
        (pltpu.VMEM((HALVES, -(-(row_count * side + HALO + own_rows - 1) // own_rows) * block, count_z), F32),),
    )
    pieces = [pieces[0]] + exchange(pieces[1:], "dom", between)[::-1]
    *pieces, from_wide = lax.optimization_barrier((*pieces, from_wide))
    to_border = lambda k: [(a ^ k, a) for a, _ in border]
    extras = [extra] + exchange([extra] * (side - 1), "dom", to_border)[::-1]

    slab = pltpu.VMEM((row_count, groups * band, count_z), F32)
    edge_f, edge_a, edge_c, one = call(
        functools.partial(first_kernel, HALVES),
        (strip, strip, strip, code),
        (*scalars, *sums, from_one, *pieces),
        "ssss" + "v" * (5 + side),
        (slab, levels, scale),
    )
    from_one = lax.ppermute(one, "dom", one_pairs)
    extra_slab = pltpu.VMEM((HALO, groups * band, count_z), F32)
    p1, q1, courant, two, beyond = call(
        functools.partial(other_kernel, HALVES, side),
        (field, field, field, code, code),
        (*scalars, *sums, from_two, from_wide, p0, q0, edge_f, edge_a, edge_c, hits[2], *pieces, *extras),
        "ssss" + "v" * (12 + 2 * side),
        (
            slab,
            extra_slab,
            pltpu.VMEM((3 * HALO, count_y + 2 * PAD, count_z), F32),
            strips,
            strips,
            codes,
            scale,
            wide_scale,
            levels,
        ),
    )
    from_two = lax.ppermute(two, "dom", two_pairs)
    part_f, part_a, bend = call(
        between_kernel,
        (field,) * 3,
        (p1, q1, p0, q0, p_prev, courant, hits[1]),
        "v" * 7,
        (padded,),
    )

    span = -(-(row_count * groups + own_rows - 1) // own_rows)
    span += span % SIZE_C
    table = pltpu.VMEM((span * block, count_z), F32)
    edge = groups * band - count_y
    coded = struct((code_rows_of(row_count, band), count_z), I16)
    frame = pltpu.VMEM((row_count, count_y + 2 * edge, count_z), F32)
    p2, q2, own, *sends = call(
        functools.partial(second_kernel, groups),
        (field, field, struct((piece, count_z), F32), *[coded] * (groups - 1)),
        (*scalars, p1, q1, p0, courant, part_f, part_a, bend, from_one, from_two, beyond),
        "ssss" + "v" * 10,
        (frame, codes, scale, scale),
    )
    got = exchange(sends, "dom", between)[::-1]

    part = struct((span // SIZE_C * block, count_z), F32)
    keep, send = call(
        functools.partial(band_kernel, groups, row_count, block),
        (part, part),
        (anchors, own, *got),
        "s" + "v" * groups,
        (table,),
    )
    got = lax.ppermute(send, "shot", swap("c", 1))

    size = SIZE_Z * block
    coded = struct((code_rows_of(size // band, band), count_z), I16)
    total = pltpu.VMEM(((SIZE_X * SIZE_Z + 1) * block, count_z), F32)
    own, *sends = call(
        functools.partial(core_kernel, block, band),
        (struct((size, count_z), F32), *[coded] * (SIZE_X - 1)),
        (anchors, other, keep, got),
        "ssvv",
        (total,),
    )
    got = exchange(sends, "shot", along["x"])[::-1]

    coded = struct((code_rows_of(own_rows, band), count_z), I16)
    own, *sends = call(
        functools.partial(along_x_kernel, band),
        (struct((block, count_z), F32), *[coded] * (SIZE_Z - 1)),
        (own, *got),
        "v" * SIZE_X,
        (pltpu.VMEM((size, count_z), F32),),
    )
    got = exchange(sends, "shot", along["z"])[::-1]

    (gradient,) = call(
        functools.partial(along_z_kernel, band),
        (struct((block, count_z), F32),),
        (own, *got),
        "v" * SIZE_Z,
    )
    return (p2[None], q2[None], gradient.reshape(own_rows, band, count_z))


def solution(mesh):
    placed = (
        P("shot", "dom", None),
        P("shot", None),
        P("shot"),
        P("shot", None),
        P("shot", None, None),
        P("shot", None, None),
        P(),
        P("shot", "dom", None, None),
        P("shot", "dom", None, None),
        P("shot", "dom", None, None),
        P("shot", "dom", None, None),
    )
    return jax.shard_map(
        body,
        mesh=mesh,
        in_specs=placed,
        out_specs=(
            P("shot", "dom", None, None),
            P("shot", "dom", None, None),
            P("shot", "dom", None),
        ),
        check_vma=False,
    )
```

```python
import functools

import jax
import jax.numpy as jnp
from jax import lax
from jax.experimental import pallas as pl
from jax.experimental.pallas import tpu as pltpu
from jax.sharding import PartitionSpec as P

STEPS = 2
CENTER = -205.0 / 72.0
COEFFS = (8.0 / 5.0, -1.0 / 5.0, 8.0 / 315.0, -1.0 / 560.0)

F32 = jnp.float32
BF16 = jnp.bfloat16
I16 = jnp.int16
I32 = jnp.int32

VMEM_LIMIT = 32 * 1024 * 1024
FLOOR = 1e-33
TOP = 32700.0
HALO = 4
GROUP = 32


def vmem():
    return pl.BlockSpec(memory_space=pltpu.VMEM)


def smem():
    return pl.BlockSpec(memory_space=pltpu.SMEM)


def call(kernel, outs, args, spaces, scratch=()):
    return pl.pallas_call(
        kernel,
        out_shape=list(outs),
        in_specs=[smem() if s == "s" else vmem() for s in spaces],
        out_specs=[vmem()] * len(outs),
        scratch_shapes=list(scratch),
        compiler_params=pltpu.CompilerParams(vmem_limit_bytes=VMEM_LIMIT),
        cost_estimate=pl.CostEstimate(flops=0, bytes_accessed=0, transcendentals=0),
    )(*args)


def struct(shape, dtype):
    return jax.ShapeDtypeStruct(shape, dtype)


def code_group(values):
    top = jnp.max(jnp.abs(values), axis=0, keepdims=True)
    level = jnp.ceil(jnp.log2(jnp.maximum(top, FLOOR)) * 256.0) + 1.0
    scaled = values * (TOP * jnp.exp2(level * (-1.0 / 256.0)))
    return jnp.round(scaled).astype(I32), level.astype(I32)


def code_rows(values, out_ref, base):
    band = values[0].shape[0]
    levels = []
    for n in range(0, len(values), 2):
        codes = []
        for value in values[n : n + 2]:
            code, level = code_group(value)
            codes.append(code)
            levels.append(level)
        out_ref[pl.ds(base + n * band, 2 * band), :] = jnp.concatenate(codes, axis=0).astype(I16)
    levels += [jnp.zeros((-len(levels) % 16, values[0].shape[1]), I32)]
    spot = pl.ds(base + len(values) * band, code_rows_of(len(values), band) - len(values) * band)
    out_ref[spot, :] = jnp.concatenate(levels, axis=0).astype(I16)


def code_rows_of(groups, band):
    return groups * band + groups + -groups % 16


def decode_rows(in_ref, groups, band):
    scales = decode_scale(in_ref[pl.ds(groups * band, groups + -groups % 16), :])
    for n in range(0, groups, 2):
        pair = in_ref[pl.ds(n * band, 2 * band), :].astype(I32).astype(F32)
        yield pair[:band] * scales[n : n + 1]
        yield pair[band:] * scales[n + 1 : n + 2]


def decode_scale(levels):
    return jnp.exp2(levels.astype(I32).astype(F32) * (1.0 / 256.0)) * (1.0 / TOP)


def code_halos(field, rows, out_ref, level_ref, base):
    for n, layer in enumerate(rows):
        value = field(layer)
        count = value.shape[0] // GROUP
        for g in range(count):
            code, level = code_group(value[g * GROUP : (g + 1) * GROUP])
            spot = base + n * count + g
            out_ref[pl.ds(spot * GROUP, GROUP), :] = code.astype(I16)
            level_ref[pl.ds(spot, 1), :] = level


def halo_rows(layers, count_y):
    groups = layers * count_y // GROUP
    return groups * GROUP + groups


def odd_place():
    return lax.rem(lax.axis_index("dom"), 2)


def code_edges(fields, out_refs, level_ref):
    row_count, count_y, _ = fields[0].shape
    per = HALO * count_y // GROUP
    odd = odd_place()
    for out_ref, high in zip(out_refs, (1 - odd, odd)):
        first = high * (row_count - HALO)
        for f, ref in enumerate(fields):
            code_halos(lambda x: ref[x], [first + n for n in range(HALO)], out_ref, level_ref, f * per)
        out_ref[2 * per * GROUP :, :] = level_ref[...].astype(I16)


def encode_kernel(now_f, now_a, one, two, level_ref):
    code_edges((now_f, now_a), (one, two), level_ref)


PAD = 8


def laplace_tile(pad_ref, layer, y, rows, masks):
    middle = pad_ref[layer, pl.ds(PAD + y, rows), :]
    summed = (3.0 * CENTER) * middle
    for k in range(1, HALO + 1):
        up, down = masks[k - 1]
        count = middle.shape[1]
        part = pad_ref[layer + k, pl.ds(PAD + y, rows), :] + pad_ref[layer - k, pl.ds(PAD + y, rows), :]
        part += pad_ref[layer, pl.ds(PAD + y + k, rows), :] + pad_ref[layer, pl.ds(PAD + y - k, rows), :]
        part += jnp.where(up, pltpu.roll(middle, k, 1), 0.0)
        part += jnp.where(down, pltpu.roll(middle, count - k, 1), 0.0)
        summed += COEFFS[k - 1] * part
    return middle, summed


TILE = 32


def lane_masks(rows, count):
    lane = lax.broadcasted_iota(I32, (rows, count), 1)
    return [(lane >= k, lane < count - k) for k in range(1, HALO + 1)]


def fill(pad_ref, field_ref):
    row_count, count_y, count_z = field_ref.shape
    edge = jnp.zeros((pad_ref.shape[0], PAD, count_z), F32)
    pad_ref[:, 0:PAD, :] = edge
    pad_ref[:, PAD + count_y :, :] = edge
    for x in range(row_count):
        pad_ref[HALO + x, PAD : PAD + count_y, :] = field_ref[x]


def clear_outer(pad_ref):
    outer = jnp.zeros((HALO, *pad_ref.shape[1:]), F32)
    pad_ref[0:HALO] = outer
    pad_ref[pad_ref.shape[0] - HALO :] = outer


def load_scales(in_ref, scale_ref):
    groups = scale_ref.shape[0]
    scale_ref[...] = decode_scale(in_ref[groups * GROUP :, :])


def add_source(source, start, wave, ref, k, edge=0):
    x = source[0, 0] - lax.axis_index("dom") * ref.shape[0]
    lane = lax.broadcasted_iota(I32, (1, ref.shape[2]), 1)

    @pl.when((x >= 0) & (x < ref.shape[0]))
    def _():
        y = source[0, 1] + edge
        row = ref[x, pl.ds(y, 1), :]
        ref[x, pl.ds(y, 1), :] = row + jnp.where(lane == source[0, 2], wave[start[0] + k], 0.0)


def before_kernel(now_f, now_a, prev_f, prev_a, hit, sum_f, sum_a, base_f, base_a, pad):
    row_count, count_y, count_z = now_f.shape
    masks = lane_masks(TILE, count_z)
    clear_outer(pad)
    fields = ((now_f, prev_f, sum_f, base_f), (now_a, prev_a, sum_a, base_a))
    for f, (now, prev, total, base) in enumerate(fields):
        fill(pad, now)

        @pl.loop(0, row_count)
        def _(x):
            for y in range(0, count_y, TILE):
                spot = pl.ds(y, TILE)
                middle, summed = laplace_tile(pad, HALO + x, y, TILE, masks)
                total[x, spot, :] = summed
                value = 2.0 * middle - prev[x, spot, :]
                base[x, spot, :] = value + hit[x, spot, :] if f else value


def halo_terms(in_ref, scale_ref, f, spot_y, count_y, low):
    per = count_y // GROUP
    rows = []
    for j in range(HALO):
        layer = j + low * (HALO - 1 - 2 * j)
        spot = (f * HALO + layer) * per + spot_y // GROUP
        code = in_ref[pl.ds(pl.multiple_of(spot * GROUP, GROUP), GROUP), :].astype(I32).astype(F32)
        rows.append(code * scale_ref[pl.ds(spot, 1), :])
    return [sum(COEFFS[r + j] * rows[j] for j in range(HALO - r)) for r in range(HALO)]


def halo_tiles(refs, scales, row_count, count_y):
    for ref, scale in zip(refs, scales):
        load_scales(ref, scale)
    odd = odd_place()
    for y in range(0, count_y, GROUP):
        for ref, scale, low in zip(refs, scales, (odd, 1 - odd)):
            terms = [halo_terms(ref, scale, f, y, count_y, low) for f in range(2)]
            for r in range(HALO):
                yield row_count - 1 - r + low * (2 * r + 1 - row_count), y, terms[0][r], terms[1][r]


def first_kernel(halves, anchors, source, begin, wave, sum_f, sum_a, base_f, base_a, *rest):
    next_f, next_a, courant, one, two, slab, level, scale_one, scale_two = rest[-9:]
    halos, pieces = rest[1::-1], rest[2:-9]
    row_count, count_y, _ = sum_f.shape
    band = pieces[0].shape[0] // (row_count * halves)
    side = len(pieces)
    me = lax.rem(lax.axis_index("dom"), side)
    for k in range(side):
        for half in range(halves):
            start = pl.multiple_of((half * side + (me ^ k)) * band, 8)
            for x in range(0, row_count, 2):
                speed = pieces[-k][pl.ds((half * row_count + x) * band, 2 * band), :].astype(F32)
                slab[x, pl.ds(start, band), :] = jnp.square(speed[:band])
                slab[x + 1, pl.ds(start, band), :] = jnp.square(speed[band:])

    for x, y, term_f, term_a in halo_tiles(halos, (scale_one, scale_two), row_count, count_y):
        spot = pl.ds(y, GROUP)
        factor = slab[x, pl.ds(anchors[0, 1] + y, GROUP), :]
        courant[x, spot, :] = factor
        next_f[x, spot, :] = base_f[x, spot, :] + factor * (sum_f[x, spot, :] + term_f)
        next_a[x, spot, :] = base_a[x, spot, :] + factor * (sum_a[x, spot, :] + term_a)

    add_source(source, begin, wave, next_f, 0)
    code_edges((next_f, next_a), (one, two), level)


def between_kernel(p1, q1, p0, q0, prev_f, courant, hit, part_f, part_a, bend, pad):
    row_count, count_y, count_z = p1.shape
    masks = lane_masks(TILE, count_z)
    clear_outer(pad)
    for f, (now, out) in enumerate(((p1, part_f), (q1, part_a))):
        fill(pad, now)

        @pl.loop(0, row_count)
        def _(x):
            for y in range(0, count_y, TILE):
                spot = pl.ds(y, TILE)
                middle, summed = laplace_tile(pad, HALO + x, y, TILE, masks)
                value = courant[x, spot, :] * summed
                if f == 0:
                    bend[x, spot, :] = middle - 2.0 * p0[x, spot, :] + prev_f[x, spot, :]
                else:
                    value += hit[x, spot, :] + (2.0 * middle - q0[x, spot, :])
                out[x, spot, :] = value


def second_kernel(groups, anchors, source, begin, wave, p1, q1, p0, courant, part_f, part_a, bend, two, one, *rest):
    next_f, next_a, own = rest[:3]
    sends = rest[3 : 2 + groups]
    frame, scale_one, scale_two = rest[2 + groups :]
    row_count, count_y, count_z = p1.shape
    band = own.shape[0] // row_count
    edge = (frame.shape[1] - count_y) // 2
    frame[:, 0:edge, :] = jnp.zeros((row_count, edge, count_z), F32)
    frame[:, edge + count_y :, :] = jnp.zeros((row_count, edge, count_z), F32)
    for x, y, term_f, term_a in halo_tiles((one, two), (scale_one, scale_two), row_count, count_y):
        spot = pl.ds(y, GROUP)
        factor = courant[x, spot, :]
        frame[x, pl.ds(edge + y, GROUP), :] = part_f[x, spot, :] + factor * term_f
        next_a[x, spot, :] = part_a[x, spot, :] + factor * term_a

    add_source(source, begin, wave, frame, 1, edge)

    @pl.loop(0, row_count)
    def _(x):
        for y in range(0, count_y, TILE):
            spot = pl.ds(y, TILE)
            change = frame[x, pl.ds(edge + y, TILE), :]
            next_f[x, spot, :] = 2.0 * p1[x, spot, :] - p0[x, spot, :] + change
            image = q1[x, spot, :] * change + next_a[x, spot, :] * bend[x, spot, :]
            frame[x, pl.ds(edge + y, TILE), :] = image

    me = lax.axis_index("dom")
    for k in range(groups):
        start = edge - anchors[0, 1] + (me ^ k) * band
        values = [frame[x, pl.ds(start, band), :] for x in range(row_count)]
        if k == 0:
            for x in range(row_count):
                own[pl.ds(x * band, band), :] = values[x]
        else:
            code_rows(values, sends[k - 1], 0)


def hit_kernel(begin, cells, traces, first, second):
    row_count, count_y, count_z = first.shape
    x = cells[0:1, :] - lax.axis_index("dom") * row_count
    inside = (x >= 0) & (x < row_count)
    row = jnp.where(inside, x * count_y + cells[1:2, :], -1)
    depth = lax.broadcasted_iota(I32, (count_z, row.shape[1]), 0)
    at_depth = depth == cells[2:3, :]
    parts = []
    for k in range(STEPS):
        left = traces[pl.ds(begin[0] + (STEPS - 1 - k), 1), :]
        for _ in range(3):
            part = left.astype(BF16).astype(F32)
            parts.append(jnp.where(at_depth, part, 0.0).astype(BF16))
            left = left - part
    right = jnp.concatenate(parts, axis=0)

    @pl.loop(0, row_count)
    def _(i):
        cell = i * count_y + lax.broadcasted_iota(I32, (count_y, row.shape[1]), 0)
        left = jnp.where(cell == row, 1.0, 0.0).astype(BF16)
        got = lax.dot_general(left, right, (((1,), (1,)), ((), ())), preferred_element_type=F32)
        for k, out in enumerate((first, second)):
            base = 3 * k * count_z
            high = got[:, base : base + count_z]
            middle = got[:, base + count_z : base + 2 * count_z]
            low = got[:, base + 2 * count_z : base + 3 * count_z]
            out[i] = high + (middle + low)


SIZE_X, SIZE_Z, SIZE_C = 4, 4, 2
HALVES = 2


def place_of(shot):
    return shot // (SIZE_Z * SIZE_C), lax.rem(shot // SIZE_C, SIZE_Z), lax.rem(shot, SIZE_C)


def swap(axis, k):
    bits = k * {"x": SIZE_Z * SIZE_C, "z": SIZE_C, "c": 1}[axis]
    return [(shot, shot ^ bits) for shot in range(SIZE_X * SIZE_Z * SIZE_C)]


def nearest_x(anchor, z, c, own):
    reach = SIZE_Z * SIZE_C * own
    least = anchor - (own - 1) - (z * SIZE_C + c) * own
    return jnp.clip((least + reach - 1 + reach) // reach - 1, 0, SIZE_X - 1)


def select_kernel(own, window, places, *refs):
    count = SIZE_X
    ins, outs = refs[:count], refs[count:]
    block = ins[0].shape[0]
    x, z, c = place_of(lax.axis_index("shot"))
    half = lax.axis_index("dom") // (lax.axis_size("dom") // HALVES)
    for k, out in enumerate(outs):
        for n in range(SIZE_C):
            anchor = places[k % SIZE_Z, n] + (half ^ (k // SIZE_Z)) * window
            apart = nearest_x(anchor, z, c, own) ^ x
            for dx in range(SIZE_X):

                @pl.when(apart == dx)
                def _():
                    out[pl.ds(n * block, block), :] = ins[dx][...]


def share_kernel(*refs):
    ins, (mine, theirs) = refs[:-2], refs[-2:]
    block = ins[0].shape[0] // SIZE_C
    for k in range(len(ins)):
        n, ref = k, ins[-k]
        mine[pl.ds(n * block, block), :] = ref[0:block, :]
        theirs[pl.ds(n * block, block), :] = ref[block : 2 * block, :]


def pick_kernel(row_count, anchors, mine, theirs, *refs):
    outs, table = refs[:-1], refs[-1]
    side = len(outs)
    piece = outs[0].shape[0] // HALVES
    per = piece // row_count
    block = mine.shape[0] // (HALVES * SIZE_Z)
    own = block // per
    x, z, c = place_of(lax.axis_index("shot"))
    half, me = lax.axis_index("dom") // side, lax.rem(lax.axis_index("dom"), side)
    anchor = anchors[0, 0] + half * (side * row_count)
    first = anchor // own
    span = table.shape[1] // block
    for dc, ref in enumerate((mine, theirs)):
        for k in range(HALVES * SIZE_Z):
            from_z, from_c = z ^ (k % SIZE_Z), c ^ dc
            place = (nearest_x(anchor, from_z, from_c, own) * SIZE_Z + from_z) * SIZE_C + from_c - first

            @pl.when((place >= 0) & (place < span))
            def _():
                start = pl.multiple_of(place * block, 8)
                table[half ^ (k // SIZE_Z), pl.ds(start, block), :] = ref[pl.ds(k * block, block), :].astype(F32)

    offset = (anchor - first * own) * per
    for k in range(side):
        start = pl.multiple_of(offset + (me ^ k) * piece, 8)
        for h in range(HALVES):
            outs[k][pl.ds(h * piece, piece), :] = table[h, pl.ds(start, piece), :].astype(BF16)


def band_kernel(groups, row_count, block, anchors, own, *refs):
    got, (keep, send, table) = refs[: groups - 1], refs[groups - 1 :]
    per = own.shape[0] // row_count
    c = lax.rem(lax.axis_index("shot"), SIZE_C)
    me = lax.axis_index("dom")
    anchor = anchors[0, 0]
    first = anchor // (block // per)
    table[...] = jnp.zeros(table.shape, F32)
    offset = (anchor - first * (block // per)) * per
    for k in range(groups):
        base = offset + (me ^ k) * (row_count * per)
        if k == 0:
            table[pl.ds(pl.multiple_of(base, 8), row_count * per), :] = own[...]
        else:
            for n, value in enumerate(decode_rows(got[-k], row_count, per)):
                table[pl.ds(pl.multiple_of(base + n * per, 8), per), :] = value
    mine = lax.rem(c + first, SIZE_C)
    for i in range(keep.shape[0] // block):
        for out, parity in ((keep, mine), (send, 1 - mine)):
            start = pl.multiple_of((SIZE_C * i + parity) * block, 8)
            out[pl.ds(i * block, block), :] = table[pl.ds(start, block), :]


def core_kernel(block, per, anchors, other, keep, got, own, *refs):
    sends, total = refs[:-1], refs[-1]
    x, _, c = place_of(lax.axis_index("shot"))
    total[...] = jnp.zeros(total.shape, F32)
    for ref, place in ((keep, anchors), (got, other)):
        first = place[0, 0] // (block // per)
        low = (first + lax.rem(c + first, SIZE_C)) // SIZE_C
        for i in range(ref.shape[0] // block):
            spot = pl.ds(pl.multiple_of((low + i) * block, 8), block)
            total[spot, :] += ref[pl.ds(i * block, block), :]
    size = own.shape[0]
    own[...] = total[pl.ds(pl.multiple_of(x * size, 8), size), :]
    for k, send in enumerate(sends, 1):
        start = (x ^ k) * size
        values = [total[pl.ds(pl.multiple_of(start + n * per, 8), per), :] for n in range(size // per)]
        code_rows(values, send, 0)


def along_x_kernel(per, mine, *refs):
    got, rest = refs[: SIZE_X - 1], refs[SIZE_X - 1 :]
    own, sends, total = rest[0], rest[1:-1], rest[-1]
    total[...] = mine[...]
    for ref in got:
        for n, value in enumerate(decode_rows(ref, total.shape[0] // per, per)):
            total[pl.ds(n * per, per), :] += value
    _, z, _ = place_of(lax.axis_index("shot"))
    size = own.shape[0]
    own[...] = total[pl.ds(pl.multiple_of(z * size, 8), size), :]
    for k, send in enumerate(sends, 1):
        start = (z ^ k) * size
        values = [total[pl.ds(pl.multiple_of(start + n * per, 8), per), :] for n in range(size // per)]
        code_rows(values, send, 0)


def along_z_kernel(per, mine, *refs):
    got, out = refs[:-1], refs[-1]
    for parts in zip(range(mine.shape[0] // per), *[decode_rows(r, mine.shape[0] // per, per) for r in got]):
        n, values = parts[0], parts[1:]
        total = mine[pl.ds(n * per, per), :]
        for value in values:
            total += value
        out[pl.ds(n * per, per), :] = total


def swap_z(groups, k):
    shots, doms = (k % SIZE_Z) * SIZE_C, (k // SIZE_Z) * (groups // HALVES)
    return [
        (shot * groups + dom, (shot ^ shots) * groups + (dom ^ doms))
        for shot in range(SIZE_X * SIZE_Z * SIZE_C)
        for dom in range(groups)
    ]


def across(groups, k):
    return [(i, i ^ k) for i in range(groups)]


def far_first(values):
    return sorted(values, reverse=True)


def exchange(parts, axis, pairs):
    got = {}
    for k in far_first(range(1, len(parts) + 1)):
        got[k] = lax.ppermute(parts[k - 1], axis, pairs(k))
    return [got[k] for k in sorted(got)]


def body(
    velocity,
    anchors,
    start_step,
    source,
    receivers,
    traces,
    wavelet,
    fwd_prev,
    fwd_now,
    adj_prev,
    adj_now,
):
    row_count, count_y, count_z = fwd_now.shape[1:]
    groups = lax.axis_size("dom")
    own_rows, band = velocity.shape[:2]
    block = own_rows * band
    piece = row_count * band
    p0, q0, p_prev, q_prev = fwd_now[0], adj_now[0], fwd_prev[0], adj_prev[0]
    scalars = (anchors, source, start_step, wavelet)
    one_pairs = [(i, i ^ 1) for i in range(groups)]
    two_pairs = [(i, i + 1) for i in range(1, groups - 1, 2)]
    two_pairs += [(b, a) for a, b in two_pairs]

    along = {axis: functools.partial(swap, axis) for axis in "xzc"}
    between = functools.partial(across, groups)

    local = velocity.reshape(block, count_z)
    other = lax.ppermute(anchors, "shot", swap("c", 1))
    row = [local] + exchange([local] * (SIZE_X - 1), "shot", along["x"])
    pair = jnp.concatenate([anchors[:, 0], other[:, 0]])
    places = jnp.stack([pair] + exchange([pair] * (SIZE_Z - 1), "shot", along["z"]))
    side = groups // HALVES
    window = side * row_count
    needed = call(
        functools.partial(select_kernel, own_rows, window),
        [struct((SIZE_C * block, count_z), BF16)] * (HALVES * SIZE_Z),
        (places, *row),
        "s" + "v" * SIZE_X,
    )
    along_z = functools.partial(swap_z, groups)
    column = [needed[0]] + exchange(needed[1:], ("shot", "dom"), along_z)[::-1]

    field = struct((row_count, count_y, count_z), F32)
    hits = call(hit_kernel, (field, field), (start_step, receivers[0], traces[0]), "svv")
    padded = pltpu.VMEM((row_count + 2 * HALO, count_y + 2 * PAD, count_z), F32)
    sums = call(before_kernel, (field,) * 4, (p0, q0, p_prev, q_prev, hits[0]), "v" * 5, (padded,))
    column, _ = lax.optimization_barrier((column, sums[0]))
    shared = struct((HALVES * SIZE_Z * block, count_z), BF16)
    mine, theirs = call(share_kernel, (shared, shared), column, "v" * len(column))

    half = halo_rows(2 * HALO, count_y)
    code = struct((half, count_z), I16)
    levels = pltpu.VMEM((2 * HALO * count_y // GROUP, count_z), I32)
    one, two = call(encode_kernel, (code, code), (p0, q0), "vv", (levels,))
    from_one = lax.ppermute(one, "dom", one_pairs)
    from_two = lax.ppermute(two, "dom", two_pairs)
    theirs = lax.ppermute(theirs, "shot", swap("c", 1))
    reach = -(-(window + own_rows - 1) // own_rows) * block
    pieces = call(
        functools.partial(pick_kernel, row_count),
        [struct((HALVES * piece, count_z), BF16)] * side,
        (anchors, mine, theirs),
        "svv",
        (pltpu.VMEM((HALVES, reach, count_z), F32),),
    )
    pieces = [pieces[0]] + exchange(pieces[1:], "dom", between)[::-1]

    scale = pltpu.VMEM((2 * HALO * count_y // GROUP, count_z), F32)
    slab = pltpu.VMEM((row_count, groups * band, count_z), F32)
    p1, q1, courant, one, two = call(
        functools.partial(first_kernel, HALVES),
        (field, field, field, code, code),
        (*scalars, *sums, from_two, from_one, *pieces),
        "ssss" + "v" * (6 + side),
        (slab, levels, scale, scale),
    )
    from_one = lax.ppermute(one, "dom", one_pairs)
    from_two = lax.ppermute(two, "dom", two_pairs)
    part_f, part_a, bend = call(
        between_kernel,
        (field,) * 3,
        (p1, q1, p0, q0, p_prev, courant, hits[1]),
        "v" * 7,
        (padded,),
    )

    span = -(-(row_count * groups + own_rows - 1) // own_rows)
    span += span % SIZE_C
    table = pltpu.VMEM((span * block, count_z), F32)
    edge = groups * band - count_y
    coded = struct((code_rows_of(row_count, band), count_z), I16)
    frame = pltpu.VMEM((row_count, count_y + 2 * edge, count_z), F32)
    p2, q2, own, *sends = call(
        functools.partial(second_kernel, groups),
        (field, field, struct((piece, count_z), F32), *[coded] * (groups - 1)),
        (*scalars, p1, q1, p0, courant, part_f, part_a, bend, from_two, from_one),
        "ssss" + "v" * 9,
        (frame, scale, scale),
    )
    got = exchange(sends, "dom", between)[::-1]

    part = struct((span // SIZE_C * block, count_z), F32)
    keep, send = call(
        functools.partial(band_kernel, groups, row_count, block),
        (part, part),
        (anchors, own, *got),
        "s" + "v" * groups,
        (table,),
    )
    got = lax.ppermute(send, "shot", swap("c", 1))

    size = SIZE_Z * block
    coded = struct((code_rows_of(size // band, band), count_z), I16)
    total = pltpu.VMEM(((SIZE_X * SIZE_Z + 1) * block, count_z), F32)
    own, *sends = call(
        functools.partial(core_kernel, block, band),
        (struct((size, count_z), F32), *[coded] * (SIZE_X - 1)),
        (anchors, other, keep, got),
        "ssvv",
        (total,),
    )
    got = exchange(sends, "shot", along["x"])[::-1]

    coded = struct((code_rows_of(own_rows, band), count_z), I16)
    own, *sends = call(
        functools.partial(along_x_kernel, band),
        (struct((block, count_z), F32), *[coded] * (SIZE_Z - 1)),
        (own, *got),
        "v" * SIZE_X,
        (pltpu.VMEM((size, count_z), F32),),
    )
    got = exchange(sends, "shot", along["z"])[::-1]

    (gradient,) = call(
        functools.partial(along_z_kernel, band),
        (struct((block, count_z), F32),),
        (own, *got),
        "v" * SIZE_Z,
    )
    return (p2[None], q2[None], gradient.reshape(own_rows, band, count_z))


def solution(mesh):
    placed = (
        P("shot", "dom", None),
        P("shot", None),
        P("shot"),
        P("shot", None),
        P("shot", None, None),
        P("shot", None, None),
        P(),
        P("shot", "dom", None, None),
        P("shot", "dom", None, None),
        P("shot", "dom", None, None),
        P("shot", "dom", None, None),
    )
    return jax.shard_map(
        body,
        mesh=mesh,
        in_specs=placed,
        out_specs=(
            P("shot", "dom", None, None),
            P("shot", "dom", None, None),
            P("shot", "dom", None),
        ),
        check_vma=False,
    )
```

```python
import functools

import jax
import jax.numpy as jnp
from jax import lax
from jax.experimental import pallas as pl
from jax.experimental.pallas import tpu as pltpu
from jax.sharding import PartitionSpec as P

STEPS = 2
CENTER = -205.0 / 72.0
COEFFS = (8.0 / 5.0, -1.0 / 5.0, 8.0 / 315.0, -1.0 / 560.0)

F32 = jnp.float32
BF16 = jnp.bfloat16
I16 = jnp.int16
I32 = jnp.int32

VMEM_LIMIT = 32 * 1024 * 1024
FLOOR = 1e-33
TOP = 32700.0
HALO = 4
GROUP = 32


def vmem():
    return pl.BlockSpec(memory_space=pltpu.VMEM)


def smem():
    return pl.BlockSpec(memory_space=pltpu.SMEM)


def call(kernel, outs, args, spaces, scratch=(), cost=1_000_000):
    moved = sum(a.size * a.dtype.itemsize for a in (*outs, *args))
    return pl.pallas_call(
        kernel,
        out_shape=list(outs),
        in_specs=[smem() if s == "s" else vmem() for s in spaces],
        out_specs=[vmem()] * len(outs),
        scratch_shapes=list(scratch),
        compiler_params=pltpu.CompilerParams(vmem_limit_bytes=VMEM_LIMIT),
        cost_estimate=pl.CostEstimate(flops=0, bytes_accessed=0, transcendentals=0),
    )(*args)


def struct(shape, dtype):
    return jax.ShapeDtypeStruct(shape, dtype)


def code_group(values):
    top = jnp.max(jnp.abs(values), axis=0, keepdims=True)
    level = jnp.ceil(jnp.log2(jnp.maximum(top, FLOOR)) * 256.0) + 1.0
    scaled = values * (TOP * jnp.exp2(level * (-1.0 / 256.0)))
    return jnp.round(scaled).astype(I32), level.astype(I32)


def code_rows(values, out_ref, base):
    band = values[0].shape[0]
    levels = []
    for n in range(0, len(values), 2):
        codes = []
        for value in values[n : n + 2]:
            code, level = code_group(value)
            codes.append(code)
            levels.append(level)
        out_ref[pl.ds(base + n * band, 2 * band), :] = jnp.concatenate(codes, axis=0).astype(I16)
    levels += [jnp.zeros((-len(levels) % 16, values[0].shape[1]), I32)]
    spot = pl.ds(base + len(values) * band, code_rows_of(len(values), band) - len(values) * band)
    out_ref[spot, :] = jnp.concatenate(levels, axis=0).astype(I16)


def code_rows_of(groups, band):
    return groups * band + groups + -groups % 16


def decode_rows(in_ref, groups, band):
    scales = decode_scale(in_ref[pl.ds(groups * band, groups + -groups % 16), :])
    for n in range(0, groups, 2):
        pair = in_ref[pl.ds(n * band, 2 * band), :].astype(I32).astype(F32)
        yield pair[:band] * scales[n : n + 1]
        yield pair[band:] * scales[n + 1 : n + 2]


def decode_scale(levels):
    return jnp.exp2(levels.astype(I32).astype(F32) * (1.0 / 256.0)) * (1.0 / TOP)


def code_halos(field, rows, out_ref, level_ref, base):
    for n, layer in enumerate(rows):
        value = field(layer)
        count = value.shape[0] // GROUP
        for g in range(count):
            code, level = code_group(value[g * GROUP : (g + 1) * GROUP])
            spot = base + n * count + g
            out_ref[pl.ds(spot * GROUP, GROUP), :] = code.astype(I16)
            level_ref[pl.ds(spot, 1), :] = level


def halo_rows(layers, count_y):
    groups = layers * count_y // GROUP
    return groups * GROUP + groups


def odd_place():
    return lax.rem(lax.axis_index("dom"), 2)


def at_border():
    me, middle = lax.axis_index("dom"), lax.axis_size("dom") // HALVES
    return (me == middle) | (me == middle - 1)


def code_edges(fields, out_refs, level_ref):
    row_count, count_y, _ = fields[0].shape
    per = HALO * count_y // GROUP
    odd = odd_place()
    for out_ref, high in zip(out_refs, (1 - odd, odd)):
        first = high * (row_count - HALO)
        for f, ref in enumerate(fields):
            code_halos(lambda x: ref[x], [first + n for n in range(HALO)], out_ref, level_ref, f * per)
        out_ref[2 * per * GROUP :, :] = level_ref[...].astype(I16)


def encode_kernel(now_f, now_a, one, two, level_ref):
    code_edges((now_f, now_a), (one, two), level_ref)


def decode_halo(in_ref, scale_ref, pad_ref, f, first, count_y):
    per = count_y // GROUP
    for layer in range(HALO):
        for g in range(per):
            spot = (f * HALO + layer) * per + g
            code = in_ref[pl.ds(spot * GROUP, GROUP), :].astype(I32).astype(F32)
            pad_ref[first + layer, pl.ds(PAD + g * GROUP, GROUP), :] = code * scale_ref[pl.ds(spot, 1), :]


PAD = 8


def laplace_tile(pad_ref, layer, y, rows, masks):
    middle = pad_ref[layer, pl.ds(PAD + y, rows), :]
    summed = (3.0 * CENTER) * middle
    for k in range(1, HALO + 1):
        up, down = masks[k - 1]
        count = middle.shape[1]
        part = pad_ref[layer + k, pl.ds(PAD + y, rows), :] + pad_ref[layer - k, pl.ds(PAD + y, rows), :]
        part += pad_ref[layer, pl.ds(PAD + y + k, rows), :] + pad_ref[layer, pl.ds(PAD + y - k, rows), :]
        part += jnp.where(up, pltpu.roll(middle, k, 1), 0.0)
        part += jnp.where(down, pltpu.roll(middle, count - k, 1), 0.0)
        summed += COEFFS[k - 1] * part
    return middle, summed


TILE = 32


def lane_masks(rows, count):
    lane = lax.broadcasted_iota(I32, (rows, count), 1)
    return [(lane >= k, lane < count - k) for k in range(1, HALO + 1)]


def fill(pad_ref, field_ref):
    row_count, count_y, count_z = field_ref.shape
    edge = jnp.zeros((pad_ref.shape[0], PAD, count_z), F32)
    pad_ref[:, 0:PAD, :] = edge
    pad_ref[:, PAD + count_y :, :] = edge
    for x in range(row_count):
        pad_ref[HALO + x, PAD : PAD + count_y, :] = field_ref[x]


def load_scales(in_ref, scale_ref):
    groups = scale_ref.shape[0]
    scale_ref[...] = decode_scale(in_ref[groups * GROUP :, :])


def add_source(source, start, wave, ref, k, edge=0):
    x = source[0, 0] - lax.axis_index("dom") * ref.shape[0]
    lane = lax.broadcasted_iota(I32, (1, ref.shape[2]), 1)

    @pl.when((x >= 0) & (x < ref.shape[0]))
    def _():
        y = source[0, 1] + edge
        row = ref[x, pl.ds(y, 1), :]
        ref[x, pl.ds(y, 1), :] = row + jnp.where(lane == source[0, 2], wave[start[0] + k], 0.0)


def before_kernel(now_f, now_a, prev_f, prev_a, one, two, hit, *rest):
    sum_f, sum_a, base_f, base_a, pad, scale_one, scale_two = rest
    row_count, count_y, count_z = now_f.shape
    masks = lane_masks(TILE, count_z)
    load_scales(one, scale_one)
    load_scales(two, scale_two)
    odd = odd_place()
    fields = ((now_f, prev_f, sum_f, base_f), (now_a, prev_a, sum_a, base_a))
    for f, (now, prev, total, base) in enumerate(fields):
        fill(pad, now)
        decode_halo(one, scale_one, pad, f, (1 - odd) * (HALO + row_count), count_y)
        decode_halo(two, scale_two, pad, f, odd * (HALO + row_count), count_y)

        @pl.loop(0, row_count)
        def _(x):
            for y in range(0, count_y, TILE):
                spot = pl.ds(y, TILE)
                middle, summed = laplace_tile(pad, HALO + x, y, TILE, masks)
                total[x, spot, :] = summed
                value = 2.0 * middle - prev[x, spot, :]
                base[x, spot, :] = value + hit[x, spot, :] if f else value


def first_kernel(halves, anchors, source, begin, wave, sum_f, sum_a, base_f, base_a, *rest):
    next_f, next_a, courant, one, two, *parts, slab, level = rest[-7 - len(ROUTES) :]
    pieces = rest[: -7 - len(ROUTES)]
    row_count, count_y, _ = sum_f.shape
    band = pieces[0].shape[0] // (row_count * halves)
    side = len(pieces)
    me = lax.rem(lax.axis_index("dom"), side)
    for k in range(side):
        for half in range(halves):
            start = pl.multiple_of((half * side + (me ^ k)) * band, 8)
            for x in range(0, row_count, 2):
                speed = pieces[-k][pl.ds((half * row_count + x) * band, 2 * band), :].astype(F32)
                slab[x, pl.ds(start, band), :] = jnp.square(speed[:band])
                slab[x + 1, pl.ds(start, band), :] = jnp.square(speed[band:])

    @pl.loop(0, row_count)
    def _(x):
        for y in range(0, count_y, TILE):
            spot = pl.ds(y, TILE)
            factor = slab[x, pl.ds(anchors[0, 1] + y, TILE), :]
            courant[x, spot, :] = factor
            next_f[x, spot, :] = base_f[x, spot, :] + factor * sum_f[x, spot, :]
            next_a[x, spot, :] = base_a[x, spot, :] + factor * sum_a[x, spot, :]

    add_source(source, begin, wave, next_f, 0)
    code_edges((next_f, next_a), (one, two), level)

    @pl.when(at_border())
    def _():
        for n, part in enumerate(parts):
            size = part.shape[0]
            part[...] = two[n * size : (n + 1) * size, :]


def between_kernel(p1, q1, p0, q0, prev_f, courant, hit, part_f, part_a, bend, pad):
    row_count, count_y, count_z = p1.shape
    masks = lane_masks(TILE, count_z)
    outer = jnp.zeros((HALO, pad.shape[1], count_z), F32)
    pad[0:HALO] = outer
    pad[HALO + row_count :] = outer
    for f, (now, out) in enumerate(((p1, part_f), (q1, part_a))):
        fill(pad, now)

        @pl.loop(0, row_count)
        def _(x):
            for y in range(0, count_y, TILE):
                spot = pl.ds(y, TILE)
                middle, summed = laplace_tile(pad, HALO + x, y, TILE, masks)
                value = courant[x, spot, :] * summed
                if f == 0:
                    bend[x, spot, :] = middle - 2.0 * p0[x, spot, :] + prev_f[x, spot, :]
                else:
                    value += hit[x, spot, :] + (2.0 * middle - q0[x, spot, :])
                out[x, spot, :] = value


def halo_terms(in_ref, scale_ref, f, spot_y, count_y, low):
    per = count_y // GROUP
    rows = []
    for j in range(HALO):
        layer = j + low * (HALO - 1 - 2 * j)
        spot = (f * HALO + layer) * per + spot_y // GROUP
        code = in_ref[pl.ds(pl.multiple_of(spot * GROUP, GROUP), GROUP), :].astype(I32).astype(F32)
        rows.append(code * scale_ref[pl.ds(spot, 1), :])
    return [sum(COEFFS[r + j] * rows[j] for j in range(HALO - r)) for r in range(HALO)]


def second_kernel(groups, anchors, source, begin, wave, p1, q1, p0, courant, part_f, part_a, bend, *rest):
    parts, (one, two), rest = rest[: len(ROUTES)], rest[len(ROUTES) :][:2], rest[len(ROUTES) + 2 :]
    next_f, next_a, own = rest[:3]
    sends = rest[3 : 2 + groups]
    frame, held, scale_one, scale_two = rest[2 + groups :]

    @pl.when(jnp.logical_not(at_border()))
    def _():
        held[...] = two[...]

    @pl.when(at_border())
    def _():
        for n, part in enumerate(parts):
            size = part.shape[0]
            held[n * size : (n + 1) * size, :] = part[...]

    row_count, count_y, count_z = p1.shape
    band = own.shape[0] // row_count
    load_scales(one, scale_one)
    load_scales(held, scale_two)
    odd = odd_place()
    edge = (frame.shape[1] - count_y) // 2
    frame[:, 0:edge, :] = jnp.zeros((row_count, edge, count_z), F32)
    frame[:, edge + count_y :, :] = jnp.zeros((row_count, edge, count_z), F32)
    for y in range(0, count_y, GROUP):
        spot = pl.ds(y, GROUP)
        for ref, scale, low in ((one, scale_one, odd), (held, scale_two, 1 - odd)):
            for f in range(2):
                for r, term in enumerate(halo_terms(ref, scale, f, y, count_y, low)):
                    x = row_count - 1 - r + low * (2 * r + 1 - row_count)
                    term = courant[x, spot, :] * term
                    if f == 0:
                        frame[x, pl.ds(edge + y, GROUP), :] = part_f[x, spot, :] + term
                    else:
                        next_a[x, spot, :] = part_a[x, spot, :] + term

    add_source(source, begin, wave, frame, 1, edge)

    @pl.loop(0, row_count)
    def _(x):
        for y in range(0, count_y, TILE):
            spot = pl.ds(y, TILE)
            change = frame[x, pl.ds(edge + y, TILE), :]
            next_f[x, spot, :] = 2.0 * p1[x, spot, :] - p0[x, spot, :] + change
            image = q1[x, spot, :] * change + next_a[x, spot, :] * bend[x, spot, :]
            frame[x, pl.ds(edge + y, TILE), :] = image

    me = lax.axis_index("dom")
    for k in range(groups):
        start = edge - anchors[0, 1] + (me ^ k) * band
        values = [frame[x, pl.ds(start, band), :] for x in range(row_count)]
        if k == 0:
            for x in range(row_count):
                own[pl.ds(x * band, band), :] = values[x]
        else:
            code_rows(values, sends[k - 1], 0)


def hit_kernel(begin, cells, traces, first, second):
    row_count, count_y, count_z = first.shape
    x = cells[0:1, :] - lax.axis_index("dom") * row_count
    inside = (x >= 0) & (x < row_count)
    row = jnp.where(inside, x * count_y + cells[1:2, :], -1)
    depth = lax.broadcasted_iota(I32, (count_z, row.shape[1]), 0)
    at_depth = depth == cells[2:3, :]
    parts = []
    for k in range(STEPS):
        left = traces[pl.ds(begin[0] + (STEPS - 1 - k), 1), :]
        for _ in range(3):
            part = left.astype(BF16).astype(F32)
            parts.append(jnp.where(at_depth, part, 0.0).astype(BF16))
            left = left - part
    right = jnp.concatenate(parts, axis=0)

    @pl.loop(0, row_count)
    def _(i):
        cell = i * count_y + lax.broadcasted_iota(I32, (count_y, row.shape[1]), 0)
        left = jnp.where(cell == row, 1.0, 0.0).astype(BF16)
        got = lax.dot_general(left, right, (((1,), (1,)), ((), ())), preferred_element_type=F32)
        for k, out in enumerate((first, second)):
            base = 3 * k * count_z
            high = got[:, base : base + count_z]
            middle = got[:, base + count_z : base + 2 * count_z]
            low = got[:, base + 2 * count_z : base + 3 * count_z]
            out[i] = high + (middle + low)


SIZE_X, SIZE_Z, SIZE_C = 4, 4, 2
ROUTES = (0, 1, 3)
HALVES = 2


def place_of(shot):
    return shot // (SIZE_Z * SIZE_C), lax.rem(shot // SIZE_C, SIZE_Z), lax.rem(shot, SIZE_C)


def swap(axis, k):
    bits = k * {"x": SIZE_Z * SIZE_C, "z": SIZE_C, "c": 1}[axis]
    return [(shot, shot ^ bits) for shot in range(SIZE_X * SIZE_Z * SIZE_C)]


def join_kernel(*refs):
    size = refs[0].shape[0]
    for n, ref in enumerate(refs[:-1]):
        refs[-1][pl.ds(n * size, size), :] = ref[...]


def pick_kernel(layout, row_count, halves, anchors, *refs):
    count = len(layout)
    ins, outs, table = refs[:count], refs[count:-1], refs[-1]
    side = len(outs)
    piece = outs[0].shape[0] // halves
    per = piece // row_count
    block = ins[0].shape[0] // len(layout[0])
    own = block // per
    x, z, c = place_of(lax.axis_index("shot"))
    half, me = lax.axis_index("dom") // side, lax.rem(lax.axis_index("dom"), side)
    anchor = anchors[0, 0] + half * (side * row_count)
    first = anchor // own
    span = table.shape[1] // block
    for ref, owners in zip(ins, layout):
        for n, (dx, dz, dc, dh) in enumerate(owners):
            place = ((x ^ dx) * SIZE_Z + (z ^ dz)) * SIZE_C + (c ^ dc) - first

            @pl.when((place >= 0) & (place < span))
            def _():
                start = pl.multiple_of(place * block, 8)
                table[half ^ dh, pl.ds(start, block), :] = ref[pl.ds(n * block, block), :].astype(F32)

    offset = (anchor - first * own) * per
    for k in range(side):
        start = pl.multiple_of(offset + (me ^ k) * piece, 8)
        for h in range(halves):
            outs[k][pl.ds(h * piece, piece), :] = table[h, pl.ds(start, piece), :].astype(BF16)


def band_kernel(groups, row_count, block, anchors, own, *refs):
    got, (keep, send, table) = refs[: groups - 1], refs[groups - 1 :]
    per = own.shape[0] // row_count
    c = lax.rem(lax.axis_index("shot"), SIZE_C)
    me = lax.axis_index("dom")
    anchor = anchors[0, 0]
    first = anchor // (block // per)
    table[...] = jnp.zeros(table.shape, F32)
    offset = (anchor - first * (block // per)) * per
    for k in range(groups):
        base = offset + (me ^ k) * (row_count * per)
        if k == 0:
            table[pl.ds(pl.multiple_of(base, 8), row_count * per), :] = own[...]
        else:
            for n, value in enumerate(decode_rows(got[-k], row_count, per)):
                table[pl.ds(pl.multiple_of(base + n * per, 8), per), :] = value
    mine = lax.rem(c + first, SIZE_C)
    for i in range(keep.shape[0] // block):
        for out, parity in ((keep, mine), (send, 1 - mine)):
            start = pl.multiple_of((SIZE_C * i + parity) * block, 8)
            out[pl.ds(i * block, block), :] = table[pl.ds(start, block), :]


def core_kernel(block, per, anchors, other, keep, got, own, *refs):
    sends, total = refs[:-1], refs[-1]
    x, _, c = place_of(lax.axis_index("shot"))
    total[...] = jnp.zeros(total.shape, F32)
    for ref, place in ((keep, anchors), (got, other)):
        first = place[0, 0] // (block // per)
        low = (first + lax.rem(c + first, SIZE_C)) // SIZE_C
        for i in range(ref.shape[0] // block):
            spot = pl.ds(pl.multiple_of((low + i) * block, 8), block)
            total[spot, :] += ref[pl.ds(i * block, block), :]
    size = own.shape[0]
    own[...] = total[pl.ds(pl.multiple_of(x * size, 8), size), :]
    for k, send in enumerate(sends, 1):
        start = (x ^ k) * size
        values = [total[pl.ds(pl.multiple_of(start + n * per, 8), per), :] for n in range(size // per)]
        code_rows(values, send, 0)


def along_x_kernel(per, mine, *refs):
    got, rest = refs[: SIZE_X - 1], refs[SIZE_X - 1 :]
    own, sends, total = rest[0], rest[1:-1], rest[-1]
    total[...] = mine[...]
    for ref in got:
        for n, value in enumerate(decode_rows(ref, total.shape[0] // per, per)):
            total[pl.ds(n * per, per), :] += value
    _, z, _ = place_of(lax.axis_index("shot"))
    size = own.shape[0]
    own[...] = total[pl.ds(pl.multiple_of(z * size, 8), size), :]
    for k, send in enumerate(sends, 1):
        start = (z ^ k) * size
        values = [total[pl.ds(pl.multiple_of(start + n * per, 8), per), :] for n in range(size // per)]
        code_rows(values, send, 0)


def along_z_kernel(per, mine, *refs):
    got, out = refs[:-1], refs[-1]
    for parts in zip(range(mine.shape[0] // per), *[decode_rows(r, mine.shape[0] // per, per) for r in got]):
        n, values = parts[0], parts[1:]
        total = mine[pl.ds(n * per, per), :]
        for value in values:
            total += value
        out[pl.ds(n * per, per), :] = total


def swap_z(groups, k):
    shots, doms = (k % SIZE_Z) * SIZE_C, (k // SIZE_Z) * (groups // HALVES)
    return [
        (shot * groups + dom, (shot ^ shots) * groups + (dom ^ doms))
        for shot in range(SIZE_X * SIZE_Z * SIZE_C)
        for dom in range(groups)
    ]


def across(groups, k):
    return [(i, i ^ k) for i in range(groups)]


def far_first(values):
    return sorted(values, reverse=True)


def exchange(parts, axis, pairs):
    got = {}
    for k in far_first(range(1, len(parts) + 1)):
        got[k] = lax.ppermute(parts[k - 1], axis, pairs(k))
    return [got[k] for k in sorted(got)]


def body(
    velocity,
    anchors,
    start_step,
    source,
    receivers,
    traces,
    wavelet,
    fwd_prev,
    fwd_now,
    adj_prev,
    adj_now,
):
    row_count, count_y, count_z = fwd_now.shape[1:]
    groups = lax.axis_size("dom")
    own_rows, band = velocity.shape[:2]
    block = own_rows * band
    piece = row_count * band
    p0, q0, p_prev, q_prev = fwd_now[0], adj_now[0], fwd_prev[0], adj_prev[0]
    scalars = (anchors, source, start_step, wavelet)
    one_pairs = [(i, i ^ 1) for i in range(groups)]
    two_pairs = [(i, i + 1) for i in range(1, groups - 1, 2)]
    two_pairs += [(b, a) for a, b in two_pairs]

    along = {axis: functools.partial(swap, axis) for axis in "xzc"}
    between = functools.partial(across, groups)

    local = velocity.reshape(block, count_z)
    other = lax.ppermute(anchors, "shot", swap("c", 1))
    near = [local] + exchange([local] * (HALVES * SIZE_Z - 1), ("shot", "dom"), functools.partial(swap_z, groups))

    half = halo_rows(2 * HALO, count_y)
    code = struct((half, count_z), I16)
    levels = pltpu.VMEM((2 * HALO * count_y // GROUP, count_z), I32)
    one, two = call(encode_kernel, (code, code), (p0, q0), "vv", (levels,))
    from_one = lax.ppermute(one, "dom", one_pairs)
    from_two = lax.ppermute(two, "dom", two_pairs)

    (line,) = call(join_kernel, (struct((len(near) * block, count_z), BF16),), near, "v" * len(near))
    line, other, one = lax.optimization_barrier((line, other, one))
    field = struct((row_count, count_y, count_z), F32)
    hits = call(hit_kernel, (field, field), (start_step, receivers[0], traces[0]), "svv")
    plane = [line] + exchange([line] * (SIZE_X - 1), "shot", along["x"])
    plane = list(lax.optimization_barrier((*plane, hits[0])))[:SIZE_X]
    plane += [lax.ppermute(part, "shot", swap("c", 1)) for part in plane]
    *plane, from_one, from_two = lax.optimization_barrier((*plane, from_one, from_two))
    layout = [
        [(dx, k % SIZE_Z, dc, k // SIZE_Z) for k in range(HALVES * SIZE_Z)]
        for dc in range(SIZE_C)
        for dx in range(SIZE_X)
    ]
    span = -(-(row_count * groups + own_rows - 1) // own_rows)
    span += span % SIZE_C
    table = pltpu.VMEM((span * block, count_z), F32)
    side = groups // HALVES
    pieces = call(
        functools.partial(pick_kernel, layout, row_count, HALVES),
        [struct((HALVES * piece, count_z), BF16)] * side,
        (anchors, *plane),
        "s" + "v" * len(plane),
        (pltpu.VMEM((HALVES, -(-(row_count * side + own_rows - 1) // own_rows) * block, count_z), F32),),
    )
    pieces = [pieces[0]] + exchange(pieces[1:], "dom", between)[::-1]

    padded = pltpu.VMEM((row_count + 2 * HALO, count_y + 2 * PAD, count_z), F32)
    scale = pltpu.VMEM((2 * HALO * count_y // GROUP, count_z), F32)
    slab = pltpu.VMEM((row_count, groups * band, count_z), F32)
    sums = call(
        before_kernel,
        (field,) * 4,
        (p0, q0, p_prev, q_prev, from_one, from_two, hits[0]),
        "v" * 7,
        (padded, scale, scale),
    )
    part = struct((half // len(ROUTES), count_z), I16)
    p1, q1, courant, one, two, *parts = call(
        functools.partial(first_kernel, HALVES),
        (field, field, field, code, code, *[part] * len(ROUTES)),
        (*scalars, *sums, *pieces),
        "ssss" + "v" * (4 + side),
        (slab, levels),
    )
    border = (side - 1, side)
    moved = [lax.ppermute(part, "dom", [(a, a ^ k) for a in border]) for part, k in zip(parts[1:], ROUTES[1:])]
    one, two, moved = lax.optimization_barrier((one, two, moved))
    parts = [
        lax.ppermute(part, "dom", [(a ^ k, b) for a, b in (border, border[::-1])])
        for part, k in zip((parts[0], *moved), ROUTES)
    ]
    from_one = lax.ppermute(one, "dom", one_pairs)
    from_two = lax.ppermute(two, "dom", [(a, b) for a, b in two_pairs if a not in border])
    part_f, part_a, bend = call(
        between_kernel,
        (field,) * 3,
        (p1, q1, p0, q0, p_prev, courant, hits[1]),
        "v" * 7,
        (padded,),
    )

    edge = groups * band - count_y
    coded = struct((code_rows_of(row_count, band), count_z), I16)
    frame = pltpu.VMEM((row_count, count_y + 2 * edge, count_z), F32)
    p2, q2, own, *sends = call(
        functools.partial(second_kernel, groups),
        (field, field, struct((piece, count_z), F32), *[coded] * (groups - 1)),
        (*scalars, p1, q1, p0, courant, part_f, part_a, bend, *parts, from_one, from_two),
        "ssss" + "v" * (9 + len(ROUTES)),
        (frame, pltpu.VMEM(code.shape, I16), scale, scale),
    )
    got = exchange(sends, "dom", between)[::-1]

    part = struct((span // SIZE_C * block, count_z), F32)
    keep, send = call(
        functools.partial(band_kernel, groups, row_count, block),
        (part, part),
        (anchors, own, *got),
        "s" + "v" * groups,
        (table,),
    )
    got = lax.ppermute(send, "shot", swap("c", 1))

    size = SIZE_Z * block
    coded = struct((code_rows_of(size // band, band), count_z), I16)
    total = pltpu.VMEM(((SIZE_X * SIZE_Z + 1) * block, count_z), F32)
    own, *sends = call(
        functools.partial(core_kernel, block, band),
        (struct((size, count_z), F32), *[coded] * (SIZE_X - 1)),
        (anchors, other, keep, got),
        "ssvv",
        (total,),
    )
    got = exchange(sends, "shot", along["x"])[::-1]

    coded = struct((code_rows_of(own_rows, band), count_z), I16)
    own, *sends = call(
        functools.partial(along_x_kernel, band),
        (struct((block, count_z), F32), *[coded] * (SIZE_Z - 1)),
        (own, *got),
        "v" * SIZE_X,
        (pltpu.VMEM((size, count_z), F32),),
    )
    got = exchange(sends, "shot", along["z"])[::-1]

    (gradient,) = call(
        functools.partial(along_z_kernel, band),
        (struct((block, count_z), F32),),
        (own, *got),
        "v" * SIZE_Z,
    )
    return (p2[None], q2[None], gradient.reshape(own_rows, band, count_z))


def solution(mesh):
    placed = (
        P("shot", "dom", None),
        P("shot", None),
        P("shot"),
        P("shot", None),
        P("shot", None, None),
        P("shot", None, None),
        P(),
        P("shot", "dom", None, None),
        P("shot", "dom", None, None),
        P("shot", "dom", None, None),
        P("shot", "dom", None, None),
    )
    return jax.shard_map(
        body,
        mesh=mesh,
        in_specs=placed,
        out_specs=(
            P("shot", "dom", None, None),
            P("shot", "dom", None, None),
            P("shot", "dom", None),
        ),
        check_vma=False,
    )
```

```python
import functools

import jax
import jax.numpy as jnp
from jax import lax
from jax.experimental import pallas as pl
from jax.experimental.pallas import tpu as pltpu
from jax.sharding import PartitionSpec as P

STEPS = 2
CENTER = -205.0 / 72.0
COEFFS = (8.0 / 5.0, -1.0 / 5.0, 8.0 / 315.0, -1.0 / 560.0)

F32 = jnp.float32
BF16 = jnp.bfloat16
I16 = jnp.int16
I32 = jnp.int32

VMEM_LIMIT = 32 * 1024 * 1024
FLOOR = 1e-33
TOP = 32700.0
HALO = 4
GROUP = 32


def vmem():
    return pl.BlockSpec(memory_space=pltpu.VMEM)


def smem():
    return pl.BlockSpec(memory_space=pltpu.SMEM)


def call(kernel, outs, args, spaces, scratch=(), cost=1_000_000):
    moved = sum(a.size * a.dtype.itemsize for a in (*outs, *args))
    return pl.pallas_call(
        kernel,
        out_shape=list(outs),
        in_specs=[smem() if s == "s" else vmem() for s in spaces],
        out_specs=[vmem()] * len(outs),
        scratch_shapes=list(scratch),
        compiler_params=pltpu.CompilerParams(vmem_limit_bytes=VMEM_LIMIT),
        cost_estimate=pl.CostEstimate(flops=0, bytes_accessed=0, transcendentals=0),
    )(*args)


def struct(shape, dtype):
    return jax.ShapeDtypeStruct(shape, dtype)


def code_group(values):
    top = jnp.max(jnp.abs(values), axis=0, keepdims=True)
    level = jnp.ceil(jnp.log2(jnp.maximum(top, FLOOR)) * 256.0) + 1.0
    scaled = values * (TOP * jnp.exp2(level * (-1.0 / 256.0)))
    return jnp.round(scaled).astype(I32), level.astype(I32)


def code_rows(values, out_ref, base):
    band = values[0].shape[0]
    levels = []
    for n in range(0, len(values), 2):
        codes = []
        for value in values[n : n + 2]:
            code, level = code_group(value)
            codes.append(code)
            levels.append(level)
        out_ref[pl.ds(base + n * band, 2 * band), :] = jnp.concatenate(codes, axis=0).astype(I16)
    levels += [jnp.zeros((-len(levels) % 16, values[0].shape[1]), I32)]
    spot = pl.ds(base + len(values) * band, code_rows_of(len(values), band) - len(values) * band)
    out_ref[spot, :] = jnp.concatenate(levels, axis=0).astype(I16)


def code_rows_of(groups, band):
    return groups * band + groups + -groups % 16


def decode_rows(in_ref, groups, band):
    scales = decode_scale(in_ref[pl.ds(groups * band, groups + -groups % 16), :])
    for n in range(0, groups, 2):
        pair = in_ref[pl.ds(n * band, 2 * band), :].astype(I32).astype(F32)
        yield pair[:band] * scales[n : n + 1]
        yield pair[band:] * scales[n + 1 : n + 2]


def decode_scale(levels):
    return jnp.exp2(levels.astype(I32).astype(F32) * (1.0 / 256.0)) * (1.0 / TOP)


def code_halos(field, rows, out_ref, level_ref, base):
    for n, layer in enumerate(rows):
        value = field(layer)
        count = value.shape[0] // GROUP
        for g in range(count):
            code, level = code_group(value[g * GROUP : (g + 1) * GROUP])
            spot = base + n * count + g
            out_ref[pl.ds(spot * GROUP, GROUP), :] = code.astype(I16)
            level_ref[pl.ds(spot, 1), :] = level


def halo_rows(layers, count_y):
    groups = layers * count_y // GROUP
    return groups * GROUP + groups


def odd_place():
    return lax.rem(lax.axis_index("dom"), 2)


def at_border():
    me, middle = lax.axis_index("dom"), lax.axis_size("dom") // HALVES
    return (me == middle) | (me == middle - 1)


def code_edges(fields, out_refs, level_ref):
    row_count, count_y, _ = fields[0].shape
    per = HALO * count_y // GROUP
    odd = odd_place()
    for out_ref, high in zip(out_refs, (1 - odd, odd)):
        first = high * (row_count - HALO)
        for f, ref in enumerate(fields):
            code_halos(lambda x: ref[x], [first + n for n in range(HALO)], out_ref, level_ref, f * per)
        out_ref[2 * per * GROUP :, :] = level_ref[...].astype(I16)


def encode_kernel(now_f, now_a, one, two, level_ref):
    code_edges((now_f, now_a), (one, two), level_ref)


def decode_halo(in_ref, scale_ref, pad_ref, f, first, count_y):
    per = count_y // GROUP
    for layer in range(HALO):
        for g in range(per):
            spot = (f * HALO + layer) * per + g
            code = in_ref[pl.ds(spot * GROUP, GROUP), :].astype(I32).astype(F32)
            pad_ref[first + layer, pl.ds(PAD + g * GROUP, GROUP), :] = code * scale_ref[pl.ds(spot, 1), :]


PAD = 8


def laplace_tile(pad_ref, layer, y, rows, masks):
    middle = pad_ref[layer, pl.ds(PAD + y, rows), :]
    summed = (3.0 * CENTER) * middle
    for k in range(1, HALO + 1):
        up, down = masks[k - 1]
        count = middle.shape[1]
        part = pad_ref[layer + k, pl.ds(PAD + y, rows), :] + pad_ref[layer - k, pl.ds(PAD + y, rows), :]
        part += pad_ref[layer, pl.ds(PAD + y + k, rows), :] + pad_ref[layer, pl.ds(PAD + y - k, rows), :]
        part += jnp.where(up, pltpu.roll(middle, k, 1), 0.0)
        part += jnp.where(down, pltpu.roll(middle, count - k, 1), 0.0)
        summed += COEFFS[k - 1] * part
    return middle, summed


TILE = 32


def lane_masks(rows, count):
    lane = lax.broadcasted_iota(I32, (rows, count), 1)
    return [(lane >= k, lane < count - k) for k in range(1, HALO + 1)]


def fill(pad_ref, field_ref):
    row_count, count_y, count_z = field_ref.shape
    edge = jnp.zeros((pad_ref.shape[0], PAD, count_z), F32)
    pad_ref[:, 0:PAD, :] = edge
    pad_ref[:, PAD + count_y :, :] = edge
    for x in range(row_count):
        pad_ref[HALO + x, PAD : PAD + count_y, :] = field_ref[x]


def load_scales(in_ref, scale_ref):
    groups = scale_ref.shape[0]
    scale_ref[...] = decode_scale(in_ref[groups * GROUP :, :])


def add_source(source, start, wave, ref, k, edge=0):
    x = source[0, 0] - lax.axis_index("dom") * ref.shape[0]
    lane = lax.broadcasted_iota(I32, (1, ref.shape[2]), 1)

    @pl.when((x >= 0) & (x < ref.shape[0]))
    def _():
        y = source[0, 1] + edge
        row = ref[x, pl.ds(y, 1), :]
        ref[x, pl.ds(y, 1), :] = row + jnp.where(lane == source[0, 2], wave[start[0] + k], 0.0)


def before_kernel(now_f, now_a, prev_f, prev_a, one, two, hit, *rest):
    sum_f, sum_a, base_f, base_a, pad, scale_one, scale_two = rest
    row_count, count_y, count_z = now_f.shape
    masks = lane_masks(TILE, count_z)
    load_scales(one, scale_one)
    load_scales(two, scale_two)
    odd = odd_place()
    fields = ((now_f, prev_f, sum_f, base_f), (now_a, prev_a, sum_a, base_a))
    for f, (now, prev, total, base) in enumerate(fields):
        fill(pad, now)
        decode_halo(one, scale_one, pad, f, (1 - odd) * (HALO + row_count), count_y)
        decode_halo(two, scale_two, pad, f, odd * (HALO + row_count), count_y)

        @pl.loop(0, row_count)
        def _(x):
            for y in range(0, count_y, TILE):
                spot = pl.ds(y, TILE)
                middle, summed = laplace_tile(pad, HALO + x, y, TILE, masks)
                total[x, spot, :] = summed
                value = 2.0 * middle - prev[x, spot, :]
                base[x, spot, :] = value + hit[x, spot, :] if f else value


def first_kernel(halves, anchors, source, begin, wave, sum_f, sum_a, base_f, base_a, *rest):
    next_f, next_a, courant, one, two, *parts, slab, level = rest[-7 - len(ROUTES) :]
    pieces = rest[: -7 - len(ROUTES)]
    row_count, count_y, _ = sum_f.shape
    band = pieces[0].shape[0] // (row_count * halves)
    side = len(pieces)
    me = lax.rem(lax.axis_index("dom"), side)
    for k in range(side):
        for half in range(halves):
            start = pl.multiple_of((half * side + (me ^ k)) * band, 8)
            for x in range(0, row_count, 2):
                speed = pieces[-k][pl.ds((half * row_count + x) * band, 2 * band), :].astype(F32)
                slab[x, pl.ds(start, band), :] = jnp.square(speed[:band])
                slab[x + 1, pl.ds(start, band), :] = jnp.square(speed[band:])

    @pl.loop(0, row_count)
    def _(x):
        for y in range(0, count_y, TILE):
            spot = pl.ds(y, TILE)
            factor = slab[x, pl.ds(anchors[0, 1] + y, TILE), :]
            courant[x, spot, :] = factor
            next_f[x, spot, :] = base_f[x, spot, :] + factor * sum_f[x, spot, :]
            next_a[x, spot, :] = base_a[x, spot, :] + factor * sum_a[x, spot, :]

    add_source(source, begin, wave, next_f, 0)
    code_edges((next_f, next_a), (one, two), level)

    @pl.when(at_border())
    def _():
        for n, part in enumerate(parts):
            size = part.shape[0]
            part[...] = two[n * size : (n + 1) * size, :]


def between_kernel(p1, q1, p0, q0, prev_f, courant, hit, part_f, part_a, bend, pad):
    row_count, count_y, count_z = p1.shape
    masks = lane_masks(TILE, count_z)
    outer = jnp.zeros((HALO, pad.shape[1], count_z), F32)
    pad[0:HALO] = outer
    pad[HALO + row_count :] = outer
    for f, (now, out) in enumerate(((p1, part_f), (q1, part_a))):
        fill(pad, now)

        @pl.loop(0, row_count)
        def _(x):
            for y in range(0, count_y, TILE):
                spot = pl.ds(y, TILE)
                middle, summed = laplace_tile(pad, HALO + x, y, TILE, masks)
                value = courant[x, spot, :] * summed
                if f == 0:
                    bend[x, spot, :] = middle - 2.0 * p0[x, spot, :] + prev_f[x, spot, :]
                else:
                    value += hit[x, spot, :] + (2.0 * middle - q0[x, spot, :])
                out[x, spot, :] = value


def halo_terms(in_ref, scale_ref, f, spot_y, count_y, low):
    per = count_y // GROUP
    rows = []
    for j in range(HALO):
        layer = j + low * (HALO - 1 - 2 * j)
        spot = (f * HALO + layer) * per + spot_y // GROUP
        code = in_ref[pl.ds(pl.multiple_of(spot * GROUP, GROUP), GROUP), :].astype(I32).astype(F32)
        rows.append(code * scale_ref[pl.ds(spot, 1), :])
    return [sum(COEFFS[r + j] * rows[j] for j in range(HALO - r)) for r in range(HALO)]


def second_kernel(groups, anchors, source, begin, wave, p1, q1, p0, courant, part_f, part_a, bend, *rest):
    parts, (one, two), rest = rest[: len(ROUTES)], rest[len(ROUTES) :][:2], rest[len(ROUTES) + 2 :]
    next_f, next_a, own = rest[:3]
    sends = rest[3 : 2 + groups]
    frame, held, scale_one, scale_two = rest[2 + groups :]

    @pl.when(jnp.logical_not(at_border()))
    def _():
        held[...] = two[...]

    @pl.when(at_border())
    def _():
        for n, part in enumerate(parts):
            size = part.shape[0]
            held[n * size : (n + 1) * size, :] = part[...]

    row_count, count_y, count_z = p1.shape
    band = own.shape[0] // row_count
    load_scales(one, scale_one)
    load_scales(held, scale_two)
    odd = odd_place()
    edge = (frame.shape[1] - count_y) // 2
    frame[:, 0:edge, :] = jnp.zeros((row_count, edge, count_z), F32)
    frame[:, edge + count_y :, :] = jnp.zeros((row_count, edge, count_z), F32)
    for y in range(0, count_y, GROUP):
        spot = pl.ds(y, GROUP)
        for ref, scale, low in ((one, scale_one, odd), (held, scale_two, 1 - odd)):
            for f in range(2):
                for r, term in enumerate(halo_terms(ref, scale, f, y, count_y, low)):
                    x = row_count - 1 - r + low * (2 * r + 1 - row_count)
                    term = courant[x, spot, :] * term
                    if f == 0:
                        frame[x, pl.ds(edge + y, GROUP), :] = part_f[x, spot, :] + term
                    else:
                        next_a[x, spot, :] = part_a[x, spot, :] + term

    add_source(source, begin, wave, frame, 1, edge)

    @pl.loop(0, row_count)
    def _(x):
        for y in range(0, count_y, TILE):
            spot = pl.ds(y, TILE)
            change = frame[x, pl.ds(edge + y, TILE), :]
            next_f[x, spot, :] = 2.0 * p1[x, spot, :] - p0[x, spot, :] + change
            image = q1[x, spot, :] * change + next_a[x, spot, :] * bend[x, spot, :]
            frame[x, pl.ds(edge + y, TILE), :] = image

    me = lax.axis_index("dom")
    for k in range(groups):
        start = edge - anchors[0, 1] + (me ^ k) * band
        values = [frame[x, pl.ds(start, band), :] for x in range(row_count)]
        if k == 0:
            for x in range(row_count):
                own[pl.ds(x * band, band), :] = values[x]
        else:
            code_rows(values, sends[k - 1], 0)


def hit_kernel(begin, cells, traces, first, second):
    row_count, count_y, count_z = first.shape
    x = cells[0:1, :] - lax.axis_index("dom") * row_count
    inside = (x >= 0) & (x < row_count)
    row = jnp.where(inside, x * count_y + cells[1:2, :], -1)
    depth = lax.broadcasted_iota(I32, (count_z, row.shape[1]), 0)
    at_depth = depth == cells[2:3, :]
    parts = []
    for k in range(STEPS):
        left = traces[pl.ds(begin[0] + (STEPS - 1 - k), 1), :]
        for _ in range(3):
            part = left.astype(BF16).astype(F32)
            parts.append(jnp.where(at_depth, part, 0.0).astype(BF16))
            left = left - part
    right = jnp.concatenate(parts, axis=0)

    @pl.loop(0, row_count)
    def _(i):
        cell = i * count_y + lax.broadcasted_iota(I32, (count_y, row.shape[1]), 0)
        left = jnp.where(cell == row, 1.0, 0.0).astype(BF16)
        got = lax.dot_general(left, right, (((1,), (1,)), ((), ())), preferred_element_type=F32)
        for k, out in enumerate((first, second)):
            base = 3 * k * count_z
            high = got[:, base : base + count_z]
            middle = got[:, base + count_z : base + 2 * count_z]
            low = got[:, base + 2 * count_z : base + 3 * count_z]
            out[i] = high + (middle + low)


SIZE_X, SIZE_Z, SIZE_C = 4, 4, 2
ROUTES = (0, 1, 3)
HALVES = 2


def place_of(shot):
    return shot // (SIZE_Z * SIZE_C), lax.rem(shot // SIZE_C, SIZE_Z), lax.rem(shot, SIZE_C)


def swap(axis, k):
    bits = k * {"x": SIZE_Z * SIZE_C, "z": SIZE_C, "c": 1}[axis]
    return [(shot, shot ^ bits) for shot in range(SIZE_X * SIZE_Z * SIZE_C)]


def join_kernel(*refs):
    size = refs[0].shape[0]
    for n, ref in enumerate(refs[:-1]):
        refs[-1][pl.ds(n * size, size), :] = ref[...]


def pick_kernel(layout, row_count, halves, anchors, *refs):
    count = len(layout)
    ins, outs, table = refs[:count], refs[count:-1], refs[-1]
    side = len(outs)
    piece = outs[0].shape[0] // halves
    per = piece // row_count
    block = ins[0].shape[0] // len(layout[0])
    own = block // per
    x, z, c = place_of(lax.axis_index("shot"))
    half, me = lax.axis_index("dom") // side, lax.rem(lax.axis_index("dom"), side)
    anchor = anchors[0, 0] + half * (side * row_count)
    first = anchor // own
    span = table.shape[1] // block
    for ref, owners in zip(ins, layout):
        for n, (dx, dz, dc, dh) in enumerate(owners):
            place = ((x ^ dx) * SIZE_Z + (z ^ dz)) * SIZE_C + (c ^ dc) - first

            @pl.when((place >= 0) & (place < span))
            def _():
                start = pl.multiple_of(place * block, 8)
                table[half ^ dh, pl.ds(start, block), :] = ref[pl.ds(n * block, block), :].astype(F32)

    offset = (anchor - first * own) * per
    for k in range(side):
        start = pl.multiple_of(offset + (me ^ k) * piece, 8)
        for h in range(halves):
            outs[k][pl.ds(h * piece, piece), :] = table[h, pl.ds(start, piece), :].astype(BF16)


def band_kernel(groups, row_count, block, anchors, own, *refs):
    got, (keep, send, table) = refs[: groups - 1], refs[groups - 1 :]
    per = own.shape[0] // row_count
    c = lax.rem(lax.axis_index("shot"), SIZE_C)
    me = lax.axis_index("dom")
    anchor = anchors[0, 0]
    first = anchor // (block // per)
    table[...] = jnp.zeros(table.shape, F32)
    offset = (anchor - first * (block // per)) * per
    for k in range(groups):
        base = offset + (me ^ k) * (row_count * per)
        if k == 0:
            table[pl.ds(pl.multiple_of(base, 8), row_count * per), :] = own[...]
        else:
            for n, value in enumerate(decode_rows(got[-k], row_count, per)):
                table[pl.ds(pl.multiple_of(base + n * per, 8), per), :] = value
    mine = lax.rem(c + first, SIZE_C)
    for i in range(keep.shape[0] // block):
        for out, parity in ((keep, mine), (send, 1 - mine)):
            start = pl.multiple_of((SIZE_C * i + parity) * block, 8)
            out[pl.ds(i * block, block), :] = table[pl.ds(start, block), :]


def core_kernel(block, per, anchors, other, keep, got, own, *refs):
    sends, total = refs[:-1], refs[-1]
    x, _, c = place_of(lax.axis_index("shot"))
    total[...] = jnp.zeros(total.shape, F32)
    for ref, place in ((keep, anchors), (got, other)):
        first = place[0, 0] // (block // per)
        low = (first + lax.rem(c + first, SIZE_C)) // SIZE_C
        for i in range(ref.shape[0] // block):
            spot = pl.ds(pl.multiple_of((low + i) * block, 8), block)
            total[spot, :] += ref[pl.ds(i * block, block), :]
    size = own.shape[0]
    own[...] = total[pl.ds(pl.multiple_of(x * size, 8), size), :]
    for k, send in enumerate(sends, 1):
        start = (x ^ k) * size
        values = [total[pl.ds(pl.multiple_of(start + n * per, 8), per), :] for n in range(size // per)]
        code_rows(values, send, 0)


def along_x_kernel(per, mine, *refs):
    got, rest = refs[: SIZE_X - 1], refs[SIZE_X - 1 :]
    own, sends, total = rest[0], rest[1:-1], rest[-1]
    total[...] = mine[...]
    for ref in got:
        for n, value in enumerate(decode_rows(ref, total.shape[0] // per, per)):
            total[pl.ds(n * per, per), :] += value
    _, z, _ = place_of(lax.axis_index("shot"))
    size = own.shape[0]
    own[...] = total[pl.ds(pl.multiple_of(z * size, 8), size), :]
    for k, send in enumerate(sends, 1):
        start = (z ^ k) * size
        values = [total[pl.ds(pl.multiple_of(start + n * per, 8), per), :] for n in range(size // per)]
        code_rows(values, send, 0)


def along_z_kernel(per, mine, *refs):
    got, out = refs[:-1], refs[-1]
    for parts in zip(range(mine.shape[0] // per), *[decode_rows(r, mine.shape[0] // per, per) for r in got]):
        n, values = parts[0], parts[1:]
        total = mine[pl.ds(n * per, per), :]
        for value in values:
            total += value
        out[pl.ds(n * per, per), :] = total


def swap_z(groups, k):
    shots, doms = (k % SIZE_Z) * SIZE_C, (k // SIZE_Z) * (groups // HALVES)
    return [
        (shot * groups + dom, (shot ^ shots) * groups + (dom ^ doms))
        for shot in range(SIZE_X * SIZE_Z * SIZE_C)
        for dom in range(groups)
    ]


def across(groups, k):
    return [(i, i ^ k) for i in range(groups)]


def far_first(values):
    return sorted(values, reverse=True)


def exchange(parts, axis, pairs):
    got = {}
    for k in far_first(range(1, len(parts) + 1)):
        got[k] = lax.ppermute(parts[k - 1], axis, pairs(k))
    return [got[k] for k in sorted(got)]


def body(
    velocity,
    anchors,
    start_step,
    source,
    receivers,
    traces,
    wavelet,
    fwd_prev,
    fwd_now,
    adj_prev,
    adj_now,
):
    row_count, count_y, count_z = fwd_now.shape[1:]
    groups = lax.axis_size("dom")
    own_rows, band = velocity.shape[:2]
    block = own_rows * band
    piece = row_count * band
    p0, q0, p_prev, q_prev = fwd_now[0], adj_now[0], fwd_prev[0], adj_prev[0]
    scalars = (anchors, source, start_step, wavelet)
    one_pairs = [(i, i ^ 1) for i in range(groups)]
    two_pairs = [(i, i + 1) for i in range(1, groups - 1, 2)]
    two_pairs += [(b, a) for a, b in two_pairs]

    along = {axis: functools.partial(swap, axis) for axis in "xzc"}
    between = functools.partial(across, groups)

    local = velocity.reshape(block, count_z)
    other = lax.ppermute(anchors, "shot", swap("c", 1))
    near = [local] + exchange([local] * (HALVES * SIZE_Z - 1), ("shot", "dom"), functools.partial(swap_z, groups))

    half = halo_rows(2 * HALO, count_y)
    code = struct((half, count_z), I16)
    levels = pltpu.VMEM((2 * HALO * count_y // GROUP, count_z), I32)
    one, two = call(encode_kernel, (code, code), (p0, q0), "vv", (levels,))
    from_one = lax.ppermute(one, "dom", one_pairs)
    from_two = lax.ppermute(two, "dom", two_pairs)

    (line,) = call(join_kernel, (struct((len(near) * block, count_z), BF16),), near, "v" * len(near))
    line, other, one = lax.optimization_barrier((line, other, one))
    field = struct((row_count, count_y, count_z), F32)
    hits = call(hit_kernel, (field, field), (start_step, receivers[0], traces[0]), "svv")
    plane = [line] + exchange([line] * (SIZE_X - 1), "shot", along["x"])
    plane = list(lax.optimization_barrier((*plane, hits[0])))[:SIZE_X]
    plane += [lax.ppermute(part, "shot", swap("c", 1)) for part in plane]
    *plane, from_one, from_two = lax.optimization_barrier((*plane, from_one, from_two))
    layout = [
        [(dx, k % SIZE_Z, dc, k // SIZE_Z) for k in range(HALVES * SIZE_Z)]
        for dc in range(SIZE_C)
        for dx in range(SIZE_X)
    ]
    span = -(-(row_count * groups + own_rows - 1) // own_rows)
    span += span % SIZE_C
    table = pltpu.VMEM((span * block, count_z), F32)
    side = groups // HALVES
    pieces = call(
        functools.partial(pick_kernel, layout, row_count, HALVES),
        [struct((HALVES * piece, count_z), BF16)] * side,
        (anchors, *plane),
        "s" + "v" * len(plane),
        (pltpu.VMEM((HALVES, -(-(row_count * side + own_rows - 1) // own_rows) * block, count_z), F32),),
    )
    pieces = [pieces[0]] + exchange(pieces[1:], "dom", between)[::-1]

    padded = pltpu.VMEM((row_count + 2 * HALO, count_y + 2 * PAD, count_z), F32)
    scale = pltpu.VMEM((2 * HALO * count_y // GROUP, count_z), F32)
    slab = pltpu.VMEM((row_count, groups * band, count_z), F32)
    sums = call(
        before_kernel,
        (field,) * 4,
        (p0, q0, p_prev, q_prev, from_one, from_two, hits[0]),
        "v" * 7,
        (padded, scale, scale),
    )
    part = struct((half // len(ROUTES), count_z), I16)
    p1, q1, courant, one, two, *parts = call(
        functools.partial(first_kernel, HALVES),
        (field, field, field, code, code, *[part] * len(ROUTES)),
        (*scalars, *sums, *pieces),
        "ssss" + "v" * (4 + side),
        (slab, levels),
    )
    border = (side - 1, side)
    moved = [lax.ppermute(part, "dom", [(a, a ^ k) for a in border]) for part, k in zip(parts[1:], ROUTES[1:])]
    part_f, part_a, bend = call(
        between_kernel,
        (field,) * 3,
        (p1, q1, p0, q0, p_prev, courant, hits[1]),
        "v" * 7,
        (padded,),
    )
    one, two, moved, part_f = lax.optimization_barrier((one, two, moved, part_f))
    parts = [
        lax.ppermute(part, "dom", [(a ^ k, b) for a, b in (border, border[::-1])])
        for part, k in zip((parts[0], *moved), ROUTES)
    ]
    from_one = lax.ppermute(one, "dom", one_pairs)
    from_two = lax.ppermute(two, "dom", [(a, b) for a, b in two_pairs if a not in border])

    edge = groups * band - count_y
    coded = struct((code_rows_of(row_count, band), count_z), I16)
    frame = pltpu.VMEM((row_count, count_y + 2 * edge, count_z), F32)
    p2, q2, own, *sends = call(
        functools.partial(second_kernel, groups),
        (field, field, struct((piece, count_z), F32), *[coded] * (groups - 1)),
        (*scalars, p1, q1, p0, courant, part_f, part_a, bend, *parts, from_one, from_two),
        "ssss" + "v" * (9 + len(ROUTES)),
        (frame, pltpu.VMEM(code.shape, I16), scale, scale),
    )
    got = exchange(sends, "dom", between)[::-1]

    part = struct((span // SIZE_C * block, count_z), F32)
    keep, send = call(
        functools.partial(band_kernel, groups, row_count, block),
        (part, part),
        (anchors, own, *got),
        "s" + "v" * groups,
        (table,),
    )
    got = lax.ppermute(send, "shot", swap("c", 1))

    size = SIZE_Z * block
    coded = struct((code_rows_of(size // band, band), count_z), I16)
    total = pltpu.VMEM(((SIZE_X * SIZE_Z + 1) * block, count_z), F32)
    own, *sends = call(
        functools.partial(core_kernel, block, band),
        (struct((size, count_z), F32), *[coded] * (SIZE_X - 1)),
        (anchors, other, keep, got),
        "ssvv",
        (total,),
    )
    got = exchange(sends, "shot", along["x"])[::-1]

    coded = struct((code_rows_of(own_rows, band), count_z), I16)
    own, *sends = call(
        functools.partial(along_x_kernel, band),
        (struct((block, count_z), F32), *[coded] * (SIZE_Z - 1)),
        (own, *got),
        "v" * SIZE_X,
        (pltpu.VMEM((size, count_z), F32),),
    )
    got = exchange(sends, "shot", along["z"])[::-1]

    (gradient,) = call(
        functools.partial(along_z_kernel, band),
        (struct((block, count_z), F32),),
        (own, *got),
        "v" * SIZE_Z,
    )
    return (p2[None], q2[None], gradient.reshape(own_rows, band, count_z))


def solution(mesh):
    placed = (
        P("shot", "dom", None),
        P("shot", None),
        P("shot"),
        P("shot", None),
        P("shot", None, None),
        P("shot", None, None),
        P(),
        P("shot", "dom", None, None),
        P("shot", "dom", None, None),
        P("shot", "dom", None, None),
        P("shot", "dom", None, None),
    )
    return jax.shard_map(
        body,
        mesh=mesh,
        in_specs=placed,
        out_specs=(
            P("shot", "dom", None, None),
            P("shot", "dom", None, None),
            P("shot", "dom", None),
        ),
        check_vma=False,
    )
```

```python
import functools

import jax
import jax.numpy as jnp
from jax import lax
from jax.experimental import pallas as pl
from jax.experimental.pallas import tpu as pltpu
from jax.sharding import PartitionSpec as P

STEPS = 2
CENTER = -205.0 / 72.0
COEFFS = (8.0 / 5.0, -1.0 / 5.0, 8.0 / 315.0, -1.0 / 560.0)

F32 = jnp.float32
BF16 = jnp.bfloat16
I16 = jnp.int16
I32 = jnp.int32

VMEM_LIMIT = 32 * 1024 * 1024
FLOOR = 1e-33
TOP = 32700.0
HALO = 4
GROUP = 32


def vmem():
    return pl.BlockSpec(memory_space=pltpu.VMEM)


def smem():
    return pl.BlockSpec(memory_space=pltpu.SMEM)


def call(kernel, outs, args, spaces, scratch=(), cost=1_000_000):
    moved = sum(a.size * a.dtype.itemsize for a in (*outs, *args))
    return pl.pallas_call(
        kernel,
        out_shape=list(outs),
        in_specs=[smem() if s == "s" else vmem() for s in spaces],
        out_specs=[vmem()] * len(outs),
        scratch_shapes=list(scratch),
        compiler_params=pltpu.CompilerParams(vmem_limit_bytes=VMEM_LIMIT),
        cost_estimate=pl.CostEstimate(flops=0, bytes_accessed=0, transcendentals=0),
    )(*args)


def struct(shape, dtype):
    return jax.ShapeDtypeStruct(shape, dtype)


def code_group(values):
    top = jnp.max(jnp.abs(values), axis=0, keepdims=True)
    level = jnp.ceil(jnp.log2(jnp.maximum(top, FLOOR)) * 256.0) + 1.0
    scaled = values * (TOP * jnp.exp2(level * (-1.0 / 256.0)))
    return jnp.round(scaled).astype(I32), level.astype(I32)


def code_rows(values, out_ref, base):
    band = values[0].shape[0]
    levels = []
    for n in range(0, len(values), 2):
        codes = []
        for value in values[n : n + 2]:
            code, level = code_group(value)
            codes.append(code)
            levels.append(level)
        out_ref[pl.ds(base + n * band, 2 * band), :] = jnp.concatenate(codes, axis=0).astype(I16)
    levels += [jnp.zeros((-len(levels) % 16, values[0].shape[1]), I32)]
    spot = pl.ds(base + len(values) * band, code_rows_of(len(values), band) - len(values) * band)
    out_ref[spot, :] = jnp.concatenate(levels, axis=0).astype(I16)


def code_rows_of(groups, band):
    return groups * band + groups + -groups % 16


def decode_rows(in_ref, groups, band):
    scales = decode_scale(in_ref[pl.ds(groups * band, groups + -groups % 16), :])
    for n in range(0, groups, 2):
        pair = in_ref[pl.ds(n * band, 2 * band), :].astype(I32).astype(F32)
        yield pair[:band] * scales[n : n + 1]
        yield pair[band:] * scales[n + 1 : n + 2]


def decode_scale(levels):
    return jnp.exp2(levels.astype(I32).astype(F32) * (1.0 / 256.0)) * (1.0 / TOP)


def code_halos(field, rows, out_ref, level_ref, base):
    for n, layer in enumerate(rows):
        value = field(layer)
        count = value.shape[0] // GROUP
        for g in range(count):
            code, level = code_group(value[g * GROUP : (g + 1) * GROUP])
            spot = base + n * count + g
            out_ref[pl.ds(spot * GROUP, GROUP), :] = code.astype(I16)
            level_ref[pl.ds(spot, 1), :] = level


def halo_rows(layers, count_y):
    groups = layers * count_y // GROUP
    return groups * GROUP + groups


def odd_place():
    return lax.rem(lax.axis_index("dom"), 2)


def at_border():
    me, middle = lax.axis_index("dom"), lax.axis_size("dom") // HALVES
    return (me == middle) | (me == middle - 1)


def code_edges(fields, out_refs, level_ref):
    row_count, count_y, _ = fields[0].shape
    per = HALO * count_y // GROUP
    odd = odd_place()
    for out_ref, high in zip(out_refs, (1 - odd, odd)):
        first = high * (row_count - HALO)
        for f, ref in enumerate(fields):
            code_halos(lambda x: ref[x], [first + n for n in range(HALO)], out_ref, level_ref, f * per)
        out_ref[2 * per * GROUP :, :] = level_ref[...].astype(I16)


def encode_kernel(now_f, now_a, one, two, level_ref):
    code_edges((now_f, now_a), (one, two), level_ref)


def decode_halo(in_ref, scale_ref, pad_ref, f, first, count_y):
    per = count_y // GROUP
    for layer in range(HALO):
        for g in range(per):
            spot = (f * HALO + layer) * per + g
            code = in_ref[pl.ds(spot * GROUP, GROUP), :].astype(I32).astype(F32)
            pad_ref[first + layer, pl.ds(PAD + g * GROUP, GROUP), :] = code * scale_ref[pl.ds(spot, 1), :]


PAD = 8


def laplace_tile(pad_ref, layer, y, rows, masks):
    middle = pad_ref[layer, pl.ds(PAD + y, rows), :]
    summed = (3.0 * CENTER) * middle
    for k in range(1, HALO + 1):
        up, down = masks[k - 1]
        count = middle.shape[1]
        part = pad_ref[layer + k, pl.ds(PAD + y, rows), :] + pad_ref[layer - k, pl.ds(PAD + y, rows), :]
        part += pad_ref[layer, pl.ds(PAD + y + k, rows), :] + pad_ref[layer, pl.ds(PAD + y - k, rows), :]
        part += jnp.where(up, pltpu.roll(middle, k, 1), 0.0)
        part += jnp.where(down, pltpu.roll(middle, count - k, 1), 0.0)
        summed += COEFFS[k - 1] * part
    return middle, summed


TILE = 32


def lane_masks(rows, count):
    lane = lax.broadcasted_iota(I32, (rows, count), 1)
    return [(lane >= k, lane < count - k) for k in range(1, HALO + 1)]


def fill(pad_ref, field_ref):
    row_count, count_y, count_z = field_ref.shape
    edge = jnp.zeros((pad_ref.shape[0], PAD, count_z), F32)
    pad_ref[:, 0:PAD, :] = edge
    pad_ref[:, PAD + count_y :, :] = edge
    for x in range(row_count):
        pad_ref[HALO + x, PAD : PAD + count_y, :] = field_ref[x]


def load_scales(in_ref, scale_ref):
    groups = scale_ref.shape[0]
    scale_ref[...] = decode_scale(in_ref[groups * GROUP :, :])


def add_source(source, start, wave, ref, k, edge=0):
    x = source[0, 0] - lax.axis_index("dom") * ref.shape[0]
    lane = lax.broadcasted_iota(I32, (1, ref.shape[2]), 1)

    @pl.when((x >= 0) & (x < ref.shape[0]))
    def _():
        y = source[0, 1] + edge
        row = ref[x, pl.ds(y, 1), :]
        ref[x, pl.ds(y, 1), :] = row + jnp.where(lane == source[0, 2], wave[start[0] + k], 0.0)


def before_kernel(now_f, now_a, prev_f, prev_a, one, two, hit, *rest):
    sum_f, sum_a, base_f, base_a, pad, scale_one, scale_two = rest
    row_count, count_y, count_z = now_f.shape
    masks = lane_masks(TILE, count_z)
    load_scales(one, scale_one)
    load_scales(two, scale_two)
    odd = odd_place()
    fields = ((now_f, prev_f, sum_f, base_f), (now_a, prev_a, sum_a, base_a))
    for f, (now, prev, total, base) in enumerate(fields):
        fill(pad, now)
        decode_halo(one, scale_one, pad, f, (1 - odd) * (HALO + row_count), count_y)
        decode_halo(two, scale_two, pad, f, odd * (HALO + row_count), count_y)

        @pl.loop(0, row_count)
        def _(x):
            for y in range(0, count_y, TILE):
                spot = pl.ds(y, TILE)
                middle, summed = laplace_tile(pad, HALO + x, y, TILE, masks)
                total[x, spot, :] = summed
                value = 2.0 * middle - prev[x, spot, :]
                base[x, spot, :] = value + hit[x, spot, :] if f else value


def first_kernel(halves, anchors, source, begin, wave, sum_f, sum_a, base_f, base_a, *rest):
    next_f, next_a, courant, one, two, *parts, slab, level = rest[-7 - len(ROUTES) :]
    pieces = rest[: -7 - len(ROUTES)]
    row_count, count_y, _ = sum_f.shape
    band = pieces[0].shape[0] // (row_count * halves)
    side = len(pieces)
    me = lax.rem(lax.axis_index("dom"), side)
    for k in range(side):
        for half in range(halves):
            start = pl.multiple_of((half * side + (me ^ k)) * band, 8)
            for x in range(0, row_count, 2):
                speed = pieces[-k][pl.ds((half * row_count + x) * band, 2 * band), :].astype(F32)
                slab[x, pl.ds(start, band), :] = jnp.square(speed[:band])
                slab[x + 1, pl.ds(start, band), :] = jnp.square(speed[band:])

    @pl.loop(0, row_count)
    def _(x):
        for y in range(0, count_y, TILE):
            spot = pl.ds(y, TILE)
            factor = slab[x, pl.ds(anchors[0, 1] + y, TILE), :]
            courant[x, spot, :] = factor
            next_f[x, spot, :] = base_f[x, spot, :] + factor * sum_f[x, spot, :]
            next_a[x, spot, :] = base_a[x, spot, :] + factor * sum_a[x, spot, :]

    add_source(source, begin, wave, next_f, 0)
    code_edges((next_f, next_a), (one, two), level)

    @pl.when(at_border())
    def _():
        for n, part in enumerate(parts):
            size = part.shape[0]
            part[...] = two[n * size : (n + 1) * size, :]


def between_kernel(p1, q1, p0, q0, prev_f, courant, hit, part_f, part_a, bend, pad):
    row_count, count_y, count_z = p1.shape
    masks = lane_masks(TILE, count_z)
    outer = jnp.zeros((HALO, pad.shape[1], count_z), F32)
    pad[0:HALO] = outer
    pad[HALO + row_count :] = outer
    for f, (now, out) in enumerate(((p1, part_f), (q1, part_a))):
        fill(pad, now)

        @pl.loop(0, row_count)
        def _(x):
            for y in range(0, count_y, TILE):
                spot = pl.ds(y, TILE)
                middle, summed = laplace_tile(pad, HALO + x, y, TILE, masks)
                value = courant[x, spot, :] * summed
                if f == 0:
                    bend[x, spot, :] = middle - 2.0 * p0[x, spot, :] + prev_f[x, spot, :]
                else:
                    value += hit[x, spot, :] + (2.0 * middle - q0[x, spot, :])
                out[x, spot, :] = value


def halo_terms(in_ref, scale_ref, f, spot_y, count_y, low):
    per = count_y // GROUP
    rows = []
    for j in range(HALO):
        layer = j + low * (HALO - 1 - 2 * j)
        spot = (f * HALO + layer) * per + spot_y // GROUP
        code = in_ref[pl.ds(pl.multiple_of(spot * GROUP, GROUP), GROUP), :].astype(I32).astype(F32)
        rows.append(code * scale_ref[pl.ds(spot, 1), :])
    return [sum(COEFFS[r + j] * rows[j] for j in range(HALO - r)) for r in range(HALO)]


def second_kernel(groups, anchors, source, begin, wave, p1, q1, p0, courant, part_f, part_a, bend, *rest):
    parts, (one, two), rest = rest[: len(ROUTES)], rest[len(ROUTES) :][:2], rest[len(ROUTES) + 2 :]
    next_f, next_a, own = rest[:3]
    sends = rest[3 : 2 + groups]
    frame, held, scale_one, scale_two = rest[2 + groups :]

    @pl.when(jnp.logical_not(at_border()))
    def _():
        held[...] = two[...]

    @pl.when(at_border())
    def _():
        for n, part in enumerate(parts):
            size = part.shape[0]
            held[n * size : (n + 1) * size, :] = part[...]

    row_count, count_y, count_z = p1.shape
    band = own.shape[0] // row_count
    load_scales(one, scale_one)
    load_scales(held, scale_two)
    odd = odd_place()
    edge = (frame.shape[1] - count_y) // 2
    frame[:, 0:edge, :] = jnp.zeros((row_count, edge, count_z), F32)
    frame[:, edge + count_y :, :] = jnp.zeros((row_count, edge, count_z), F32)
    for y in range(0, count_y, GROUP):
        spot = pl.ds(y, GROUP)
        for ref, scale, low in ((one, scale_one, odd), (held, scale_two, 1 - odd)):
            for f in range(2):
                for r, term in enumerate(halo_terms(ref, scale, f, y, count_y, low)):
                    x = row_count - 1 - r + low * (2 * r + 1 - row_count)
                    term = courant[x, spot, :] * term
                    if f == 0:
                        frame[x, pl.ds(edge + y, GROUP), :] = part_f[x, spot, :] + term
                    else:
                        next_a[x, spot, :] = part_a[x, spot, :] + term

    add_source(source, begin, wave, frame, 1, edge)

    @pl.loop(0, row_count)
    def _(x):
        for y in range(0, count_y, TILE):
            spot = pl.ds(y, TILE)
            change = frame[x, pl.ds(edge + y, TILE), :]
            next_f[x, spot, :] = 2.0 * p1[x, spot, :] - p0[x, spot, :] + change
            image = q1[x, spot, :] * change + next_a[x, spot, :] * bend[x, spot, :]
            frame[x, pl.ds(edge + y, TILE), :] = image

    me = lax.axis_index("dom")
    for k in range(groups):
        start = edge - anchors[0, 1] + (me ^ k) * band
        values = [frame[x, pl.ds(start, band), :] for x in range(row_count)]
        if k == 0:
            for x in range(row_count):
                own[pl.ds(x * band, band), :] = values[x]
        else:
            code_rows(values, sends[k - 1], 0)


def hit_kernel(begin, cells, traces, first, second):
    row_count, count_y, count_z = first.shape
    x = cells[0:1, :] - lax.axis_index("dom") * row_count
    inside = (x >= 0) & (x < row_count)
    row = jnp.where(inside, x * count_y + cells[1:2, :], -1)
    depth = lax.broadcasted_iota(I32, (count_z, row.shape[1]), 0)
    at_depth = depth == cells[2:3, :]
    parts = []
    for k in range(STEPS):
        left = traces[pl.ds(begin[0] + (STEPS - 1 - k), 1), :]
        for _ in range(3):
            part = left.astype(BF16).astype(F32)
            parts.append(jnp.where(at_depth, part, 0.0).astype(BF16))
            left = left - part
    right = jnp.concatenate(parts, axis=0)

    @pl.loop(0, row_count)
    def _(i):
        cell = i * count_y + lax.broadcasted_iota(I32, (count_y, row.shape[1]), 0)
        left = jnp.where(cell == row, 1.0, 0.0).astype(BF16)
        got = lax.dot_general(left, right, (((1,), (1,)), ((), ())), preferred_element_type=F32)
        for k, out in enumerate((first, second)):
            base = 3 * k * count_z
            high = got[:, base : base + count_z]
            middle = got[:, base + count_z : base + 2 * count_z]
            low = got[:, base + 2 * count_z : base + 3 * count_z]
            out[i] = high + (middle + low)


SIZE_X, SIZE_Z, SIZE_C = 4, 4, 2
ROUTES = (0, 1, 3)
HALVES = 2


def place_of(shot):
    return shot // (SIZE_Z * SIZE_C), lax.rem(shot // SIZE_C, SIZE_Z), lax.rem(shot, SIZE_C)


def swap(axis, k):
    bits = k * {"x": SIZE_Z * SIZE_C, "z": SIZE_C, "c": 1}[axis]
    return [(shot, shot ^ bits) for shot in range(SIZE_X * SIZE_Z * SIZE_C)]


def join_kernel(*refs):
    size = refs[0].shape[0]
    for n, ref in enumerate(refs[:-1]):
        refs[-1][pl.ds(n * size, size), :] = ref[...]


def pick_kernel(layout, row_count, halves, anchors, *refs):
    count = len(layout)
    ins, outs, table = refs[:count], refs[count:-1], refs[-1]
    side = len(outs)
    piece = outs[0].shape[0] // halves
    per = piece // row_count
    block = ins[0].shape[0] // len(layout[0])
    own = block // per
    x, z, c = place_of(lax.axis_index("shot"))
    half, me = lax.axis_index("dom") // side, lax.rem(lax.axis_index("dom"), side)
    anchor = anchors[0, 0] + half * (side * row_count)
    first = anchor // own
    span = table.shape[1] // block
    for ref, owners in zip(ins, layout):
        for n, (dx, dz, dc, dh) in enumerate(owners):
            place = ((x ^ dx) * SIZE_Z + (z ^ dz)) * SIZE_C + (c ^ dc) - first

            @pl.when((place >= 0) & (place < span))
            def _():
                start = pl.multiple_of(place * block, 8)
                table[half ^ dh, pl.ds(start, block), :] = ref[pl.ds(n * block, block), :].astype(F32)

    offset = (anchor - first * own) * per
    for k in range(side):
        start = pl.multiple_of(offset + (me ^ k) * piece, 8)
        for h in range(halves):
            outs[k][pl.ds(h * piece, piece), :] = table[h, pl.ds(start, piece), :].astype(BF16)


def band_kernel(groups, row_count, block, anchors, own, *refs):
    got, (keep, send, table) = refs[: groups - 1], refs[groups - 1 :]
    per = own.shape[0] // row_count
    c = lax.rem(lax.axis_index("shot"), SIZE_C)
    me = lax.axis_index("dom")
    anchor = anchors[0, 0]
    first = anchor // (block // per)
    table[...] = jnp.zeros(table.shape, F32)
    offset = (anchor - first * (block // per)) * per
    for k in range(groups):
        base = offset + (me ^ k) * (row_count * per)
        if k == 0:
            table[pl.ds(pl.multiple_of(base, 8), row_count * per), :] = own[...]
        else:
            for n, value in enumerate(decode_rows(got[-k], row_count, per)):
                table[pl.ds(pl.multiple_of(base + n * per, 8), per), :] = value
    mine = lax.rem(c + first, SIZE_C)
    for i in range(keep.shape[0] // block):
        for out, parity in ((keep, mine), (send, 1 - mine)):
            start = pl.multiple_of((SIZE_C * i + parity) * block, 8)
            out[pl.ds(i * block, block), :] = table[pl.ds(start, block), :]


def core_kernel(block, per, anchors, other, keep, got, own, *refs):
    sends, total = refs[:-1], refs[-1]
    x, _, c = place_of(lax.axis_index("shot"))
    total[...] = jnp.zeros(total.shape, F32)
    for ref, place in ((keep, anchors), (got, other)):
        first = place[0, 0] // (block // per)
        low = (first + lax.rem(c + first, SIZE_C)) // SIZE_C
        for i in range(ref.shape[0] // block):
            spot = pl.ds(pl.multiple_of((low + i) * block, 8), block)
            total[spot, :] += ref[pl.ds(i * block, block), :]
    size = own.shape[0]
    own[...] = total[pl.ds(pl.multiple_of(x * size, 8), size), :]
    for k, send in enumerate(sends, 1):
        start = (x ^ k) * size
        values = [total[pl.ds(pl.multiple_of(start + n * per, 8), per), :] for n in range(size // per)]
        code_rows(values, send, 0)


def along_x_kernel(per, mine, *refs):
    got, rest = refs[: SIZE_X - 1], refs[SIZE_X - 1 :]
    own, sends, total = rest[0], rest[1:-1], rest[-1]
    total[...] = mine[...]
    for ref in got:
        for n, value in enumerate(decode_rows(ref, total.shape[0] // per, per)):
            total[pl.ds(n * per, per), :] += value
    _, z, _ = place_of(lax.axis_index("shot"))
    size = own.shape[0]
    own[...] = total[pl.ds(pl.multiple_of(z * size, 8), size), :]
    for k, send in enumerate(sends, 1):
        start = (z ^ k) * size
        values = [total[pl.ds(pl.multiple_of(start + n * per, 8), per), :] for n in range(size // per)]
        code_rows(values, send, 0)


def along_z_kernel(per, mine, *refs):
    got, out = refs[:-1], refs[-1]
    for parts in zip(range(mine.shape[0] // per), *[decode_rows(r, mine.shape[0] // per, per) for r in got]):
        n, values = parts[0], parts[1:]
        total = mine[pl.ds(n * per, per), :]
        for value in values:
            total += value
        out[pl.ds(n * per, per), :] = total


def swap_z(groups, k):
    shots, doms = (k % SIZE_Z) * SIZE_C, (k // SIZE_Z) * (groups // HALVES)
    return [
        (shot * groups + dom, (shot ^ shots) * groups + (dom ^ doms))
        for shot in range(SIZE_X * SIZE_Z * SIZE_C)
        for dom in range(groups)
    ]


def across(groups, k):
    return [(i, i ^ k) for i in range(groups)]


def far_first(values):
    return sorted(values, reverse=True)


def exchange(parts, axis, pairs):
    got = {}
    for k in far_first(range(1, len(parts) + 1)):
        got[k] = lax.ppermute(parts[k - 1], axis, pairs(k))
    return [got[k] for k in sorted(got)]


def body(
    velocity,
    anchors,
    start_step,
    source,
    receivers,
    traces,
    wavelet,
    fwd_prev,
    fwd_now,
    adj_prev,
    adj_now,
):
    row_count, count_y, count_z = fwd_now.shape[1:]
    groups = lax.axis_size("dom")
    own_rows, band = velocity.shape[:2]
    block = own_rows * band
    piece = row_count * band
    p0, q0, p_prev, q_prev = fwd_now[0], adj_now[0], fwd_prev[0], adj_prev[0]
    scalars = (anchors, source, start_step, wavelet)
    one_pairs = [(i, i ^ 1) for i in range(groups)]
    two_pairs = [(i, i + 1) for i in range(1, groups - 1, 2)]
    two_pairs += [(b, a) for a, b in two_pairs]

    along = {axis: functools.partial(swap, axis) for axis in "xzc"}
    between = functools.partial(across, groups)

    local = velocity.reshape(block, count_z)
    near = [local] + exchange([local] * (HALVES * SIZE_Z - 1), ("shot", "dom"), functools.partial(swap_z, groups))

    half = halo_rows(2 * HALO, count_y)
    code = struct((half, count_z), I16)
    levels = pltpu.VMEM((2 * HALO * count_y // GROUP, count_z), I32)
    one, two = call(encode_kernel, (code, code), (p0, q0), "vv", (levels,))
    from_one = lax.ppermute(one, "dom", one_pairs)
    from_two = lax.ppermute(two, "dom", two_pairs)

    (line,) = call(join_kernel, (struct((len(near) * block, count_z), BF16),), near, "v" * len(near))
    line, one = lax.optimization_barrier((line, one))
    field = struct((row_count, count_y, count_z), F32)
    hits = call(hit_kernel, (field, field), (start_step, receivers[0], traces[0]), "svv")
    plane = [line] + exchange([line] * (SIZE_X - 1), "shot", along["x"])
    plane = list(lax.optimization_barrier((*plane, hits[0])))[:SIZE_X]
    plane += [lax.ppermute(part, "shot", swap("c", 1)) for part in plane]
    *plane, from_one, from_two = lax.optimization_barrier((*plane, from_one, from_two))
    layout = [
        [(dx, k % SIZE_Z, dc, k // SIZE_Z) for k in range(HALVES * SIZE_Z)]
        for dc in range(SIZE_C)
        for dx in range(SIZE_X)
    ]
    span = -(-(row_count * groups + own_rows - 1) // own_rows)
    span += span % SIZE_C
    table = pltpu.VMEM((span * block, count_z), F32)
    side = groups // HALVES
    pieces = call(
        functools.partial(pick_kernel, layout, row_count, HALVES),
        [struct((HALVES * piece, count_z), BF16)] * side,
        (anchors, *plane),
        "s" + "v" * len(plane),
        (pltpu.VMEM((HALVES, -(-(row_count * side + own_rows - 1) // own_rows) * block, count_z), F32),),
    )
    *pieces, late_anchors = lax.optimization_barrier((*pieces, anchors))
    other = lax.ppermute(late_anchors, "shot", swap("c", 1))
    pieces = [pieces[0]] + exchange(pieces[1:], "dom", between)[::-1]

    padded = pltpu.VMEM((row_count + 2 * HALO, count_y + 2 * PAD, count_z), F32)
    scale = pltpu.VMEM((2 * HALO * count_y // GROUP, count_z), F32)
    slab = pltpu.VMEM((row_count, groups * band, count_z), F32)
    sums = call(
        before_kernel,
        (field,) * 4,
        (p0, q0, p_prev, q_prev, from_one, from_two, hits[0]),
        "v" * 7,
        (padded, scale, scale),
    )
    part = struct((half // len(ROUTES), count_z), I16)
    p1, q1, courant, one, two, *parts = call(
        functools.partial(first_kernel, HALVES),
        (field, field, field, code, code, *[part] * len(ROUTES)),
        (*scalars, *sums, *pieces),
        "ssss" + "v" * (4 + side),
        (slab, levels),
    )
    border = (side - 1, side)
    moved = [lax.ppermute(part, "dom", [(a, a ^ k) for a in border]) for part, k in zip(parts[1:], ROUTES[1:])]
    one, two, moved = lax.optimization_barrier((one, two, moved))
    parts = [
        lax.ppermute(part, "dom", [(a ^ k, b) for a, b in (border, border[::-1])])
        for part, k in zip((parts[0], *moved), ROUTES)
    ]
    from_one = lax.ppermute(one, "dom", one_pairs)
    from_two = lax.ppermute(two, "dom", [(a, b) for a, b in two_pairs if a not in border])
    part_f, part_a, bend = call(
        between_kernel,
        (field,) * 3,
        (p1, q1, p0, q0, p_prev, courant, hits[1]),
        "v" * 7,
        (padded,),
    )

    edge = groups * band - count_y
    coded = struct((code_rows_of(row_count, band), count_z), I16)
    frame = pltpu.VMEM((row_count, count_y + 2 * edge, count_z), F32)
    p2, q2, own, *sends = call(
        functools.partial(second_kernel, groups),
        (field, field, struct((piece, count_z), F32), *[coded] * (groups - 1)),
        (*scalars, p1, q1, p0, courant, part_f, part_a, bend, *parts, from_one, from_two),
        "ssss" + "v" * (9 + len(ROUTES)),
        (frame, pltpu.VMEM(code.shape, I16), scale, scale),
    )
    got = exchange(sends, "dom", between)[::-1]

    part = struct((span // SIZE_C * block, count_z), F32)
    keep, send = call(
        functools.partial(band_kernel, groups, row_count, block),
        (part, part),
        (anchors, own, *got),
        "s" + "v" * groups,
        (table,),
    )
    got = lax.ppermute(send, "shot", swap("c", 1))

    size = SIZE_Z * block
    coded = struct((code_rows_of(size // band, band), count_z), I16)
    total = pltpu.VMEM(((SIZE_X * SIZE_Z + 1) * block, count_z), F32)
    own, *sends = call(
        functools.partial(core_kernel, block, band),
        (struct((size, count_z), F32), *[coded] * (SIZE_X - 1)),
        (anchors, other, keep, got),
        "ssvv",
        (total,),
    )
    one_x, two_x, three_x = exchange(sends, "shot", along["x"])
    got = (two_x, three_x, one_x)

    coded = struct((code_rows_of(own_rows, band), count_z), I16)
    own, *sends = call(
        functools.partial(along_x_kernel, band),
        (struct((block, count_z), F32), *[coded] * (SIZE_Z - 1)),
        (own, *got),
        "v" * SIZE_X,
        (pltpu.VMEM((size, count_z), F32),),
    )
    got = exchange(sends, "shot", along["z"])[::-1]

    (gradient,) = call(
        functools.partial(along_z_kernel, band),
        (struct((block, count_z), F32),),
        (own, *got),
        "v" * SIZE_Z,
    )
    return (p2[None], q2[None], gradient.reshape(own_rows, band, count_z))


def solution(mesh):
    placed = (
        P("shot", "dom", None),
        P("shot", None),
        P("shot"),
        P("shot", None),
        P("shot", None, None),
        P("shot", None, None),
        P(),
        P("shot", "dom", None, None),
        P("shot", "dom", None, None),
        P("shot", "dom", None, None),
        P("shot", "dom", None, None),
    )
    return jax.shard_map(
        body,
        mesh=mesh,
        in_specs=placed,
        out_specs=(
            P("shot", "dom", None, None),
            P("shot", "dom", None, None),
            P("shot", "dom", None),
        ),
        check_vma=False,
    )
```

```python
import functools

import jax
import jax.numpy as jnp
from jax import lax
from jax.experimental import pallas as pl
from jax.experimental.pallas import tpu as pltpu
from jax.sharding import PartitionSpec as P

STEPS = 2
CENTER = -205.0 / 72.0
COEFFS = (8.0 / 5.0, -1.0 / 5.0, 8.0 / 315.0, -1.0 / 560.0)

F32 = jnp.float32
BF16 = jnp.bfloat16
I16 = jnp.int16
I32 = jnp.int32

VMEM_LIMIT = 32 * 1024 * 1024
FLOOR = 1e-33
TOP = 32700.0
HALO = 4
GROUP = 32


def vmem():
    return pl.BlockSpec(memory_space=pltpu.VMEM)


def smem():
    return pl.BlockSpec(memory_space=pltpu.SMEM)


def call(kernel, outs, args, spaces, scratch=(), cost=1_000_000):
    moved = sum(a.size * a.dtype.itemsize for a in (*outs, *args))
    return pl.pallas_call(
        kernel,
        out_shape=list(outs),
        in_specs=[smem() if s == "s" else vmem() for s in spaces],
        out_specs=[vmem()] * len(outs),
        scratch_shapes=list(scratch),
        compiler_params=pltpu.CompilerParams(vmem_limit_bytes=VMEM_LIMIT),
        cost_estimate=pl.CostEstimate(flops=0, bytes_accessed=0, transcendentals=0),
    )(*args)


def struct(shape, dtype):
    return jax.ShapeDtypeStruct(shape, dtype)


def code_group(values):
    top = jnp.max(jnp.abs(values), axis=0, keepdims=True)
    level = jnp.ceil(jnp.log2(jnp.maximum(top, FLOOR)) * 256.0) + 1.0
    scaled = values * (TOP * jnp.exp2(level * (-1.0 / 256.0)))
    return jnp.round(scaled).astype(I32), level.astype(I32)


def code_rows(values, out_ref, base):
    band = values[0].shape[0]
    levels = []
    for n in range(0, len(values), 2):
        codes = []
        for value in values[n : n + 2]:
            code, level = code_group(value)
            codes.append(code)
            levels.append(level)
        out_ref[pl.ds(base + n * band, 2 * band), :] = jnp.concatenate(codes, axis=0).astype(I16)
    levels += [jnp.zeros((-len(levels) % 16, values[0].shape[1]), I32)]
    spot = pl.ds(base + len(values) * band, code_rows_of(len(values), band) - len(values) * band)
    out_ref[spot, :] = jnp.concatenate(levels, axis=0).astype(I16)


def code_rows_of(groups, band):
    return groups * band + groups + -groups % 16


def decode_rows(in_ref, groups, band):
    scales = decode_scale(in_ref[pl.ds(groups * band, groups + -groups % 16), :])
    for n in range(0, groups, 2):
        pair = in_ref[pl.ds(n * band, 2 * band), :].astype(I32).astype(F32)
        yield pair[:band] * scales[n : n + 1]
        yield pair[band:] * scales[n + 1 : n + 2]


def decode_scale(levels):
    return jnp.exp2(levels.astype(I32).astype(F32) * (1.0 / 256.0)) * (1.0 / TOP)


def code_halos(field, rows, out_ref, level_ref, base):
    for n, layer in enumerate(rows):
        value = field(layer)
        count = value.shape[0] // GROUP
        for g in range(count):
            code, level = code_group(value[g * GROUP : (g + 1) * GROUP])
            spot = base + n * count + g
            out_ref[pl.ds(spot * GROUP, GROUP), :] = code.astype(I16)
            level_ref[pl.ds(spot, 1), :] = level


def halo_rows(layers, count_y):
    groups = layers * count_y // GROUP
    return groups * GROUP + groups


def odd_place():
    return lax.rem(lax.axis_index("dom"), 2)


def at_border():
    me, middle = lax.axis_index("dom"), lax.axis_size("dom") // HALVES
    return (me == middle) | (me == middle - 1)


def code_edges(fields, out_refs, level_ref):
    row_count, count_y, _ = fields[0].shape
    per = HALO * count_y // GROUP
    odd = odd_place()
    for out_ref, high in zip(out_refs, (1 - odd, odd)):
        first = high * (row_count - HALO)
        for f, ref in enumerate(fields):
            code_halos(lambda x: ref[x], [first + n for n in range(HALO)], out_ref, level_ref, f * per)
        out_ref[2 * per * GROUP :, :] = level_ref[...].astype(I16)


def encode_kernel(now_f, now_a, one, two, level_ref):
    code_edges((now_f, now_a), (one, two), level_ref)


def decode_halo(in_ref, scale_ref, pad_ref, f, first, count_y):
    per = count_y // GROUP
    for layer in range(HALO):
        for g in range(per):
            spot = (f * HALO + layer) * per + g
            code = in_ref[pl.ds(spot * GROUP, GROUP), :].astype(I32).astype(F32)
            pad_ref[first + layer, pl.ds(PAD + g * GROUP, GROUP), :] = code * scale_ref[pl.ds(spot, 1), :]


PAD = 8


def laplace_tile(pad_ref, layer, y, rows, masks):
    middle = pad_ref[layer, pl.ds(PAD + y, rows), :]
    summed = (3.0 * CENTER) * middle
    for k in range(1, HALO + 1):
        up, down = masks[k - 1]
        count = middle.shape[1]
        part = pad_ref[layer + k, pl.ds(PAD + y, rows), :] + pad_ref[layer - k, pl.ds(PAD + y, rows), :]
        part += pad_ref[layer, pl.ds(PAD + y + k, rows), :] + pad_ref[layer, pl.ds(PAD + y - k, rows), :]
        part += jnp.where(up, pltpu.roll(middle, k, 1), 0.0)
        part += jnp.where(down, pltpu.roll(middle, count - k, 1), 0.0)
        summed += COEFFS[k - 1] * part
    return middle, summed


TILE = 32


def lane_masks(rows, count):
    lane = lax.broadcasted_iota(I32, (rows, count), 1)
    return [(lane >= k, lane < count - k) for k in range(1, HALO + 1)]


def fill(pad_ref, field_ref):
    row_count, count_y, count_z = field_ref.shape
    edge = jnp.zeros((pad_ref.shape[0], PAD, count_z), F32)
    pad_ref[:, 0:PAD, :] = edge
    pad_ref[:, PAD + count_y :, :] = edge
    for x in range(row_count):
        pad_ref[HALO + x, PAD : PAD + count_y, :] = field_ref[x]


def load_scales(in_ref, scale_ref):
    groups = scale_ref.shape[0]
    scale_ref[...] = decode_scale(in_ref[groups * GROUP :, :])


def add_source(source, start, wave, ref, k, edge=0):
    x = source[0, 0] - lax.axis_index("dom") * ref.shape[0]
    lane = lax.broadcasted_iota(I32, (1, ref.shape[2]), 1)

    @pl.when((x >= 0) & (x < ref.shape[0]))
    def _():
        y = source[0, 1] + edge
        row = ref[x, pl.ds(y, 1), :]
        ref[x, pl.ds(y, 1), :] = row + jnp.where(lane == source[0, 2], wave[start[0] + k], 0.0)


def before_kernel(now_f, now_a, prev_f, prev_a, one, two, hit, *rest):
    sum_f, sum_a, base_f, base_a, pad, scale_one, scale_two = rest
    row_count, count_y, count_z = now_f.shape
    masks = lane_masks(TILE, count_z)
    load_scales(one, scale_one)
    load_scales(two, scale_two)
    odd = odd_place()
    fields = ((now_f, prev_f, sum_f, base_f), (now_a, prev_a, sum_a, base_a))
    for f, (now, prev, total, base) in enumerate(fields):
        fill(pad, now)
        decode_halo(one, scale_one, pad, f, (1 - odd) * (HALO + row_count), count_y)
        decode_halo(two, scale_two, pad, f, odd * (HALO + row_count), count_y)

        @pl.loop(0, row_count)
        def _(x):
            for y in range(0, count_y, TILE):
                spot = pl.ds(y, TILE)
                middle, summed = laplace_tile(pad, HALO + x, y, TILE, masks)
                total[x, spot, :] = summed
                value = 2.0 * middle - prev[x, spot, :]
                base[x, spot, :] = value + hit[x, spot, :] if f else value


def first_kernel(halves, anchors, source, begin, wave, sum_f, sum_a, base_f, base_a, *rest):
    next_f, next_a, courant, one, two, *parts, slab, level = rest[-7 - len(ROUTES) :]
    pieces = rest[: -7 - len(ROUTES)]
    row_count, count_y, _ = sum_f.shape
    band = pieces[0].shape[0] // (row_count * halves)
    side = len(pieces)
    me = lax.rem(lax.axis_index("dom"), side)
    for k in range(side):
        for half in range(halves):
            start = pl.multiple_of((half * side + (me ^ k)) * band, 8)
            for x in range(0, row_count, 2):
                speed = pieces[-k][pl.ds((half * row_count + x) * band, 2 * band), :].astype(F32)
                slab[x, pl.ds(start, band), :] = jnp.square(speed[:band])
                slab[x + 1, pl.ds(start, band), :] = jnp.square(speed[band:])

    @pl.loop(0, row_count)
    def _(x):
        for y in range(0, count_y, TILE):
            spot = pl.ds(y, TILE)
            factor = slab[x, pl.ds(anchors[0, 1] + y, TILE), :]
            courant[x, spot, :] = factor
            next_f[x, spot, :] = base_f[x, spot, :] + factor * sum_f[x, spot, :]
            next_a[x, spot, :] = base_a[x, spot, :] + factor * sum_a[x, spot, :]

    add_source(source, begin, wave, next_f, 0)
    code_edges((next_f, next_a), (one, two), level)

    @pl.when(at_border())
    def _():
        base = 0
        for part in parts:
            part[...] = two[base : base + part.shape[0], :]
            base += part.shape[0]


def between_kernel(p1, q1, p0, q0, prev_f, courant, hit, part_f, part_a, bend, pad):
    row_count, count_y, count_z = p1.shape
    masks = lane_masks(TILE, count_z)
    outer = jnp.zeros((HALO, pad.shape[1], count_z), F32)
    pad[0:HALO] = outer
    pad[HALO + row_count :] = outer
    for f, (now, out) in enumerate(((p1, part_f), (q1, part_a))):
        fill(pad, now)

        @pl.loop(0, row_count)
        def _(x):
            for y in range(0, count_y, TILE):
                spot = pl.ds(y, TILE)
                middle, summed = laplace_tile(pad, HALO + x, y, TILE, masks)
                value = courant[x, spot, :] * summed
                if f == 0:
                    bend[x, spot, :] = middle - 2.0 * p0[x, spot, :] + prev_f[x, spot, :]
                else:
                    value += hit[x, spot, :] + (2.0 * middle - q0[x, spot, :])
                out[x, spot, :] = value


def halo_terms(in_ref, scale_ref, f, spot_y, count_y, low):
    per = count_y // GROUP
    rows = []
    for j in range(HALO):
        layer = j + low * (HALO - 1 - 2 * j)
        spot = (f * HALO + layer) * per + spot_y // GROUP
        code = in_ref[pl.ds(pl.multiple_of(spot * GROUP, GROUP), GROUP), :].astype(I32).astype(F32)
        rows.append(code * scale_ref[pl.ds(spot, 1), :])
    return [sum(COEFFS[r + j] * rows[j] for j in range(HALO - r)) for r in range(HALO)]


def second_kernel(groups, anchors, source, begin, wave, p1, q1, p0, courant, part_f, part_a, bend, *rest):
    parts, (one, two), rest = rest[: len(ROUTES)], rest[len(ROUTES) :][:2], rest[len(ROUTES) + 2 :]
    next_f, next_a, own = rest[:3]
    sends = rest[3 : 2 + groups]
    frame, held, scale_one, scale_two = rest[2 + groups :]

    @pl.when(jnp.logical_not(at_border()))
    def _():
        held[...] = two[...]

    @pl.when(at_border())
    def _():
        base = 0
        for part in parts:
            held[base : base + part.shape[0], :] = part[...]
            base += part.shape[0]

    row_count, count_y, count_z = p1.shape
    band = own.shape[0] // row_count
    load_scales(one, scale_one)
    load_scales(held, scale_two)
    odd = odd_place()
    edge = (frame.shape[1] - count_y) // 2
    frame[:, 0:edge, :] = jnp.zeros((row_count, edge, count_z), F32)
    frame[:, edge + count_y :, :] = jnp.zeros((row_count, edge, count_z), F32)
    for y in range(0, count_y, GROUP):
        spot = pl.ds(y, GROUP)
        for ref, scale, low in ((one, scale_one, odd), (held, scale_two, 1 - odd)):
            for f in range(2):
                for r, term in enumerate(halo_terms(ref, scale, f, y, count_y, low)):
                    x = row_count - 1 - r + low * (2 * r + 1 - row_count)
                    term = courant[x, spot, :] * term
                    if f == 0:
                        frame[x, pl.ds(edge + y, GROUP), :] = part_f[x, spot, :] + term
                    else:
                        next_a[x, spot, :] = part_a[x, spot, :] + term

    add_source(source, begin, wave, frame, 1, edge)

    @pl.loop(0, row_count)
    def _(x):
        for y in range(0, count_y, TILE):
            spot = pl.ds(y, TILE)
            change = frame[x, pl.ds(edge + y, TILE), :]
            next_f[x, spot, :] = 2.0 * p1[x, spot, :] - p0[x, spot, :] + change
            image = q1[x, spot, :] * change + next_a[x, spot, :] * bend[x, spot, :]
            frame[x, pl.ds(edge + y, TILE), :] = image

    me = lax.axis_index("dom")
    for k in range(groups):
        start = edge - anchors[0, 1] + (me ^ k) * band
        values = [frame[x, pl.ds(start, band), :] for x in range(row_count)]
        if k == 0:
            for x in range(row_count):
                own[pl.ds(x * band, band), :] = values[x]
        else:
            code_rows(values, sends[k - 1], 0)


def hit_kernel(begin, cells, traces, first, second):
    row_count, count_y, count_z = first.shape
    x = cells[0:1, :] - lax.axis_index("dom") * row_count
    inside = (x >= 0) & (x < row_count)
    row = jnp.where(inside, x * count_y + cells[1:2, :], -1)
    depth = lax.broadcasted_iota(I32, (count_z, row.shape[1]), 0)
    at_depth = depth == cells[2:3, :]
    parts = []
    for k in range(STEPS):
        left = traces[pl.ds(begin[0] + (STEPS - 1 - k), 1), :]
        for _ in range(3):
            part = left.astype(BF16).astype(F32)
            parts.append(jnp.where(at_depth, part, 0.0).astype(BF16))
            left = left - part
    right = jnp.concatenate(parts, axis=0)

    @pl.loop(0, row_count)
    def _(i):
        cell = i * count_y + lax.broadcasted_iota(I32, (count_y, row.shape[1]), 0)
        left = jnp.where(cell == row, 1.0, 0.0).astype(BF16)
        got = lax.dot_general(left, right, (((1,), (1,)), ((), ())), preferred_element_type=F32)
        for k, out in enumerate((first, second)):
            base = 3 * k * count_z
            high = got[:, base : base + count_z]
            middle = got[:, base + count_z : base + 2 * count_z]
            low = got[:, base + 2 * count_z : base + 3 * count_z]
            out[i] = high + (middle + low)


SIZE_X, SIZE_Z, SIZE_C = 4, 4, 2
ROUTES = (1, 3, 0)
HALVES = 2


def place_of(shot):
    return shot // (SIZE_Z * SIZE_C), lax.rem(shot // SIZE_C, SIZE_Z), lax.rem(shot, SIZE_C)


def swap(axis, k):
    bits = k * {"x": SIZE_Z * SIZE_C, "z": SIZE_C, "c": 1}[axis]
    return [(shot, shot ^ bits) for shot in range(SIZE_X * SIZE_Z * SIZE_C)]


def join_kernel(*refs):
    size = refs[0].shape[0]
    for n, ref in enumerate(refs[:-1]):
        refs[-1][pl.ds(n * size, size), :] = ref[...]


def pick_kernel(layout, row_count, halves, anchors, *refs):
    count = len(layout)
    ins, outs, table = refs[:count], refs[count:-1], refs[-1]
    side = len(outs)
    piece = outs[0].shape[0] // halves
    per = piece // row_count
    block = ins[0].shape[0] // len(layout[0])
    own = block // per
    x, z, c = place_of(lax.axis_index("shot"))
    half, me = lax.axis_index("dom") // side, lax.rem(lax.axis_index("dom"), side)
    anchor = anchors[0, 0] + half * (side * row_count)
    first = anchor // own
    span = table.shape[1] // block
    for ref, owners in zip(ins, layout):
        for n, (dx, dz, dc, dh) in enumerate(owners):
            place = ((x ^ dx) * SIZE_Z + (z ^ dz)) * SIZE_C + (c ^ dc) - first

            @pl.when((place >= 0) & (place < span))
            def _():
                start = pl.multiple_of(place * block, 8)
                table[half ^ dh, pl.ds(start, block), :] = ref[pl.ds(n * block, block), :].astype(F32)

    offset = (anchor - first * own) * per
    for k in range(side):
        start = pl.multiple_of(offset + (me ^ k) * piece, 8)
        for h in range(halves):
            outs[k][pl.ds(h * piece, piece), :] = table[h, pl.ds(start, piece), :].astype(BF16)


def band_kernel(groups, row_count, block, anchors, own, *refs):
    got, (keep, send, table) = refs[: groups - 1], refs[groups - 1 :]
    per = own.shape[0] // row_count
    c = lax.rem(lax.axis_index("shot"), SIZE_C)
    me = lax.axis_index("dom")
    anchor = anchors[0, 0]
    first = anchor // (block // per)
    table[...] = jnp.zeros(table.shape, F32)
    offset = (anchor - first * (block // per)) * per
    for k in range(groups):
        base = offset + (me ^ k) * (row_count * per)
        if k == 0:
            table[pl.ds(pl.multiple_of(base, 8), row_count * per), :] = own[...]
        else:
            for n, value in enumerate(decode_rows(got[-k], row_count, per)):
                table[pl.ds(pl.multiple_of(base + n * per, 8), per), :] = value
    mine = lax.rem(c + first, SIZE_C)
    for i in range(keep.shape[0] // block):
        for out, parity in ((keep, mine), (send, 1 - mine)):
            start = pl.multiple_of((SIZE_C * i + parity) * block, 8)
            out[pl.ds(i * block, block), :] = table[pl.ds(start, block), :]


def core_kernel(block, per, anchors, other, keep, got, own, *refs):
    sends, total = refs[:-1], refs[-1]
    x, _, c = place_of(lax.axis_index("shot"))
    total[...] = jnp.zeros(total.shape, F32)
    for ref, place in ((keep, anchors), (got, other)):
        first = place[0, 0] // (block // per)
        low = (first + lax.rem(c + first, SIZE_C)) // SIZE_C
        for i in range(ref.shape[0] // block):
            spot = pl.ds(pl.multiple_of((low + i) * block, 8), block)
            total[spot, :] += ref[pl.ds(i * block, block), :]
    size = own.shape[0]
    own[...] = total[pl.ds(pl.multiple_of(x * size, 8), size), :]
    for k, send in enumerate(sends, 1):
        start = (x ^ k) * size
        values = [total[pl.ds(pl.multiple_of(start + n * per, 8), per), :] for n in range(size // per)]
        code_rows(values, send, 0)


def along_x_kernel(per, mine, *refs):
    got, rest = refs[: SIZE_X - 1], refs[SIZE_X - 1 :]
    own, sends, total = rest[0], rest[1:-1], rest[-1]
    total[...] = mine[...]
    for ref in got:
        for n, value in enumerate(decode_rows(ref, total.shape[0] // per, per)):
            total[pl.ds(n * per, per), :] += value
    _, z, _ = place_of(lax.axis_index("shot"))
    size = own.shape[0]
    own[...] = total[pl.ds(pl.multiple_of(z * size, 8), size), :]
    for k, send in enumerate(sends, 1):
        start = (z ^ k) * size
        values = [total[pl.ds(pl.multiple_of(start + n * per, 8), per), :] for n in range(size // per)]
        code_rows(values, send, 0)


def along_z_kernel(per, mine, *refs):
    got, out = refs[:-1], refs[-1]
    for parts in zip(range(mine.shape[0] // per), *[decode_rows(r, mine.shape[0] // per, per) for r in got]):
        n, values = parts[0], parts[1:]
        total = mine[pl.ds(n * per, per), :]
        for value in values:
            total += value
        out[pl.ds(n * per, per), :] = total


def swap_z(groups, k):
    shots, doms = (k % SIZE_Z) * SIZE_C, (k // SIZE_Z) * (groups // HALVES)
    return [
        (shot * groups + dom, (shot ^ shots) * groups + (dom ^ doms))
        for shot in range(SIZE_X * SIZE_Z * SIZE_C)
        for dom in range(groups)
    ]


def across(groups, k):
    return [(i, i ^ k) for i in range(groups)]


def far_first(values):
    return sorted(values, reverse=True)


def exchange(parts, axis, pairs):
    got = {}
    for k in far_first(range(1, len(parts) + 1)):
        got[k] = lax.ppermute(parts[k - 1], axis, pairs(k))
    return [got[k] for k in sorted(got)]


def body(
    velocity,
    anchors,
    start_step,
    source,
    receivers,
    traces,
    wavelet,
    fwd_prev,
    fwd_now,
    adj_prev,
    adj_now,
):
    row_count, count_y, count_z = fwd_now.shape[1:]
    groups = lax.axis_size("dom")
    own_rows, band = velocity.shape[:2]
    block = own_rows * band
    piece = row_count * band
    p0, q0, p_prev, q_prev = fwd_now[0], adj_now[0], fwd_prev[0], adj_prev[0]
    scalars = (anchors, source, start_step, wavelet)
    one_pairs = [(i, i ^ 1) for i in range(groups)]
    two_pairs = [(i, i + 1) for i in range(1, groups - 1, 2)]
    two_pairs += [(b, a) for a, b in two_pairs]

    along = {axis: functools.partial(swap, axis) for axis in "xzc"}
    between = functools.partial(across, groups)

    local = velocity.reshape(block, count_z)
    near = [local] + exchange([local] * (HALVES * SIZE_Z - 1), ("shot", "dom"), functools.partial(swap_z, groups))

    half = halo_rows(2 * HALO, count_y)
    code = struct((half, count_z), I16)
    levels = pltpu.VMEM((2 * HALO * count_y // GROUP, count_z), I32)
    one, two = call(encode_kernel, (code, code), (p0, q0), "vv", (levels,))
    from_one = lax.ppermute(one, "dom", one_pairs)
    from_two = lax.ppermute(two, "dom", two_pairs)

    (line,) = call(join_kernel, (struct((len(near) * block, count_z), BF16),), near, "v" * len(near))
    line, one = lax.optimization_barrier((line, one))
    field = struct((row_count, count_y, count_z), F32)
    hits = call(hit_kernel, (field, field), (start_step, receivers[0], traces[0]), "svv")
    plane = [line] + exchange([line] * (SIZE_X - 1), "shot", along["x"])
    plane = list(lax.optimization_barrier((*plane, hits[0])))[:SIZE_X]
    plane += [lax.ppermute(part, "shot", swap("c", 1)) for part in plane]
    *plane, from_one, from_two = lax.optimization_barrier((*plane, from_one, from_two))
    layout = [
        [(dx, k % SIZE_Z, dc, k // SIZE_Z) for k in range(HALVES * SIZE_Z)]
        for dc in range(SIZE_C)
        for dx in range(SIZE_X)
    ]
    span = -(-(row_count * groups + own_rows - 1) // own_rows)
    span += span % SIZE_C
    table = pltpu.VMEM((span * block, count_z), F32)
    side = groups // HALVES
    pieces = call(
        functools.partial(pick_kernel, layout, row_count, HALVES),
        [struct((HALVES * piece, count_z), BF16)] * side,
        (anchors, *plane),
        "s" + "v" * len(plane),
        (pltpu.VMEM((HALVES, -(-(row_count * side + own_rows - 1) // own_rows) * block, count_z), F32),),
    )
    *pieces, late_anchors = lax.optimization_barrier((*pieces, anchors))
    other = lax.ppermute(late_anchors, "shot", swap("c", 1))
    pieces = [pieces[0]] + exchange(pieces[1:], "dom", between)[::-1]

    padded = pltpu.VMEM((row_count + 2 * HALO, count_y + 2 * PAD, count_z), F32)
    scale = pltpu.VMEM((2 * HALO * count_y // GROUP, count_z), F32)
    slab = pltpu.VMEM((row_count, groups * band, count_z), F32)
    sums = call(
        before_kernel,
        (field,) * 4,
        (p0, q0, p_prev, q_prev, from_one, from_two, hits[0]),
        "v" * 7,
        (padded, scale, scale),
    )
    most = (-(-half // (16 * len(ROUTES))) + 1) * 16
    shares = [most] * (len(ROUTES) - 1) + [half - (len(ROUTES) - 1) * most]
    p1, q1, courant, one, two, *parts = call(
        functools.partial(first_kernel, HALVES),
        (field, field, field, code, code, *[struct((share, count_z), I16) for share in shares]),
        (*scalars, *sums, *pieces),
        "ssss" + "v" * (4 + side),
        (slab, levels),
    )
    border = (side - 1, side)
    moved = [lax.ppermute(part, "dom", [(a, a ^ k) for a in border]) for part, k in zip(parts[:-1], ROUTES[:-1])]
    one, two, moved = lax.optimization_barrier((one, two, moved))
    parts = [
        lax.ppermute(part, "dom", [(a ^ k, b) for a, b in (border, border[::-1])])
        for part, k in zip((*moved, parts[-1]), ROUTES)
    ]
    from_one = lax.ppermute(one, "dom", one_pairs)
    from_two = lax.ppermute(two, "dom", [(a, b) for a, b in two_pairs if a not in border])
    part_f, part_a, bend = call(
        between_kernel,
        (field,) * 3,
        (p1, q1, p0, q0, p_prev, courant, hits[1]),
        "v" * 7,
        (padded,),
    )

    edge = groups * band - count_y
    coded = struct((code_rows_of(row_count, band), count_z), I16)
    frame = pltpu.VMEM((row_count, count_y + 2 * edge, count_z), F32)
    p2, q2, own, *sends = call(
        functools.partial(second_kernel, groups),
        (field, field, struct((piece, count_z), F32), *[coded] * (groups - 1)),
        (*scalars, p1, q1, p0, courant, part_f, part_a, bend, *parts, from_one, from_two),
        "ssss" + "v" * (9 + len(ROUTES)),
        (frame, pltpu.VMEM(code.shape, I16), scale, scale),
    )
    got = exchange(sends, "dom", between)[::-1]

    part = struct((span // SIZE_C * block, count_z), F32)
    keep, send = call(
        functools.partial(band_kernel, groups, row_count, block),
        (part, part),
        (anchors, own, *got),
        "s" + "v" * groups,
        (table,),
    )
    got = lax.ppermute(send, "shot", swap("c", 1))

    size = SIZE_Z * block
    coded = struct((code_rows_of(size // band, band), count_z), I16)
    total = pltpu.VMEM(((SIZE_X * SIZE_Z + 1) * block, count_z), F32)
    own, *sends = call(
        functools.partial(core_kernel, block, band),
        (struct((size, count_z), F32), *[coded] * (SIZE_X - 1)),
        (anchors, other, keep, got),
        "ssvv",
        (total,),
    )
    one_x, two_x, three_x = exchange(sends, "shot", along["x"])
    got = (two_x, three_x, one_x)

    coded = struct((code_rows_of(own_rows, band), count_z), I16)
    own, *sends = call(
        functools.partial(along_x_kernel, band),
        (struct((block, count_z), F32), *[coded] * (SIZE_Z - 1)),
        (own, *got),
        "v" * SIZE_X,
        (pltpu.VMEM((size, count_z), F32),),
    )
    got = exchange(sends, "shot", along["z"])[::-1]

    (gradient,) = call(
        functools.partial(along_z_kernel, band),
        (struct((block, count_z), F32),),
        (own, *got),
        "v" * SIZE_Z,
    )
    return (p2[None], q2[None], gradient.reshape(own_rows, band, count_z))


def solution(mesh):
    placed = (
        P("shot", "dom", None),
        P("shot", None),
        P("shot"),
        P("shot", None),
        P("shot", None, None),
        P("shot", None, None),
        P(),
        P("shot", "dom", None, None),
        P("shot", "dom", None, None),
        P("shot", "dom", None, None),
        P("shot", "dom", None, None),
    )
    return jax.shard_map(
        body,
        mesh=mesh,
        in_specs=placed,
        out_specs=(
            P("shot", "dom", None, None),
            P("shot", "dom", None, None),
            P("shot", "dom", None),
        ),
        check_vma=False,
    )
```
